32 devices in a mesh: sp: 4 (over z), dp: 8 (over y, x, core).
Axes of the slice: x: 2, y: 2, z: 4, core: 2. Of those that a mesh axis runs over, the one named last changes fastest.
Arguments:
- tokens: bfloat16 [128, 32, 32, 384], P('dp', 'sp'), may hold values from -6 to 6
- extents: int32 [128, 2], P('dp'), may hold values from 16 to 32, as said below
- keep_mask: int32 [128], P('dp'), may hold values 0 or 1
- cotangent: bfloat16 [128, 16, 16, 768], P('dp', 'sp'), may hold values from -6 to 6
- dw_kernel: float32 [7, 7, 384], replicated, may hold values from -0.875 to 0.875
- dw_bias: float32 [384], replicated, may hold values from -3 to 3
- norm_gain: float32 [384], replicated, may hold values from 0.25 to 1.75
- norm_bias: float32 [384], replicated, may hold values from -2 to 2
- expand_weight: bfloat16 [384, 1536], replicated, may hold values from -0.3125 to 0.3125
- expand_bias: float32 [1536], replicated, may hold values from -2 to 2
- project_weight: bfloat16 [1536, 384], replicated, may hold values from -0.15625 to 0.15625
- project_bias: float32 [384], replicated, may hold values from -2 to 2
- layer_scale: float32 [384], replicated, may hold values from 0.5 to 2
- down_gain: float32 [384], replicated, may hold values from 0.25 to 1.75
- down_shift: float32 [384], replicated, may hold values from -2 to 2
- down_weight: bfloat16 [2, 2, 384, 768], replicated, may hold values from -0.15625 to 0.15625
- down_bias: float32 [768], replicated, may hold values from -2 to 2
Outputs:
- downsampled: bfloat16 [128, 16, 16, 768], P('dp', 'sp')
- input_grad: bfloat16 [128, 32, 32, 384], P('dp', 'sp')
- grad_dw_kernel: float32 [7, 7, 384], replicated
- grad_dw_bias: float32 [384], replicated
- grad_norm_gain: float32 [384], replicated
- grad_norm_bias: float32 [384], replicated
- grad_expand_weight: float32 [384, 1536], replicated
- grad_expand_bias: float32 [1536], replicated
- grad_project_weight: float32 [1536, 384], replicated
- grad_project_bias: float32 [384], replicated
- grad_layer_scale: float32 [384], replicated
- grad_down_gain: float32 [384], replicated
- grad_down_shift: float32 [384], replicated
- grad_down_weight: float32 [2, 2, 384, 768], replicated
- grad_down_bias: float32 [768], replicated
The draws below stay inside these ranges and needn't reach their ends.
Inputs may be any that keep to these rules, and one draw needn't show every extreme that they name: extents[b] holds the valid rows (at least 16) and valid columns (at least 16) of image b; among the 16 images of each index of dp, one chosen by the seed has all 32 rows valid.
All inputs are finite; a program needn't handle non-finite values. No bound on the sum of `keep_mask` on one device may be relied on, other than what follows from the above.
Results may differ from the reference program's by a relative error of at most 0.0072.
Values may be sent and summed in bfloat16 or wider, within the bound.
A program may use at most 192 MiB of HBM per device.

```python
import math
import jax
import jax.numpy as jnp
from jax import lax

C = 384
HID = 1536
COUT = 768
H = 32
W = 32
IMG_GRP = 16
IMAGES = 128


def draw_extents(key, part):
    key = jax.random.fold_in(key, 11)
    key_rows, key_cols, key_full = jax.random.split(key, 3)
    row_valid = jax.random.randint(key_rows, (IMAGES,), H // 2, H + 1, dtype=jnp.int32)
    col_valid = jax.random.randint(key_cols, (IMAGES,), W // 2, W + 1, dtype=jnp.int32)
    group_count = IMAGES // IMG_GRP
    chosen = jax.random.randint(key_full, (group_count,), 0, IMG_GRP, dtype=jnp.int32)
    full_rows = (jnp.arange(IMG_GRP, dtype=jnp.int32)[None, :] == chosen[:, None]).reshape(IMAGES)
    row_valid = jnp.where(full_rows, jnp.int32(H), row_valid)
    return jnp.stack([row_valid, col_valid], axis=1)


def with_ends(values, key, low, high):
    index_at = [jax.random.randint(jax.random.fold_in(key, axis), (), 0, length) for axis, length in enumerate(values.shape)]
    main_axis = values.shape.index(max(values.shape))
    next_to = index_at[:main_axis] + [(index_at[main_axis] + 1) % values.shape[main_axis]] + index_at[main_axis + 1:]
    return values.at[tuple(index_at)].set(low).at[tuple(next_to)].set(high)


def steps_of(stream_key, shape, cuts, low, top_value):
    gain = 1.0
    for dim, blocks in cuts:
        heights = jax.random.uniform(jax.random.fold_in(jax.random.fold_in(stream_key, 6), dim), (blocks,), jnp.float32, low / len(cuts), top_value / len(cuts))
        gain = gain * jnp.repeat(jnp.exp(heights), shape[dim] // blocks).reshape((-1,) + (1,) * (len(shape) - 1 - dim))
    return gain


def normal_values(stream_key, dims, width, most, cuts=(), kind=jnp.bfloat16):
    entries = jax.random.normal(stream_key, dims, jnp.float32) * width
    if len(cuts) > 0:
        entries = steps_of(stream_key, dims, cuts, -0.22, 0.18) * entries
    return jnp.clip(entries, min=-most, max=most).astype(kind)


def setup_inputs(seed: int = 0) -> dict:
    streams_of = jax.random.split(jax.random.key(seed), 18)
    return {
        "tokens": normal_values(streams_of[0], (IMAGES, H, W, C), 1.0, 6.0, ((0, 8), (1, 4))),
        "extents": draw_extents(jax.random.fold_in(streams_of[17], 71), 0),
        "keep_mask": with_ends((jax.random.randint(streams_of[2], (IMAGES,), 0, 8) < 7).astype(jnp.int32), jax.random.fold_in(streams_of[2], 1), 0, 1),
        "cotangent": normal_values(streams_of[3], (IMAGES, H // 2, W // 2, COUT), 1.0, 6.0, ((0, 8), (1, 4))),
        "dw_kernel": normal_values(streams_of[4], (7, 7, C), 49 ** -0.5, 0.875, (), jnp.float32),
        "dw_bias": normal_values(streams_of[5], (C,), 0.5, 3.0, (), jnp.float32),
        "norm_gain": jnp.clip(1.0 + 0.15 * jax.random.normal(streams_of[6], (C,), jnp.float32), 0.25, 1.75),
        "norm_bias": normal_values(streams_of[7], (C,), 0.3, 2.0, (), jnp.float32),
        "expand_weight": normal_values(streams_of[8], (C, HID), C ** -0.5, 0.3125),
        "expand_bias": normal_values(streams_of[9], (HID,), 0.3, 2.0, (), jnp.float32),
        "project_weight": normal_values(streams_of[10], (HID, C), HID ** -0.5, 0.15625),
        "project_bias": normal_values(streams_of[11], (C,), 0.3, 2.0, (), jnp.float32),
        "layer_scale": jnp.clip(jnp.exp(jax.random.uniform(streams_of[12], (C,), jnp.float32, math.log(0.5), math.log(2.0))), 0.5, 2.0),
        "down_gain": jnp.clip(1.0 + 0.15 * jax.random.normal(streams_of[13], (C,), jnp.float32), 0.25, 1.75),
        "down_shift": normal_values(streams_of[14], (C,), 0.3, 2.0, (), jnp.float32),
        "down_weight": normal_values(streams_of[15], (2, 2, C, COUT), (4 * C) ** -0.5, 0.15625),
        "down_bias": normal_values(streams_of[16], (COUT,), 0.3, 2.0, (), jnp.float32),
    }


epsilon = 1e-06
survival = 0.875

@jax.custom_vjp
def low(v):
    return lax.optimization_barrier(v.astype(jnp.bfloat16)).astype(jnp.float32)

@jax.custom_vjp
def low_back(v):
    return v

def low_keep(v):
    return (low(v), None)

def low_pass(kept, grad):
    return (grad,)

def back_keep(v):
    return (v, None)

def back_low(kept, grad):
    return (low(grad),)
low.defvjp(low_keep, low_pass)
low_back.defvjp(back_keep, back_low)

def inside(extents, first_row, row_total, col_total, stride):
    row_index = first_row + stride * jnp.arange(row_total, dtype=jnp.int32)
    col_index = stride * jnp.arange(col_total, dtype=jnp.int32)
    inside_mask = (row_index[None, :, None] < extents[:, 0][:, None, None]) & (col_index[None, None, :] < extents[:, 1][:, None, None])
    return inside_mask.astype(jnp.float32)[..., None]

def depthwise(padded, kernel):
    row_total = padded.shape[1] - 6
    col_total = padded.shape[2]
    widened = jnp.pad(padded, ((0, 0), (0, 0), (3, 3), (0, 0)))
    running = jnp.zeros((padded.shape[0], row_total, col_total, padded.shape[3]), jnp.float32)
    for row_tap in range(7):
        for col_tap in range(7):
            running = running + widened[:, row_tap:row_tap + row_total, col_tap:col_tap + col_total, :] * kernel[row_tap, col_tap]
    return running

def normalize(values):
    average = lax.optimization_barrier(jnp.mean(values, axis=-1, keepdims=True))
    centred = values - average
    return centred * lax.rsqrt(lax.optimization_barrier(jnp.mean(centred * centred, axis=-1, keepdims=True)) + epsilon)

def forward(field, extents, keep_mask, params):
    dw_kernel, dw_bias, norm_gain, norm_bias, expand_weight, expand_bias, project_weight, project_bias, layer_scale, down_gain, down_shift, down_weight, down_bias = params
    img_count, height, across, channels = field.shape
    pixel_mask = inside(extents, jnp.int32(0), height, across, 1)
    coarse_mask = inside(extents, jnp.int32(0), height // 2, across // 2, 2)
    masked = field * pixel_mask
    padded = jnp.pad(masked, ((0, 0), (3, 3), (0, 0), (0, 0)))
    mixed = (depthwise(padded, dw_kernel) + dw_bias).reshape(-1, channels)
    normed = low(normalize(mixed) * norm_gain + norm_bias)
    hidden = low_back(jnp.dot(normed, expand_weight, preferred_element_type=jnp.float32, precision=lax.Precision.HIGHEST) + expand_bias)
    activated = low(jax.nn.gelu(hidden, approximate=False))
    branch = low_back(jnp.dot(activated, project_weight, preferred_element_type=jnp.float32, precision=lax.Precision.HIGHEST) + project_bias)
    factor = (pixel_mask * (keep_mask.astype(jnp.float32) / survival)[:, None, None, None]).reshape(-1, 1)
    residual = masked.reshape(-1, channels) + factor * layer_scale * branch
    reduced = low((normalize(residual) * down_gain + down_shift) * pixel_mask.reshape(-1, 1))
    patches = reduced.reshape(img_count, height // 2, 2, across // 2, 2, channels).transpose(0, 1, 3, 2, 4, 5).reshape(-1, 4 * channels)
    outward = jnp.dot(patches, down_weight.reshape(4 * channels, -1), preferred_element_type=jnp.float32, precision=lax.Precision.HIGHEST) + down_bias
    outward = outward * coarse_mask.reshape(-1, 1)
    return outward.reshape(img_count, height // 2, across // 2, -1)

def reference(tokens, extents, keep_mask, cotangent, dw_kernel, dw_bias, norm_gain, norm_bias, expand_weight, expand_bias, project_weight, project_bias, layer_scale, down_gain, down_shift, down_weight, down_bias):
    weights = (dw_kernel, dw_bias, norm_gain, norm_bias, expand_weight.astype(jnp.float32), expand_bias, project_weight.astype(jnp.float32), project_bias, layer_scale, down_gain, down_shift, down_weight.astype(jnp.float32), down_bias)
    group_size = 4
    blocks = IMAGES // group_size
    inputs = tokens.astype(jnp.float32).reshape(blocks, group_size, H, W, C)
    block_extents = extents.reshape(blocks, group_size, 2)
    block_keep = keep_mask.reshape(blocks, group_size)
    block_cot = cotangent.astype(jnp.float32).reshape(blocks, group_size, H // 2, W // 2, COUT)

    def step(totals, pieces):
        piece_field, piece_extents, piece_keep, piece_cot = pieces
        outward, pullback = jax.vjp(lambda field, params: forward(field, piece_extents, piece_keep, params), piece_field, weights)
        grad_field, grad_params = pullback(piece_cot)
        totals = jax.tree.map(lambda running, addend: running + addend, totals, grad_params)
        return (totals, (outward.astype(jnp.bfloat16), grad_field.astype(jnp.bfloat16)))
    start_sums = jax.tree.map(jnp.zeros_like, weights)
    totals, (outputs, field_grads) = lax.scan(step, start_sums, (inputs, block_extents, block_keep, block_cot))
    downsampled = outputs.reshape(IMAGES, H // 2, W // 2, COUT)
    input_grad = field_grads.reshape(IMAGES, H, W, C)
    return (downsampled, input_grad, totals[0], totals[1], totals[2], totals[3], totals[4], totals[5], totals[6], totals[7], totals[8], totals[9], totals[10], totals[11], totals[12])
```

```python
import functools

import jax
import jax.numpy as jnp
import numpy as np
from jax import lax
from jax.experimental import pallas as pl
from jax.experimental.pallas import tpu as pltpu
from jax.sharding import PartitionSpec as P

bf16 = jnp.bfloat16
f32 = jnp.float32
epsilon = 1e-06
survival = 0.875
VMEM = 60 * 1024 * 1024


def tables(h, across):
    nr, nc = h + 6, across + 3
    us, vs, ms = [], [], []
    for v in range(nc // 2 + 1):
        for u in range(nr):
            mu, mv = (-u) % nr, (-v) % nc
            if (mv, mu) < (v, u):
                continue
            us.append(u)
            vs.append(v)
            ms.append(1.0 if (mu, mv) == (u, v) else 2.0)
    n = len(us)
    nf = -(-n // 128) * 128
    us, vs, ms = (np.array(a + [0] * (nf - n), np.float64) for a in (us, vs, ms))
    live = (np.arange(nf) < n)[:, None]

    def angle(r, c):
        turns = (np.outer(us, r.ravel()) * nc + np.outer(vs, c.ravel()) * nr) % (nr * nc)
        return 2 * np.pi * turns / (nr * nc)

    def waves(a):
        return np.concatenate([np.cos(a) * live, -np.sin(a) * live])

    r_all, c_all = np.meshgrid(np.arange(h + 6), np.arange(across), indexing="ij")
    p, q, i, j = np.meshgrid(
        np.arange(2), np.arange(2), np.arange(h // 2), np.arange(across // 2), indexing="ij"
    )
    r_own, c_own = (2 * i + p).ravel(), (2 * j + q).ravel()
    pick = np.zeros((h * across, (h + 6) * across))
    pick[np.arange(h * across), (r_own + 3) * across + c_own] = 1.0
    every, own = waves(angle(r_all, c_all)), waves(angle(r_own, c_own))
    ki, kj = np.meshgrid(np.arange(7), np.arange(7) - 3, indexing="ij")
    taps = angle(ki, kj)
    weight = (ms / (nr * nc))[:, None]
    spectrum = np.concatenate([np.cos(taps) * weight, np.sin(taps) * weight])
    back = np.concatenate([np.cos(taps) * weight, -np.sin(taps) * weight]).T
    back = np.pad(back, ((0, 7), (0, 0)))
    return (
        nf,
        np.concatenate([every, pick]),
        own.T,
        own,
        np.concatenate([every, pick]).T,
        spectrum,
        back,
    )


def dot(a, b):
    return jnp.dot(a, b, preferred_element_type=f32)


def dot_nt(a, b):
    return lax.dot_general(a, b, (((1,), (1,)), ((), ())), preferred_element_type=f32)


def dot_tn(a, b):
    return lax.dot_general(a, b, (((0,), (0,)), ((), ())), preferred_element_type=f32)


def mean(x):
    return jnp.sum(x, axis=-1, keepdims=True) * (1.0 / x.shape[-1])


def total(x):
    return jnp.sum(x, axis=0, keepdims=True)


def lanes(x, width):
    return jnp.concatenate([x] * (width // 128), axis=1)


def gelu_parts(v):
    e = jnp.exp(v * v * -0.5)
    t = 1.0 / (1.0 + jnp.abs(v) * (0.3275911 * 0.7071067811865476))
    q = (
        t
        * (
            0.127414796
            + t * (-0.142248368 + t * (0.7107068705 + t * (-0.7265760135 + t * 0.5307027145)))
        )
        * e
    )
    phi = jnp.where(v < 0.0, q, 1.0 - q)
    return v * phi, phi + v * e * 0.3989422804014327


class Masks:
    def __init__(self, h, across):
        n = lax.broadcasted_iota(jnp.int32, ((h + 6) * across, 128), 0)
        shift, low = across.bit_length() - 1, across - 1
        self.row, self.col = (n >> shift) - 3, n & low
        quarter = h * across // 4
        m = lax.broadcasted_iota(jnp.int32, (h * across, 128), 0)
        part, at = m >> (quarter.bit_length() - 1), m & (quarter - 1)
        self.own_row = 2 * (at >> (shift - 1)) + (part >> 1)
        self.own_col = 2 * (at & (across // 2 - 1)) + (part & 1)
        self.quarter = quarter

    def every(self, rows, cols):
        return ((self.row < rows) & (self.col < cols)).astype(f32)

    def own(self, rows, cols):
        return ((self.own_row < rows) & (self.own_col < cols)).astype(f32)


def forward_kernel(
    G, h, across, nf,
    ext, keep, top, own, bot, cot, fwd, inv, spec, dwb, ng, nb, ew, eb, pw, pb, ls, dg, ds, dw, db,
    out, act, slope, xhat, fh_out, nm, inv1_out, sh_out, inv2_out, gdw,
    mix, field, fac,
):
    g = pl.program_id(0)
    pixels = h * across
    C = own.shape[-1]
    masks = Masks(h, across)
    Q = masks.quarter
    kr, ki = spec[:nf], spec[nf:]
    for b in range(G):
        rows, cols = ext[g * G + b, 0], ext[g * G + b, 1]
        here = pl.ds(b * pixels, pixels)
        x = jnp.concatenate([top[b], own[b], bot[b]], axis=0)
        x = x * lanes(masks.every(rows, cols).astype(bf16), C)
        hat = dot(fwd[...], x)
        xr, xi = hat[:nf], hat[nf : 2 * nf]
        field[here, :] = hat[2 * nf :]
        xhat[b] = hat[: 2 * nf].astype(bf16)
        product = jnp.concatenate(
            [(xr * kr - xi * ki).astype(bf16), (xr * ki + xi * kr).astype(bf16)], axis=0
        )
        mix[here, :] = dot(inv[...], product)
        fac[here, :] = masks.own(rows, cols) * (
            keep[g * G + b].astype(f32) * (1.0 / survival)
        )
    mixed = mix[...] + dwb[...]
    d = mixed - mean(mixed)
    inv1 = lax.rsqrt(mean(d * d) + epsilon)
    fh = d * inv1
    fh_out[...] = fh.astype(bf16)
    inv1_out[...] = jnp.broadcast_to(inv1, inv1_out.shape)
    nm[...] = (fh * ng[...] + nb[...]).astype(bf16)
    HC = 512
    for k in range(ew.shape[1] // HC):
        part = pl.ds(k * HC, HC)
        hidden = dot(nm[...], ew[:, part]) + eb[:, part]
        a, s = gelu_parts(hidden)
        act[:, part] = a.astype(bf16)
        slope[:, part] = s.astype(bf16)
    branch = dot(act[...], pw[...]) + pb[...]
    res = field[...] + lanes(fac[...], C) * ls[...] * branch
    d = res - mean(res)
    inv2 = lax.rsqrt(mean(d * d) + epsilon)
    sh = d * inv2
    sh_out[...] = sh.astype(bf16)
    inv2_out[...] = jnp.broadcast_to(inv2, inv2_out.shape)
    reduced = sh * dg[...] + ds[...]
    patches, ups = [], []
    for b in range(G):
        rows, cols = ext[g * G + b, 0], ext[g * G + b, 1]
        valid = masks.own(rows, cols)
        rb = (reduced[b * pixels : (b + 1) * pixels] * lanes(valid, C)).astype(bf16)
        patches.append(jnp.concatenate([rb[k * Q : (k + 1) * Q] for k in range(4)], axis=1))
        coarse = lanes(valid[:Q], cot.shape[-1])
        ups.append(cot[b] * coarse.astype(bf16))
        out[b] = ((dot(patches[-1], dw[...]) + db[...]) * coarse).astype(bf16)
    term = dot_tn(jnp.concatenate(patches, axis=0), jnp.concatenate(ups, axis=0))

    @pl.when(g == 0)
    def _():
        gdw[...] = term

    @pl.when(g != 0)
    def _():
        gdw[...] += term


def forward(G, h, across, nf, n_img, ext, keep, top, own, bot, cot, *consts):
    pixels, C, CO = h * across, own.shape[-1], cot.shape[-1]
    HID = consts[6].shape[1]
    Q, NP = pixels // 4, n_img * pixels

    def whole(a):
        return pl.BlockSpec(a.shape, lambda g: (0,) * a.ndim)

    def img(*s):
        return pl.BlockSpec((G,) + s, lambda g: (g,) + (0,) * len(s))

    def pix(c):
        return pl.BlockSpec((G * pixels, c), lambda g: (g, 0))

    smem = pl.BlockSpec(memory_space=pltpu.SMEM)
    sds = jax.ShapeDtypeStruct
    return pl.pallas_call(
        functools.partial(forward_kernel, G, h, across, nf),
        grid=(n_img // G,),
        in_specs=[smem, smem, img(3 * across, C), img(pixels, C), img(3 * across, C), img(Q, CO)]
        + [whole(a) for a in consts],
        out_specs=[
            img(Q, CO), pix(HID), pix(HID), img(2 * nf, C), pix(C), pix(C), pix(128), pix(C), pix(128),
            pl.BlockSpec((4 * C, CO), lambda g: (0, 0)),
        ],
        out_shape=[
            sds((n_img, Q, CO), bf16), sds((NP, HID), bf16), sds((NP, HID), bf16), sds((n_img, 2 * nf, C), bf16),
            sds((NP, C), bf16), sds((NP, C), bf16), sds((NP, 128), f32), sds((NP, C), bf16), sds((NP, 128), f32),
            sds((4 * C, CO), f32),
        ],
        scratch_shapes=[
            pltpu.VMEM((G * pixels, C), f32), pltpu.VMEM((G * pixels, C), f32), pltpu.VMEM((G * pixels, 128), f32),
        ],
        compiler_params=pltpu.CompilerParams(vmem_limit_bytes=VMEM),
        name="forward",
    )(ext, keep, top, own, bot, cot, *consts)


def backward_kernel(
    G, h, across, nf,
    ext, keep, cot, sh_in, inv2, act, slope, nm, fh_in, inv1, xhat,
    dw, dg, ls, pw, ew, ng, fwd_own, inv_all, spec, back,
    own_out, top_out, bot_out, gpw, gew, gdk, vecs, geb, gdb,
    gb_s, gres_s, gm_s, acc,
):
    phase, g = pl.program_id(0), pl.program_id(1)
    pixels = h * across
    C = sh_in.shape[-1]
    masks = Masks(h, across)
    Q = masks.quarter
    rows_here = pl.ds(pl.multiple_of(g * (G * pixels), G * pixels), G * pixels)

    @pl.when((phase == 0) & (g == 0))
    def _():
        for ref in (gpw, gew, vecs, geb, gdb, acc):
            ref[...] = jnp.zeros_like(ref)

    @pl.when(phase == 0)
    def _():
        ups, valids = [], []
        for b in range(G):
            valid = masks.own(ext[g * G + b, 0], ext[g * G + b, 1])
            valids.append(valid)
            ups.append(cot[b] * lanes(valid[:Q].astype(bf16), cot.shape[-1]))
        up = jnp.concatenate(ups, axis=0)
        gdb[...] += total(up.astype(f32))
        gp = dot_nt(up, dw[...])
        slabs = []
        for b in range(G):
            for k in range(4):
                slabs.append(gp[b * Q : (b + 1) * Q, k * C : (k + 1) * C])
        valid = jnp.concatenate(valids, axis=0)
        gr = jnp.concatenate(slabs, axis=0) * lanes(valid, C)
        sh = sh_in[...].astype(f32)
        vecs[0:1, :] += total(gr * sh)
        vecs[1:2, :] += total(gr)
        u = gr * dg[...]
        gres = lanes(inv2[...], C) * (u - mean(u) - sh * mean(u * sh))
        gres_s[rows_here, :] = gres.astype(bf16)
        fac = jnp.concatenate(
            [valids[b] * (keep[g * G + b].astype(f32) * (1.0 / survival)) for b in range(G)], axis=0
        )
        gb = (gres * lanes(fac, C) * ls[...]).astype(bf16)
        gb_s[rows_here, :] = gb
        vecs[2:3, :] += total(gb.astype(f32))
        gpw[...] += dot_tn(gb, act[...])

    @pl.when(phase == 1)
    def _():
        gb = gb_s[rows_here, :]
        HC = 512
        gn = None
        for k in range(ew.shape[1] // HC):
            part = pl.ds(k * HC, HC)
            ga = dot_nt(gb, pw[part, :])
            gh = (ga * slope[:, part].astype(f32)).astype(bf16)
            geb[:, part] += total(gh.astype(f32))
            gew[:, part] += dot_tn(nm[...], gh)
            term = dot_nt(gh, ew[:, part])
            gn = term if gn is None else gn + term
        fh = fh_in[...].astype(f32)
        vecs[3:4, :] += total(gn * fh)
        vecs[4:5, :] += total(gn)
        w = gn * ng[...]
        gm = lanes(inv1[...], C) * (w - mean(w) - fh * mean(w * fh))
        vecs[5:6, :] += total(gm)
        gm_s[rows_here, :] = gm.astype(bf16)

    @pl.when(phase == 2)
    def _():
        kr, ki = spec[:nf], spec[nf:]
        sr, si = acc[:nf], acc[nf:]
        for b in range(G):
            here = pl.ds(pl.multiple_of((g * G + b) * pixels, pixels), pixels)
            hat = dot(fwd_own[...], gm_s[here, :])
            gr, gi = hat[:nf], hat[nf:]
            xr, xi = xhat[b, :nf].astype(f32), xhat[b, nf:].astype(f32)
            sr = sr + gr * xr + gi * xi
            si = si + gr * xi - gi * xr
            q = jnp.concatenate(
                [
                    (gr * kr + gi * ki).astype(bf16),
                    (gi * kr - gr * ki).astype(bf16),
                    gres_s[here, :],
                ],
                axis=0,
            )
            o = dot(inv_all[...], q)
            o = (o * lanes(masks.every(ext[g * G + b, 0], ext[g * G + b, 1]), C)).astype(bf16)
            top_out[b] = o[: 3 * across]
            own_out[b] = o[3 * across : 3 * across + pixels]
            bot_out[b] = o[3 * across + pixels :]
        acc[:nf] = sr
        acc[nf:] = si

    @pl.when((phase == 2) & (g == pl.num_programs(1) - 1))
    def _():
        gdk[...] = jnp.dot(
            back[...], acc[...], preferred_element_type=f32, precision=lax.Precision.HIGHEST
        )


def backward(G, h, across, nf, n_img, ext, keep, cot, sh, inv2, act, slope, nm, fh, inv1, xhat, *consts):
    pixels, C, CO = h * across, sh.shape[-1], cot.shape[-1]
    HID = act.shape[1]
    Q, NP, steps = pixels // 4, n_img * pixels, n_img // G

    def whole(a):
        return pl.BlockSpec(a.shape, lambda t, g: (0,) * a.ndim)

    def at(phase):
        def index(t, g):
            return jnp.where(t < phase, 0, jnp.where(t > phase, steps - 1, g))

        return index

    def img(phase, *s):
        index = at(phase)
        return pl.BlockSpec((G,) + s, lambda t, g: (index(t, g),) + (0,) * len(s))

    def pix(phase, c):
        index = at(phase)
        return pl.BlockSpec((G * pixels, c), lambda t, g: (index(t, g), 0))

    def result(*s):
        return pl.BlockSpec(s, lambda t, g: (0,) * len(s))

    smem = pl.BlockSpec(memory_space=pltpu.SMEM)
    sds = jax.ShapeDtypeStruct
    return pl.pallas_call(
        functools.partial(backward_kernel, G, h, across, nf),
        grid=(3, steps),
        in_specs=[
            smem, smem, img(0, Q, CO), pix(0, C), pix(0, 128), pix(0, HID), pix(1, HID), pix(1, C), pix(1, C), pix(1, 128),
            img(2, 2 * nf, C),
        ]
        + [whole(a) for a in consts],
        out_specs=[
            img(2, pixels, C), img(2, 3 * across, C), img(2, 3 * across, C),
            result(C, HID), result(C, HID), result(56, C), result(8, C), result(1, HID), result(1, CO),
        ],
        out_shape=[
            sds((n_img, pixels, C), bf16), sds((n_img, 3 * across, C), bf16), sds((n_img, 3 * across, C), bf16),
            sds((C, HID), f32), sds((C, HID), f32), sds((56, C), f32), sds((8, C), f32), sds((1, HID), f32), sds((1, CO), f32),
        ],
        scratch_shapes=[
            pltpu.VMEM((NP, C), bf16), pltpu.VMEM((NP, C), bf16), pltpu.VMEM((NP, C), bf16), pltpu.VMEM((2 * nf, C), f32),
        ],
        compiler_params=pltpu.CompilerParams(vmem_limit_bytes=VMEM),
        name="backward",
    )(ext, keep, cot, sh, inv2, act, slope, nm, fh, inv1, xhat, *consts)


def per_device(n_sp, *arrays):
    (
        tokens, extents, keep_mask, cotangent, dw_kernel, dw_bias, norm_gain, norm_bias, expand_weight, expand_bias,
        project_weight, project_bias, layer_scale, down_gain, down_shift, down_weight, down_bias,
    ) = arrays
    n_img, h, across, C = tokens.shape
    CO = cotangent.shape[-1]
    pixels = h * across
    G = 1024 // pixels
    nf, fwd, inv, fwd_own, inv_all, spectrum, back = tables(h, across)
    fwd, inv, fwd_own, inv_all = (jnp.asarray(a, bf16) for a in (fwd, inv, fwd_own, inv_all))
    back = jnp.asarray(back, f32)
    down = [(i, i + 1) for i in range(n_sp - 1)]
    up = [(i + 1, i) for i in range(n_sp - 1)]
    top = lax.ppermute(tokens[:, h - 3 :], "sp", down).reshape(n_img, 3 * across, C)
    bot = lax.ppermute(tokens[:, :3], "sp", up).reshape(n_img, 3 * across, C)
    first = lax.axis_index("sp") * h
    ext = extents - jnp.stack([first, jnp.zeros_like(first)])[None, :]
    spec = jnp.dot(
        jnp.asarray(spectrum, f32), dw_kernel.reshape(49, C), preferred_element_type=f32, precision=lax.Precision.HIGHEST
    )
    own = tokens.reshape(n_img, pixels, C)
    cot = cotangent.reshape(n_img, pixels // 4, CO)
    row = lambda v: v.reshape(1, -1)
    dw = down_weight.reshape(4 * C, CO)
    out, act, slope, xhat, fh, nm, inv1, sh, inv2, gdw = forward(
        G, h, across, nf, n_img, ext, keep_mask, top, own, bot, cot, fwd, inv, spec, row(dw_bias), row(norm_gain),
        row(norm_bias), expand_weight, row(expand_bias), project_weight, row(project_bias), row(layer_scale),
        row(down_gain), row(down_shift), dw, row(down_bias),
    )
    grad, top_g, bot_g, gpw, gew, gdk, vecs, geb, gdb = backward(
        G, h, across, nf, n_img, ext, keep_mask, cot, sh, inv2, act, slope, nm, fh, inv1, xhat, dw, row(down_gain),
        row(layer_scale), project_weight, expand_weight, row(norm_gain), fwd_own, inv_all, spec, back,
    )
    from_above = lax.ppermute(bot_g, "sp", down).reshape(n_img, 3, across, C)
    from_below = lax.ppermute(top_g, "sp", up).reshape(n_img, 3, across, C)
    grad = grad.reshape(n_img, h, across, C)
    gap = ((0, 0), (0, h - 3), (0, 0), (0, 0))
    pog = ((0, 0), (h - 3, 0), (0, 0), (0, 0))
    grad = (
        grad.astype(f32) + jnp.pad(from_above, gap).astype(f32) + jnp.pad(from_below, pog).astype(f32)
    ).astype(bf16)
    gdw, gpw, gew, gdk, vecs, geb, gdb = lax.psum((gdw, gpw, gew, gdk, vecs, geb, gdb), ("sp", "dp"))
    gpw = gpw.T
    gls = (jnp.sum(project_weight.astype(f32) * gpw, axis=0) + project_bias * vecs[2]) / layer_scale
    return (
        out.reshape(n_img, h // 2, across // 2, CO), grad, gdk[:49].reshape(7, 7, C), vecs[5], vecs[3], vecs[4], gew,
        geb[0], gpw, vecs[2], gls, vecs[0], vecs[1], gdw.reshape(down_weight.shape), gdb[0],
    )


def solution(mesh):
    maps = P("dp", "sp", None, None)
    return jax.shard_map(
        functools.partial(per_device, mesh.shape["sp"]),
        mesh=mesh,
        in_specs=(maps, P("dp", None), P("dp"), maps) + (P(),) * 13,
        out_specs=(maps, maps) + (P(),) * 13,
        check_vma=False,
    )
```

```python
import functools

import jax
import jax.numpy as jnp
import numpy as np
from jax import lax
from jax.experimental import pallas as pl
from jax.experimental.pallas import tpu as pltpu
from jax.sharding import PartitionSpec as P

bf16 = jnp.bfloat16
f32 = jnp.float32
epsilon = 1e-06
survival = 0.875
VMEM = 63 * 1024 * 1024


def tables(h, across):
    nr, nc = h + 6, across + 3
    us, vs, ms = [], [], []
    for v in range(nc // 2 + 1):
        for u in range(nr):
            mu, mv = (-u) % nr, (-v) % nc
            if (mv, mu) < (v, u):
                continue
            us.append(u)
            vs.append(v)
            ms.append(1.0 if (mu, mv) == (u, v) else 2.0)
    n = len(us)
    nf = -(-n // 128) * 128
    us, vs, ms = (np.array(a + [0] * (nf - n), np.float64) for a in (us, vs, ms))
    live = (np.arange(nf) < n)[:, None]

    def angle(r, c):
        turns = (np.outer(us, r.ravel()) * nc + np.outer(vs, c.ravel()) * nr) % (nr * nc)
        return 2 * np.pi * turns / (nr * nc)

    def waves(a):
        return np.concatenate([np.cos(a) * live, -np.sin(a) * live])

    r_all, c_all = np.meshgrid(np.arange(h + 6), np.arange(across), indexing="ij")
    p, q, i, j = np.meshgrid(
        np.arange(2), np.arange(2), np.arange(h // 2), np.arange(across // 2), indexing="ij"
    )
    r_own, c_own = (2 * i + p).ravel(), (2 * j + q).ravel()
    pick = np.zeros((h * across, (h + 6) * across))
    pick[np.arange(h * across), (r_own + 3) * across + c_own] = 1.0
    every, own = waves(angle(r_all, c_all)), waves(angle(r_own, c_own))
    ki, kj = np.meshgrid(np.arange(7), np.arange(7) - 3, indexing="ij")
    taps = angle(ki, kj)
    weight = (ms / (nr * nc))[:, None]
    spectrum = np.concatenate([np.cos(taps) * weight, np.sin(taps) * weight])
    back = np.concatenate([np.cos(taps) * weight, -np.sin(taps) * weight]).T
    back = np.pad(back, ((0, 7), (0, 0)))
    return (
        nf,
        np.concatenate([every, pick]),
        own.T,
        own,
        np.concatenate([every, pick]).T,
        spectrum,
        back,
    )


def dot(a, b):
    return jnp.dot(a, b, preferred_element_type=f32)


def dot_nt(a, b):
    return lax.dot_general(a, b, (((1,), (1,)), ((), ())), preferred_element_type=f32)


def dot_tn(a, b):
    return lax.dot_general(a, b, (((0,), (0,)), ((), ())), preferred_element_type=f32)


def mean(x):
    return jnp.sum(x, axis=-1, keepdims=True) * (1.0 / x.shape[-1])


def total(x):
    return jnp.sum(x, axis=0, keepdims=True)


def lanes(x, width):
    return jnp.concatenate([x] * (width // 128), axis=1)


def gelu_parts(v):
    e = jnp.exp(v * v * -0.5)
    t = 1.0 / (1.0 + jnp.abs(v) * (0.3275911 * 0.7071067811865476))
    q = (
        t
        * (
            0.127414796
            + t * (-0.142248368 + t * (0.7107068705 + t * (-0.7265760135 + t * 0.5307027145)))
        )
        * e
    )
    phi = jnp.where(v < 0.0, q, 1.0 - q)
    return v * phi, phi + v * e * 0.3989422804014327


class Masks:
    def __init__(self, h, across):
        n = lax.broadcasted_iota(jnp.int32, ((h + 6) * across, 128), 0)
        shift, low = across.bit_length() - 1, across - 1
        self.row, self.col = (n >> shift) - 3, n & low
        quarter = h * across // 4
        m = lax.broadcasted_iota(jnp.int32, (h * across, 128), 0)
        part, at = m >> (quarter.bit_length() - 1), m & (quarter - 1)
        self.own_row = 2 * (at >> (shift - 1)) + (part >> 1)
        self.own_col = 2 * (at & (across // 2 - 1)) + (part & 1)
        self.quarter = quarter

    def every(self, rows, cols):
        return ((self.row < rows) & (self.col < cols)).astype(f32)

    def own(self, rows, cols):
        return ((self.own_row < rows) & (self.own_col < cols)).astype(f32)


def forward_kernel(
    G, h, across, nf,
    ext, keep, top, own, bot, cot, fwd, inv, spec, dwb, ng, nb, ew, eb, pw, pb, ls, dg, ds, dw, db,
    out, act, slope, xhat, fh_out, nm, inv1_out, sh_out, inv2_out, gdw,
    mix, field, fac, gdw_s,
):
    g = pl.program_id(0)
    pixels = h * across
    C = own.shape[-1]
    masks = Masks(h, across)
    Q = masks.quarter
    kr, ki = spec[:nf], spec[nf:]
    for b in range(G):
        rows, cols = ext[g * G + b, 0], ext[g * G + b, 1]
        here = pl.ds(b * pixels, pixels)
        x = jnp.concatenate([top[b], own[b], bot[b]], axis=0)
        x = x * lanes(masks.every(rows, cols).astype(bf16), C)
        hat = dot(fwd[...], x)
        xr, xi = hat[:nf], hat[nf : 2 * nf]
        field[here, :] = hat[2 * nf :]
        xhat[b] = hat[: 2 * nf].astype(bf16)
        product = jnp.concatenate(
            [(xr * kr - xi * ki).astype(bf16), (xr * ki + xi * kr).astype(bf16)], axis=0
        )
        mix[here, :] = dot(inv[...], product)
        fac[here, :] = masks.own(rows, cols) * (
            keep[g * G + b].astype(f32) * (1.0 / survival)
        )
    mixed = mix[...] + dwb[...]
    d = mixed - mean(mixed)
    inv1 = lax.rsqrt(mean(d * d) + epsilon)
    fh = d * inv1
    fh_out[...] = fh.astype(bf16)
    inv1_out[...] = jnp.broadcast_to(inv1, inv1_out.shape)
    nm[...] = (fh * ng[...] + nb[...]).astype(bf16)
    HC = 512
    for k in range(ew.shape[1] // HC):
        part = pl.ds(k * HC, HC)
        hidden = dot(nm[...], ew[:, part]) + eb[:, part]
        a, s = gelu_parts(hidden)
        act[:, part] = a.astype(bf16)
        slope[:, part] = s.astype(bf16)
    branch = dot(act[...], pw[...]) + pb[...]
    res = field[...] + lanes(fac[...], C) * ls[...] * branch
    d = res - mean(res)
    inv2 = lax.rsqrt(mean(d * d) + epsilon)
    sh = d * inv2
    sh_out[...] = sh.astype(bf16)
    inv2_out[...] = jnp.broadcast_to(inv2, inv2_out.shape)
    reduced = sh * dg[...] + ds[...]
    patches, ups = [], []
    for b in range(G):
        rows, cols = ext[g * G + b, 0], ext[g * G + b, 1]
        valid = masks.own(rows, cols)
        rb = (reduced[b * pixels : (b + 1) * pixels] * lanes(valid, C)).astype(bf16)
        patches.append(jnp.concatenate([rb[k * Q : (k + 1) * Q] for k in range(4)], axis=1))
        coarse = lanes(valid[:Q], cot.shape[-1])
        ups.append(cot[b] * coarse.astype(bf16))
        out[b] = ((dot(patches[-1], dw[...]) + db[...]) * coarse).astype(bf16)
    term = dot_tn(jnp.concatenate(patches, axis=0), jnp.concatenate(ups, axis=0))

    @pl.when(g == 0)
    def _():
        gdw_s[...] = term

    @pl.when(g != 0)
    def _():
        gdw_s[...] += term

    @pl.when(g == pl.num_programs(0) - 1)
    def _():
        gdw[...] = gdw_s[...].astype(gdw.dtype)


def forward(sum_type, G, h, across, nf, n_img, ext, keep, top, own, bot, cot, *consts):
    pixels, C, CO = h * across, own.shape[-1], cot.shape[-1]
    HID = consts[6].shape[1]
    Q, NP = pixels // 4, n_img * pixels

    def whole(a):
        return pl.BlockSpec(a.shape, lambda g: (0,) * a.ndim)

    def img(*s):
        return pl.BlockSpec((G,) + s, lambda g: (g,) + (0,) * len(s))

    def pix(c):
        return pl.BlockSpec((G * pixels, c), lambda g: (g, 0))

    smem = pl.BlockSpec(memory_space=pltpu.SMEM)
    sds = jax.ShapeDtypeStruct
    return pl.pallas_call(
        functools.partial(forward_kernel, G, h, across, nf),
        grid=(n_img // G,),
        in_specs=[smem, smem, img(3 * across, C), img(pixels, C), img(3 * across, C), img(Q, CO)]
        + [whole(a) for a in consts],
        out_specs=[
            img(Q, CO), pix(HID), pix(HID), img(2 * nf, C), pix(C), pix(C), pix(128), pix(C), pix(128),
            pl.BlockSpec((4 * C, CO), lambda g: (0, 0)),
        ],
        out_shape=[
            sds((n_img, Q, CO), bf16), sds((NP, HID), bf16), sds((NP, HID), bf16), sds((n_img, 2 * nf, C), bf16),
            sds((NP, C), bf16), sds((NP, C), bf16), sds((NP, 128), f32), sds((NP, C), bf16), sds((NP, 128), f32),
            sds((4 * C, CO), sum_type),
        ],
        scratch_shapes=[
            pltpu.VMEM((G * pixels, C), f32), pltpu.VMEM((G * pixels, C), f32), pltpu.VMEM((G * pixels, 128), f32),
            pltpu.VMEM((4 * C, CO), f32),
        ],
        compiler_params=pltpu.CompilerParams(vmem_limit_bytes=VMEM),
        name="forward",
    )(ext, keep, top, own, bot, cot, *consts)


def local_backward_kernel(
    G, h, across, nf,
    ext, keep, cot, sh_in, inv2, act, slope, nm, fh_in, inv1, xhat,
    dw, dg, ls, pw, ew, ng, fwd_own, inv_all, spec, back,
    own_out, top_out, bot_out, gpw, gew, gdk, vecs, geb, gdb,
    gb_s, gres_s, gm_s, acc,
):
    phase, g = pl.program_id(0), pl.program_id(1)
    pixels = h * across
    C = sh_in.shape[-1]
    masks = Masks(h, across)
    Q = masks.quarter
    rows_here = pl.ds(pl.multiple_of(g * (G * pixels), G * pixels), G * pixels)

    @pl.when((phase == 0) & (g == 0))
    def _():
        for ref in (gpw, gew, vecs, geb, gdb, acc):
            ref[...] = jnp.zeros_like(ref)

    @pl.when(phase == 0)
    def _():
        ups, valids = [], []
        for b in range(G):
            valid = masks.own(ext[g * G + b, 0], ext[g * G + b, 1])
            valids.append(valid)
            ups.append(cot[b] * lanes(valid[:Q].astype(bf16), cot.shape[-1]))
        up = jnp.concatenate(ups, axis=0)
        gdb[...] += total(up.astype(f32))
        gp = dot_nt(up, dw[...])
        slabs = []
        for b in range(G):
            for k in range(4):
                slabs.append(gp[b * Q : (b + 1) * Q, k * C : (k + 1) * C])
        valid = jnp.concatenate(valids, axis=0)
        gr = jnp.concatenate(slabs, axis=0) * lanes(valid, C)
        sh = sh_in[...].astype(f32)
        vecs[0:1, :] += total(gr * sh)
        vecs[1:2, :] += total(gr)
        u = gr * dg[...]
        gres = lanes(inv2[...], C) * (u - mean(u) - sh * mean(u * sh))
        gres_s[rows_here, :] = gres.astype(bf16)
        fac = jnp.concatenate(
            [valids[b] * (keep[g * G + b].astype(f32) * (1.0 / survival)) for b in range(G)], axis=0
        )
        gb = (gres * lanes(fac, C) * ls[...]).astype(bf16)
        gb_s[rows_here, :] = gb
        vecs[2:3, :] += total(gb.astype(f32))
        gpw[...] += dot_tn(gb, act[...])

    @pl.when(phase == 1)
    def _():
        gb = gb_s[rows_here, :]
        HC = 512
        gn = None
        for k in range(ew.shape[1] // HC):
            part = pl.ds(k * HC, HC)
            ga = dot_nt(gb, pw[part, :])
            gh = (ga * slope[:, part].astype(f32)).astype(bf16)
            geb[:, part] += total(gh.astype(f32))
            gew[:, part] += dot_tn(nm[...], gh)
            term = dot_nt(gh, ew[:, part])
            gn = term if gn is None else gn + term
        fh = fh_in[...].astype(f32)
        vecs[3:4, :] += total(gn * fh)
        vecs[4:5, :] += total(gn)
        w = gn * ng[...]
        gm = lanes(inv1[...], C) * (w - mean(w) - fh * mean(w * fh))
        vecs[5:6, :] += total(gm)
        gm_s[rows_here, :] = gm.astype(bf16)

    @pl.when(phase == 2)
    def _():
        kr, ki = spec[:nf], spec[nf:]
        sr, si = acc[:nf], acc[nf:]
        for b in range(G):
            here = pl.ds(pl.multiple_of((g * G + b) * pixels, pixels), pixels)
            hat = dot(fwd_own[...], gm_s[here, :])
            gr, gi = hat[:nf], hat[nf:]
            xr, xi = xhat[b, :nf].astype(f32), xhat[b, nf:].astype(f32)
            sr = sr + gr * xr + gi * xi
            si = si + gr * xi - gi * xr
            q = jnp.concatenate(
                [
                    (gr * kr + gi * ki).astype(bf16),
                    (gi * kr - gr * ki).astype(bf16),
                    gres_s[here, :],
                ],
                axis=0,
            )
            o = dot(inv_all[...], q)
            o = (o * lanes(masks.every(ext[g * G + b, 0], ext[g * G + b, 1]), C)).astype(bf16)
            top_out[b] = o[: 3 * across]
            own_out[b] = o[3 * across : 3 * across + pixels]
            bot_out[b] = o[3 * across + pixels :]
        acc[:nf] = sr
        acc[nf:] = si

    @pl.when((phase == 2) & (g == pl.num_programs(1) - 1))
    def _():
        gdk[...] = jnp.dot(
            back[...], acc[...], preferred_element_type=f32, precision=lax.Precision.HIGHEST
        )


def local_backward(G, h, across, nf, n_img, ext, keep, cot, sh, inv2, act, slope, nm, fh, inv1, xhat, *consts):
    pixels, C, CO = h * across, sh.shape[-1], cot.shape[-1]
    HID = act.shape[1]
    Q, NP, steps = pixels // 4, n_img * pixels, n_img // G

    def whole(a):
        return pl.BlockSpec(a.shape, lambda t, g: (0,) * a.ndim)

    def at(phase):
        def index(t, g):
            return jnp.where(t < phase, 0, jnp.where(t > phase, steps - 1, g))

        return index

    def img(phase, *s):
        index = at(phase)
        return pl.BlockSpec((G,) + s, lambda t, g: (index(t, g),) + (0,) * len(s))

    def pix(phase, c):
        index = at(phase)
        return pl.BlockSpec((G * pixels, c), lambda t, g: (index(t, g), 0))

    def result(*s):
        return pl.BlockSpec(s, lambda t, g: (0,) * len(s))

    smem = pl.BlockSpec(memory_space=pltpu.SMEM)
    sds = jax.ShapeDtypeStruct
    return pl.pallas_call(
        functools.partial(local_backward_kernel, G, h, across, nf),
        grid=(3, steps),
        in_specs=[
            smem, smem, img(0, Q, CO), pix(0, C), pix(0, 128), pix(0, HID), pix(1, HID), pix(1, C), pix(1, C), pix(1, 128),
            img(2, 2 * nf, C),
        ]
        + [whole(a) for a in consts],
        out_specs=[
            img(2, pixels, C), img(2, 3 * across, C), img(2, 3 * across, C),
            result(C, HID), result(C, HID), result(56, C), result(8, C), result(1, HID), result(1, CO),
        ],
        out_shape=[
            sds((n_img, pixels, C), bf16), sds((n_img, 3 * across, C), bf16), sds((n_img, 3 * across, C), bf16),
            sds((C, HID), f32), sds((C, HID), f32), sds((56, C), f32), sds((8, C), f32), sds((1, HID), f32), sds((1, CO), f32),
        ],
        scratch_shapes=[
            pltpu.VMEM((NP, C), bf16), pltpu.VMEM((NP, C), bf16), pltpu.VMEM((NP, C), bf16), pltpu.VMEM((2 * nf, C), f32),
        ],
        compiler_params=pltpu.CompilerParams(vmem_limit_bytes=VMEM),
        name="local_backward",
    )(ext, keep, cot, sh, inv2, act, slope, nm, fh, inv1, xhat, *consts)


class Sum:
    def __init__(self, place, full, half, plane_in, z_in, send, recv, out, first_col=0, by_cols=False):
        self.place, self.full, self.half = place, full, half
        self.plane_in, self.z_in, self.send, self.recv = plane_in, z_in, send, recv
        self.out, self.by_cols = out, by_cols
        self.col = first_col
        self.rows, self.cols = half.shape
        self.plane_rows = self.rows // place.planes
        self.z_rows = self.plane_rows if by_cols else self.plane_rows // place.zs
        self.z_cols = self.cols // place.zs if by_cols else self.cols

    def z_at(self, j, base, first_col):
        if self.by_cols:
            return (pl.ds(base, self.z_rows), pl.ds(pl.multiple_of(first_col + j * self.z_cols, self.z_cols), self.z_cols))
        return (pl.ds(pl.multiple_of(base + j * self.z_rows, self.z_rows), self.z_rows), pl.ds(first_col, self.z_cols))

    def copy(self, src, dst, slot, where):
        return pltpu.make_async_remote_copy(
            src_ref=src,
            dst_ref=dst,
            send_sem=self.send.at[slot],
            recv_sem=self.recv.at[slot],
            device_id=where,
            device_id_type=pl.DeviceIdType.MESH,
        )

    def copies(self, stage):
        p = self.place
        wide = pl.ds(self.col, self.cols)
        mine = pl.multiple_of(p.plane * self.plane_rows, self.plane_rows)
        first = pl.multiple_of(p.core * self.rows, self.rows)
        if stage == 0:
            other = pl.multiple_of((1 - p.core) * self.rows, self.rows)
            return [self.copy(self.full.at[pl.ds(other, self.rows)], self.half, 0, p.pair)]
        if stage == 1:
            return [
                self.copy(
                    self.half.at[pl.ds(pl.multiple_of(j * self.plane_rows, self.plane_rows), self.plane_rows)],
                    self.plane_in.at[d],
                    1 + d,
                    where,
                )
                for d, (j, where) in enumerate(p.plane_peers)
            ]
        base = 1 + len(p.plane_peers)
        if stage == 2:
            return [
                self.copy(self.half.at[self.z_at(j, mine, 0)], self.z_in.at[d], base + d, where)
                for d, (j, where) in enumerate(p.z_peers)
            ]
        base += len(p.z_peers)
        if stage == 3:
            there = self.out.at[self.z_at(p.z, first + mine, self.col)]
            return [
                self.copy(self.half.at[self.z_at(p.z, mine, 0)], there, base + d, where)
                for d, (_, where) in enumerate(p.z_peers)
            ]
        base += len(p.z_peers)
        if stage == 4:
            there = self.out.at[pl.ds(pl.multiple_of(first + mine, self.plane_rows), self.plane_rows), wide]
            return [self.copy(there, there, base + d, where) for d, (_, where) in enumerate(p.plane_peers)]
        base += len(p.plane_peers)
        there = self.out.at[pl.ds(first, self.rows), wide]
        return [self.copy(there, there, base, p.pair)]

    def own_copy(self):
        p = self.place
        mine = pl.multiple_of(p.plane * self.plane_rows, self.plane_rows)
        first = pl.multiple_of(p.core * self.rows, self.rows)
        return pltpu.make_async_copy(
            self.half.at[self.z_at(p.z, mine, 0)],
            self.out.at[self.z_at(p.z, first + mine, self.col)],
            self.send.at[self.send.shape[0] - 1],
        )

    def step(self, stage):
        p = self.place
        mine = pl.multiple_of(p.plane * self.plane_rows, self.plane_rows)
        if stage > 0:
            for c in self.copies(stage - 1):
                c.wait_recv()
        if stage == 1:
            first = pl.multiple_of(p.core * self.rows, self.rows)
            own = self.full[pl.ds(first, self.rows), :]
            self.half[...] = (self.half[...].astype(f32) + own.astype(f32)).astype(self.half.dtype)
        if stage == 2:
            at = (pl.ds(mine, self.plane_rows), slice(None))
            value = self.half[at].astype(f32)
            for d in range(len(p.plane_peers)):
                value = value + self.plane_in[d].astype(f32)
            self.half[at] = value.astype(self.half.dtype)
        if stage == 3:
            at = self.z_at(p.z, mine, 0)
            value = self.half[at].astype(f32)
            for d in range(len(p.z_peers)):
                value = value + self.z_in[d].astype(f32)
            self.half[at] = value.astype(self.half.dtype)
            self.own_copy().start()
        if stage == 4:
            self.own_copy().wait()
        if stage < 6:
            for c in self.copies(stage):
                c.start()
        else:
            for k in range(6):
                for c in self.copies(k):
                    c.wait_send()


class Place:
    def __init__(self, zs, planes):
        self.zs, self.planes = zs, planes
        self.z, dp = lax.axis_index("sp"), lax.axis_index("dp")
        self.core, self.plane = dp % 2, dp // 2
        self.pair = self.at(self.z, self.plane * 2 + (1 - self.core))
        self.plane_peers, self.z_peers = [], []
        for d in range(1, planes):
            j = (self.plane + d) % planes
            self.plane_peers.append((j, self.at(self.z, j * 2 + self.core)))
        for d in range(1, zs):
            j = (self.z + d) % zs
            self.z_peers.append((j, self.at(j, dp)))
        self.above, self.below = self.at(self.z - 1, dp), self.at(self.z + 1, dp)

    def at(self, z, dp):
        return {"sp": z, "dp": dp}


CHUNK = 512
SMALL = 256


def backward_kernel(
    G, h, across, nf, steps, chunks, zs, planes, stages,
    ext, keep, cot, sh_in, inv2, act, slope, nm, fh_in, inv1, xhat, gdw_own,
    dw, dg, ls, pw, ew, ng, fwd_own, inv_all, spec, back,
    own_out, top_in, bot_in, gdw_out, gpw_out, gew_out, small_out,
    q_s, gres_s, gn_s, acc, gpw, gew, geb, gdb, small, halo_top, halo_bot, halo_sem, *sums,
):
    step = pl.program_id(0)
    second = steps * (1 + chunks)
    third = second + steps
    pixels = h * across
    C = sh_in.shape[-1]
    masks = Masks(h, across)
    Q = masks.quarter
    place = Place(zs, planes)
    buffers = [sums[6 * k : 6 * k + 6] for k in range(3 + chunks)]
    reduced = {"down": Sum(place, gdw_own, *buffers[0][1:], gdw_out)}
    reduced["project"] = Sum(place, *buffers[1], gpw_out)
    reduced["small"] = Sum(place, *buffers[2], small_out)
    for k in range(chunks):
        reduced[f"expand{k}"] = Sum(place, *buffers[3 + k], gew_out, first_col=k * CHUNK, by_cols=True)

    @pl.when(step == 0)
    def _():
        barrier = pltpu.get_barrier_semaphore()
        peers = [place.pair] + [w for _, w in place.plane_peers] + [w for _, w in place.z_peers]
        for where in peers:
            pl.semaphore_signal(barrier, inc=1, device_id=where, device_id_type=pl.DeviceIdType.MESH)
        pl.semaphore_wait(barrier, len(peers))
        for ref in (gpw, geb, gdb, small, acc):
            ref[...] = jnp.zeros_like(ref)

    def run(at):
        for name, stage in stages.get(at, ()):
            if stage == 0 and name == "project":
                reduced[name].full[...] = gpw[...].T.astype(bf16)
            if stage == 0 and name.startswith("expand"):
                reduced[name].full[...] = gew[...].astype(bf16)
            if stage == 0 and name == "small":
                for k in range(geb.shape[1] // C):
                    small[64 + k : 65 + k, :] = geb[:, k * C : (k + 1) * C]
                for k in range(gdb.shape[1] // C):
                    small[72 + k : 73 + k, :] = gdb[:, k * C : (k + 1) * C]
                reduced[name].full[...] = small[...]
            reduced[name].step(stage)

    for at in range(third + steps):
        if at in stages:
            pl.when(step == at)(functools.partial(run, at))

    @pl.when(step < steps)
    def _():
        g = step
        rows_here = pl.ds(pl.multiple_of(g * (G * pixels), G * pixels), G * pixels)
        ups, valids = [], []
        for b in range(G):
            valid = masks.own(ext[g * G + b, 0], ext[g * G + b, 1])
            valids.append(valid)
            ups.append(cot[b] * lanes(valid[:Q].astype(bf16), cot.shape[-1]))
        up = jnp.concatenate(ups, axis=0)
        gdb[...] += total(up.astype(f32))
        gp = dot_nt(up, dw[...])
        slabs = []
        for b in range(G):
            for k in range(4):
                slabs.append(gp[b * Q : (b + 1) * Q, k * C : (k + 1) * C])
        valid = jnp.concatenate(valids, axis=0)
        gr = jnp.concatenate(slabs, axis=0) * lanes(valid, C)
        sh = sh_in[...].astype(f32)
        small[56:57, :] += total(gr * sh)
        small[57:58, :] += total(gr)
        u = gr * dg[...]
        gres = lanes(inv2[...], C) * (u - mean(u) - sh * mean(u * sh))
        gres_s[rows_here, :] = gres.astype(bf16)
        fac = jnp.concatenate(
            [valids[b] * (keep[g * G + b].astype(f32) * (1.0 / survival)) for b in range(G)], axis=0
        )
        gb = (gres * lanes(fac, C) * ls[...]).astype(bf16)
        for b in range(G):
            q_s[g * G + b, :pixels, :] = gb[b * pixels : (b + 1) * pixels]
        small[58:59, :] += total(gb.astype(f32))
        gpw[...] += dot_tn(gb, act[...])

    @pl.when((step >= steps) & (step < second))
    def _():
        g = (step - steps) % steps
        rows_here = pl.ds(pl.multiple_of(g * (G * pixels), G * pixels), G * pixels)
        k = (step - steps) // steps
        gb = jnp.concatenate([q_s[g * G + b, :pixels, :] for b in range(G)], axis=0)
        ga = dot_nt(gb, pw[...])
        gh = (ga * slope[...].astype(f32)).astype(bf16)
        part = pl.ds(pl.multiple_of(k * CHUNK, CHUNK), CHUNK)
        geb[:, part] += total(gh.astype(f32))
        term = dot_tn(nm[...], gh)

        @pl.when(g == 0)
        def _():
            gew[...] = term

        @pl.when(g != 0)
        def _():
            gew[...] += term

        gn = dot_nt(gh, ew[...])

        @pl.when(k == 0)
        def _():
            gn_s[rows_here, :] = gn

        @pl.when(k != 0)
        def _():
            gn_s[rows_here, :] += gn

    @pl.when((step >= second) & (step < third))
    def _():
        g = step - second
        rows_here = pl.ds(pl.multiple_of(g * (G * pixels), G * pixels), G * pixels)
        kr, ki = spec[:nf], spec[nf:]
        gn = gn_s[rows_here, :]
        fh = fh_in[...].astype(f32)
        small[59:60, :] += total(gn * fh)
        small[60:61, :] += total(gn)
        w = gn * ng[...]
        gm = lanes(inv1[...], C) * (w - mean(w) - fh * mean(w * fh))
        small[61:62, :] += total(gm)
        gm = gm.astype(bf16)
        sr, si = acc[:nf], acc[nf:]
        for b in range(G):
            hat = dot(fwd_own[...], gm[b * pixels : (b + 1) * pixels])
            gr, gi = hat[:nf], hat[nf:]
            xr, xi = xhat[b, :nf].astype(f32), xhat[b, nf:].astype(f32)
            sr = sr + gr * xr + gi * xi
            si = si + gr * xi - gi * xr
            q_s[g * G + b, :nf, :] = (gr * kr + gi * ki).astype(bf16)
            q_s[g * G + b, nf:, :] = (gi * kr - gr * ki).astype(bf16)
        acc[:nf] = sr
        acc[nf:] = si

    @pl.when(step == third - 1)
    def _():
        small[0:56, :] = jnp.dot(
            back[...], acc[...], preferred_element_type=f32, precision=lax.Precision.HIGHEST
        )

    def halo(buffer, target, g, side, where):
        part = pl.ds(pl.multiple_of(g * G, G), G)
        return pltpu.make_async_remote_copy(
            src_ref=buffer.at[part],
            dst_ref=target.at[part],
            send_sem=halo_sem.at[0, side, g],
            recv_sem=halo_sem.at[1, side, g],
            device_id=where,
            device_id_type=pl.DeviceIdType.MESH,
        )

    above, below = place.above, place.below

    @pl.when(step >= third)
    def _():
        g = step - third
        for b in range(G):
            here = pl.ds(pl.multiple_of((g * G + b) * pixels, pixels), pixels)
            q = jnp.concatenate([q_s[g * G + b], gres_s[here, :]], axis=0)
            o = dot(inv_all[...], q)
            o = (o * lanes(masks.every(ext[g * G + b, 0], ext[g * G + b, 1]), C)).astype(bf16)
            halo_top[g * G + b] = o[: 3 * across]
            own_out[b] = o[3 * across : 3 * across + pixels]
            halo_bot[g * G + b] = o[3 * across + pixels :]

        @pl.when(place.z > 0)
        def _():
            halo(halo_top, bot_in, g, 0, above).start()

        @pl.when(place.z < zs - 1)
        def _():
            halo(halo_bot, top_in, g, 1, below).start()

    @pl.when(step == third + steps - 1)
    def _():
        run(third + steps)

        @pl.when(place.z > 0)
        def _():
            for g in range(steps):
                halo(halo_top, bot_in, g, 0, above).wait_send()
                halo(halo_bot, top_in, g, 1, below).wait_recv()

        @pl.when(place.z < zs - 1)
        def _():
            for g in range(steps):
                halo(halo_bot, top_in, g, 1, below).wait_send()
                halo(halo_top, bot_in, g, 0, above).wait_recv()


def schedule(steps, chunks):
    at = {
        "down": (0, 1, 4, 7, 10, 16, 18),
        "project": (4, 5, 9, 11, 13, 18, 20),
        "expand0": (8, 9, 11, 13, 15, 18, 20),
        "expand1": (12, 13, 15, 16, 17, 19, 21),
        "expand2": (16, 17, 18, 19, 20, 21, 22),
        "small": (20, 21, 22, 23, 24, 24, 24),
    }
    table = {}
    for name, when in at.items():
        for stage, step in enumerate(when):
            table.setdefault(step, []).append((name, stage))
    return table


def backward(zs, planes, G, h, across, nf, n_img, ext, keep, cot, sh, inv2, act, slope, nm, fh, inv1, xhat, gdw, *consts):
    pixels, C, CO = h * across, sh.shape[-1], cot.shape[-1]
    HID = act.shape[1]
    Q, NP, steps = pixels // 4, n_img * pixels, n_img // G
    chunks = HID // CHUNK
    second = steps * (1 + chunks)
    third = second + steps
    dw, dg, ls, pw, ew, ng, fwd_own, inv_all, spec, back = consts

    def whole(a):
        return pl.BlockSpec(a.shape, lambda t: (0,) * a.ndim, pipeline_mode=pl.Buffered(1))

    def group(first):
        return lambda t: jnp.clip(t - first, 0, steps - 1)

    def img(first, *s):
        return pl.BlockSpec((G,) + s, lambda t: (group(first)(t),) + (0,) * len(s))

    def pix(first, c):
        return pl.BlockSpec((G * pixels, c), lambda t: (group(first)(t), 0))

    def inner(t):
        n = jnp.clip(t - steps, 0, steps * chunks - 1)
        return n % steps, n // steps

    any_space = pl.BlockSpec(memory_space=pl.ANY)
    smem = pl.BlockSpec(memory_space=pltpu.SMEM)
    sds = jax.ShapeDtypeStruct

    def sum_buffers(rows, cols, by_cols, dtype, full):
        half, plane = rows // 2, rows // 2 // planes
        z = (plane, cols // zs) if by_cols else (plane // zs, cols)
        n = 2 + 2 * (planes - 1) + 2 * (zs - 1)
        return [
            pltpu.VMEM((rows, cols) if full else (16, 128), dtype),
            pltpu.VMEM((half, cols), dtype),
            pltpu.VMEM((planes - 1, plane, cols), dtype),
            pltpu.VMEM((zs - 1,) + z, dtype),
            pltpu.SemaphoreType.DMA((n + 1,)),
            pltpu.SemaphoreType.DMA((n,)),
        ]

    sums = sum_buffers(4 * C, CO, False, bf16, False)
    sums += sum_buffers(HID, C, False, bf16, True)
    sums += sum_buffers(SMALL, C, False, f32, True)
    for _ in range(chunks):
        sums += sum_buffers(C, CHUNK, True, bf16, True)
    return pl.pallas_call(
        functools.partial(
            backward_kernel, G, h, across, nf, steps, chunks, zs, planes, schedule(steps, chunks)
        ),
        grid=(third + steps,),
        in_specs=[
            smem, smem, img(0, Q, CO), pix(0, C), pix(0, 128), pix(0, HID),
            pl.BlockSpec((G * pixels, CHUNK), lambda t: inner(t)),
            pl.BlockSpec((G * pixels, C), lambda t: (inner(t)[0], 0)),
            pix(second, C), pix(second, 128), img(second, 2 * nf, C), whole(gdw),
            whole(dw), whole(dg), whole(ls),
            pl.BlockSpec((CHUNK, C), lambda t: (inner(t)[1], 0)),
            pl.BlockSpec((C, CHUNK), lambda t: (0, inner(t)[1])),
            whole(ng), whole(fwd_own), whole(inv_all), whole(spec), whole(back),
        ],
        out_specs=[img(third, pixels, C)] + [any_space] * 6,
        out_shape=[
            sds((n_img, pixels, C), bf16), sds((n_img, 3 * across, C), bf16), sds((n_img, 3 * across, C), bf16),
            sds((4 * C, CO), bf16), sds((HID, C), bf16), sds((C, HID), bf16), sds((SMALL, C), f32),
        ],
        scratch_shapes=[
            pltpu.VMEM((n_img, 2 * nf, C), bf16), pltpu.VMEM((NP, C), bf16), pltpu.VMEM((NP, C), f32),
            pltpu.VMEM((2 * nf, C), f32), pltpu.VMEM((C, HID), f32), pltpu.VMEM((C, CHUNK), f32),
            pltpu.VMEM((1, HID), f32), pltpu.VMEM((1, CO), f32), pltpu.VMEM((SMALL, C), f32),
            pltpu.VMEM((n_img, 3 * across, C), bf16), pltpu.VMEM((n_img, 3 * across, C), bf16),
            pltpu.SemaphoreType.DMA((2, 2, steps)),
        ]
        + sums,
        compiler_params=pltpu.CompilerParams(vmem_limit_bytes=VMEM, collective_id=0, has_side_effects=True),
        name="backward",
    )(ext, keep, cot, sh, inv2, act, slope, nm, fh, inv1, xhat, gdw, *consts)


def per_device(n_sp, n_dp, *arrays):
    (
        tokens, extents, keep_mask, cotangent, dw_kernel, dw_bias, norm_gain, norm_bias, expand_weight, expand_bias,
        project_weight, project_bias, layer_scale, down_gain, down_shift, down_weight, down_bias,
    ) = arrays
    n_img, h, across, C = tokens.shape
    CO, HID = cotangent.shape[-1], expand_weight.shape[1]
    pixels = h * across
    G = 1024 // pixels
    fused = n_sp == 4 and n_dp == 8 and n_img // G == 4 and HID == 3 * CHUNK
    nf, fwd, inv, fwd_own, inv_all, spectrum, back = tables(h, across)
    fwd, inv, fwd_own, inv_all = (jnp.asarray(a, bf16) for a in (fwd, inv, fwd_own, inv_all))
    back = jnp.asarray(back, f32)
    down = [(i, i + 1) for i in range(n_sp - 1)]
    up = [(i + 1, i) for i in range(n_sp - 1)]
    top = lax.ppermute(tokens[:, h - 3 :], "sp", down).reshape(n_img, 3 * across, C)
    bot = lax.ppermute(tokens[:, :3], "sp", up).reshape(n_img, 3 * across, C)
    z = lax.axis_index("sp")
    first = z * h
    ext = extents - jnp.stack([first, jnp.zeros_like(first)])[None, :]
    spec = jnp.dot(
        jnp.asarray(spectrum, f32), dw_kernel.reshape(49, C), preferred_element_type=f32, precision=lax.Precision.HIGHEST
    )
    own = tokens.reshape(n_img, pixels, C)
    cot = cotangent.reshape(n_img, pixels // 4, CO)
    row = lambda v: v.reshape(1, -1)
    dw = down_weight.reshape(4 * C, CO)
    out, act, slope, xhat, fh, nm, inv1, sh, inv2, gdw = forward(
        bf16 if fused else f32,
        G, h, across, nf, n_img, ext, keep_mask, top, own, bot, cot, fwd, inv, spec, row(dw_bias), row(norm_gain),
        row(norm_bias), expand_weight, row(expand_bias), project_weight, row(project_bias), row(layer_scale),
        row(down_gain), row(down_shift), dw, row(down_bias),
    )
    consts = (
        dw, row(down_gain), row(layer_scale), project_weight, expand_weight, row(norm_gain), fwd_own, inv_all, spec, back
    )
    saved = (ext, keep_mask, cot, sh, inv2, act, slope, nm, fh, inv1, xhat)
    if fused:
        grad, from_above, from_below, gdw, gpw, gew, small = backward(
            n_sp, n_dp // 2, G, h, across, nf, n_img, *saved, gdw, *consts
        )
        from_above = jnp.where(z > 0, from_above, jnp.zeros_like(from_above))
        from_below = jnp.where(z < n_sp - 1, from_below, jnp.zeros_like(from_below))
        gdw, gpw, gew = (a.astype(f32) for a in (gdw, gpw, gew))
        gdk, vecs, geb, gdb = small[:49], small[56:64], small[64 : 64 + HID // C].reshape(HID), small[72 : 72 + CO // C].reshape(CO)
    else:
        grad, top_g, bot_g, gpw, gew, gdk, vecs, geb, gdb = local_backward(
            G, h, across, nf, n_img, *saved, *consts
        )
        from_above = lax.ppermute(bot_g, "sp", down)
        from_below = lax.ppermute(top_g, "sp", up)
        gdw, gpw, gew, gdk, vecs, geb, gdb = lax.psum((gdw, gpw, gew, gdk, vecs, geb, gdb), ("sp", "dp"))
        gpw, gdk, geb, gdb = gpw.T, gdk[:49], geb[0], gdb[0]
    gap = ((0, 0), (0, h - 3), (0, 0), (0, 0))
    pog = ((0, 0), (h - 3, 0), (0, 0), (0, 0))
    grad = (
        grad.reshape(n_img, h, across, C).astype(f32)
        + jnp.pad(from_above.reshape(n_img, 3, across, C), gap).astype(f32)
        + jnp.pad(from_below.reshape(n_img, 3, across, C), pog).astype(f32)
    ).astype(bf16)
    gls = (jnp.sum(project_weight.astype(f32) * gpw, axis=0) + project_bias * vecs[2]) / layer_scale
    return (
        out.reshape(n_img, h // 2, across // 2, CO), grad, gdk.reshape(7, 7, C), vecs[5], vecs[3], vecs[4], gew,
        geb, gpw, vecs[2], gls, vecs[0], vecs[1], gdw.reshape(down_weight.shape), gdb,
    )


def solution(mesh):
    maps = P("dp", "sp", None, None)
    return jax.shard_map(
        functools.partial(per_device, mesh.shape["sp"], mesh.shape["dp"]),
        mesh=mesh,
        in_specs=(maps, P("dp", None), P("dp"), maps) + (P(),) * 13,
        out_specs=(maps, maps) + (P(),) * 13,
        check_vma=False,
    )
```

```python
import functools

import jax
import jax.numpy as jnp
import numpy as np
from jax import lax
from jax.experimental import pallas as pl
from jax.experimental.pallas import tpu as pltpu
from jax.sharding import PartitionSpec as P

bf16 = jnp.bfloat16
f32 = jnp.float32
epsilon = 1e-06
survival = 0.875
VMEM = 63 * 1024 * 1024
MESH = pl.DeviceIdType.MESH
EARLY = 1024
DWB, NG, NB, PB, LS, DG, DS, DB, EB = 0, 1, 2, 3, 4, 5, 6, 7, 9
SMALL, V_DG, V_DS, V_PB, V_NG, V_NB, V_DWB, V_EB, V_DB = 128, 56, 57, 58, 59, 60, 61, 64, 72


def tables(h, across):
    nr, nc = h + 6, across + 3
    us, vs, ms = [], [], []
    for v in range(nc // 2 + 1):
        for u in range(nr):
            mu, mv = (-u) % nr, (-v) % nc
            if (mv, mu) < (v, u):
                continue
            us.append(u)
            vs.append(v)
            ms.append(1.0 if (mu, mv) == (u, v) else 2.0)
    n = len(us)
    nf = -(-n // 128) * 128
    us, vs, ms = (np.array(a + [0] * (nf - n), np.float64) for a in (us, vs, ms))
    live = (np.arange(nf) < n)[:, None]

    def angle(r, c):
        turns = (np.outer(us, r.ravel()) * nc + np.outer(vs, c.ravel()) * nr) % (nr * nc)
        return 2 * np.pi * turns / (nr * nc)

    def waves(a):
        return np.concatenate([np.cos(a) * live, -np.sin(a) * live])

    every = waves(angle(*np.meshgrid(np.arange(h + 6), np.arange(across), indexing="ij")))
    own = waves(angle(*np.meshgrid(np.arange(h), np.arange(across), indexing="ij")))
    ki, kj = np.meshgrid(np.arange(7), np.arange(8) - 3, indexing="ij")
    taps = angle(ki, kj)
    weight = (ms / (nr * nc))[:, None] * (kj.ravel() < 4)[None, :]
    spectrum = np.concatenate([np.cos(taps) * weight, np.sin(taps) * weight])
    back = np.concatenate([np.cos(taps) * weight, -np.sin(taps) * weight]).T
    return nf, every, own.T, own, every.T, spectrum, back


def dot(a, b):
    return jnp.dot(a, b, preferred_element_type=f32)


def dot_nt(a, b):
    return lax.dot_general(a, b, (((1,), (1,)), ((), ())), preferred_element_type=f32)


def dot_tn(a, b):
    return lax.dot_general(a, b, (((0,), (0,)), ((), ())), preferred_element_type=f32)


def dot_exact(a, b):
    return jnp.dot(a, b, preferred_element_type=f32, precision=lax.Precision.HIGHEST)


def mean(x):
    return jnp.sum(x, axis=-1, keepdims=True) * (1.0 / x.shape[-1])


def total(x):
    return jnp.sum(x, axis=0, keepdims=True)


def lanes(x, width):
    return jnp.concatenate([x] * (width // x.shape[1]), axis=1)


def stack(parts, axis):
    return parts[0] if len(parts) == 1 else jnp.concatenate(parts, axis=axis)


def gelu_parts(v):
    u = v * v
    p = 0.7978667366454887 + u * (
        0.03640226973029483
        + u * (-9.53235048862514e-05 + u * (-3.491248211005391e-05 + u * 1.3019431827058075e-06))
    )
    phi = 0.5 + 0.5 * jnp.tanh(v * p)
    density = jnp.exp2(u * -0.7213475204444817 - 1.3257480647361595)
    return v * phi, phi + v * density


class Masks:
    def __init__(self, h, across):
        n = lax.broadcasted_iota(jnp.int32, ((h + 6) * across, 128), 0)
        self.row, self.col = (n >> (across.bit_length() - 1)) - 3, n & (across - 1)
        self.own_rows = slice(3 * across, (3 + h) * across)
        q = lax.broadcasted_iota(jnp.int32, (h * across // 4, 128), 0)
        half = across // 2
        self.coarse_row, self.coarse_col = 2 * (q >> (half.bit_length() - 1)), 2 * (q & (half - 1))

    def every(self, rows, cols):
        return ((self.row < rows) & (self.col < cols)).astype(f32)

    def own(self, rows, cols):
        r, c = self.row[self.own_rows], self.col[self.own_rows]
        return ((r < rows) & (c < cols)).astype(f32)

    def coarse(self, rows, cols):
        return ((self.coarse_row < rows) & (self.coarse_col < cols)).astype(f32)


def remote(src, dst, send, recv, where):
    return pltpu.make_async_remote_copy(
        src_ref=src, dst_ref=dst, send_sem=send, recv_sem=recv, device_id=where, device_id_type=MESH
    )


def greet(peers):
    barrier = pltpu.get_barrier_semaphore()
    for where in peers:
        pl.semaphore_signal(barrier, inc=1, device_id=where, device_id_type=MESH)
    pl.semaphore_wait(barrier, len(peers))


def tap_rows(dwk):
    gap = jnp.zeros((1, dwk.shape[-1]), f32)
    return jnp.concatenate([x for i in range(7) for x in (dwk[i], gap)], axis=0)


def forward_kernel(
    G, T, h, across, nf, zs, steps,
    ext, keep, tok, own, cot, fwd, inv, taps, dwk, vec, ew, pw, dw,
    out, act, slope_early, slope_late, xhat, fh_out, nm, inv1_out, sh_out, inv2_out, gdw,
    top, bot, spec, red, gdw_s, sem,
):
    g = pl.program_id(0)
    pixels = h * across
    edge = 3 * across
    C = own.shape[-1]
    z, dp = lax.axis_index("sp"), lax.axis_index("dp")
    above, below = {"sp": z - 1, "dp": dp}, {"sp": z + 1, "dp": dp}

    def halo(k, up):
        part = pl.ds(k * G, G)
        if up:
            return remote(tok.at[part, pl.ds(0, edge)], bot.at[part], sem.at[0, 0, k], sem.at[1, 0, k], above)
        return remote(tok.at[part, pl.ds(pixels - edge, edge)], top.at[part], sem.at[0, 1, k], sem.at[1, 1, k], below)

    def each(k, up_act, down_act):
        if up_act is not None:
            pl.when(z > 0)(lambda: up_act(halo(k, True)))
        if down_act is not None:
            pl.when(z < zs - 1)(lambda: down_act(halo(k, False)))

    @pl.when(g == 0)
    def _():
        greet([{"sp": (z + 1) % zs, "dp": dp}, {"sp": (z + zs - 1) % zs, "dp": dp}])
        for k in range(steps):
            each(k, lambda c: c.start(), lambda c: c.start())

        @pl.when(z == 0)
        def _():
            top[...] = jnp.zeros_like(top)

        @pl.when(z == zs - 1)
        def _():
            bot[...] = jnp.zeros_like(bot)

        spec[...] = dot_exact(taps[...], tap_rows(dwk))

    for k in range(steps):

        @pl.when(g == k)
        def _():
            pl.when(z < zs - 1)(lambda: halo(k, True).wait_recv())
            pl.when(z > 0)(lambda: halo(k, False).wait_recv())

    masks = Masks(h, across)
    kr, ki = lanes(spec[:nf], T * C), lanes(spec[nf:], T * C)
    eb = jnp.concatenate([vec[EB + k : EB + k + 1, :] for k in range(ew.shape[1] // C)], axis=1)
    db = jnp.concatenate([vec[DB + k : DB + k + 1, :] for k in range(cot.shape[-1] // C)], axis=1)
    HC = 512
    for team in range(G // T):
        xs, fields, valids, facs = [], [], [], []
        for t in range(T):
            b = team * T + t
            rows, cols = ext[g * G + b, 0], ext[g * G + b, 1]
            x = jnp.concatenate([top[g * G + b], own[b], bot[g * G + b]], axis=0)
            every = masks.every(rows, cols)
            x = x * lanes(every.astype(bf16), C)
            xs.append(x)
            fields.append(x[masks.own_rows])
            valids.append(every[masks.own_rows])
            facs.append(valids[-1] * (keep[g * G + b].astype(f32) * (1.0 / survival)))
        hat = dot(fwd[...], stack(xs, 1))
        xr, xi = hat[:nf], hat[nf:]
        for t in range(T):
            xhat[team * T + t] = hat[:, t * C : (t + 1) * C].astype(bf16)
        product = jnp.concatenate(
            [(xr * kr - xi * ki).astype(bf16), (xr * ki + xi * kr).astype(bf16)], axis=0
        )
        mixed = dot(inv[...], product)
        mixed = stack([mixed[:, t * C : (t + 1) * C] for t in range(T)], 0) + vec[DWB : DWB + 1, :]
        here = pl.ds(team * T * pixels, T * pixels)
        d = mixed - mean(mixed)
        inv1 = lax.rsqrt(mean(d * d) + epsilon)
        fh = d * inv1
        fh_out[here, :] = fh.astype(bf16)
        inv1_out[here, :] = jnp.broadcast_to(inv1, (T * pixels, 128))
        normed = (fh * vec[NG : NG + 1, :] + vec[NB : NB + 1, :]).astype(bf16)
        nm[here, :] = normed
        branch = vec[PB : PB + 1, :]
        for k in range(ew.shape[1] // HC):
            part = slice(k * HC, (k + 1) * HC)
            a, s = gelu_parts(dot(normed, ew[:, part]) + eb[:, part])
            a = a.astype(bf16)
            act[here, part] = a
            if k * HC < EARLY:
                slope_early[here, part] = s.astype(bf16)
            else:
                slope_late[here, k * HC - EARLY : (k + 1) * HC - EARLY] = s.astype(bf16)
            branch = branch + dot(a, pw[part, :])
        valid, fac = stack(valids, 0), stack(facs, 0)
        res = stack(fields, 0).astype(f32) + lanes(fac, C) * (branch * vec[LS : LS + 1, :])
        d = res - mean(res)
        inv2 = lax.rsqrt(mean(d * d) + epsilon)
        sh = d * inv2
        sh_out[here, :] = sh.astype(bf16)
        inv2_out[here, :] = jnp.broadcast_to(inv2, (T * pixels, 128))
        reduced = (sh * vec[DG : DG + 1, :] + vec[DS : DS + 1, :]) * lanes(valid, C)
        rows_here = T * h // 2
        for k in range(C // 128):
            slab = reduced[:, k * 128 : (k + 1) * 128].reshape(rows_here, 2, across, 128)
            red[k, team * rows_here : (team + 1) * rows_here] = slab
    patch = jnp.concatenate(
        [
            red[k, :, p, pl.ds(q, across // 2, stride=2), :].reshape(G * pixels // 4, 128).astype(bf16)
            for p in range(2)
            for q in range(2)
            for k in range(C // 128)
        ],
        axis=1,
    )
    coarse = stack([masks.coarse(ext[g * G + b, 0], ext[g * G + b, 1]) for b in range(G)], 0)
    coarse = lanes(coarse, cot.shape[-1])
    up = cot[...].reshape(coarse.shape) * coarse.astype(bf16)
    out[...] = ((dot(patch, dw[...]) + db) * coarse).astype(bf16).reshape(out.shape)
    term = dot_tn(patch, up)

    @pl.when(g == 0)
    def _():
        gdw_s[...] = term

    @pl.when(g != 0)
    def _():
        gdw_s[...] += term

    @pl.when(g == steps - 1)
    def _():
        gdw[...] = gdw_s[...].astype(gdw.dtype)
        for k in range(steps):
            each(k, lambda c: c.wait_send(), lambda c: c.wait_send())


def whole(a):
    return pl.BlockSpec(a.shape, lambda t: (0,) * a.ndim, pipeline_mode=pl.Buffered(1))


def forward(sum_type, zs, G, T, h, across, nf, n_img, ext, keep, own, cot, *consts):
    pixels, C, CO = h * across, own.shape[-1], cot.shape[-1]
    HID = consts[-3].shape[1]
    Q, NP, steps = pixels // 4, n_img * pixels, n_img // G

    def img(*s):
        return pl.BlockSpec((G,) + s, lambda g: (g,) + (0,) * len(s))

    def pix(c):
        return pl.BlockSpec((G * pixels, c), lambda g: (g, 0))

    smem = pl.BlockSpec(memory_space=pltpu.SMEM)
    sds = jax.ShapeDtypeStruct
    return pl.pallas_call(
        functools.partial(forward_kernel, G, T, h, across, nf, zs, steps),
        grid=(steps,),
        in_specs=[smem, smem, pl.BlockSpec(memory_space=pl.ANY), img(pixels, C), img(Q, CO)] + [whole(a) for a in consts],
        out_specs=[
            img(Q, CO), pix(HID), pix(EARLY), pix(HID - EARLY), img(2 * nf, C), pix(C), pix(C), pix(128), pix(C), pix(128),
            pl.BlockSpec((4 * C, CO), lambda g: (0, 0)),
        ],
        out_shape=[
            sds((n_img, Q, CO), bf16), sds((NP, HID), bf16), sds((NP, EARLY), bf16), sds((NP, HID - EARLY), bf16), sds((n_img, 2 * nf, C), bf16),
            sds((NP, C), bf16), sds((NP, C), bf16), sds((NP, 128), f32), sds((NP, C), bf16), sds((NP, 128), f32),
            sds((4 * C, CO), sum_type),
        ],
        scratch_shapes=[
            pltpu.VMEM((n_img, 3 * across, C), bf16), pltpu.VMEM((n_img, 3 * across, C), bf16),
            pltpu.VMEM((2 * nf, C), f32), pltpu.VMEM((C // 128, G * h // 2, 2, across, 128), f32), pltpu.VMEM((4 * C, CO), f32),
            pltpu.SemaphoreType.DMA((2, 2, steps)),
        ],
        compiler_params=pltpu.CompilerParams(vmem_limit_bytes=VMEM, collective_id=1, has_side_effects=True),
        name="forward",
    )(ext, keep, own, own, cot, *consts)


class Place:
    def __init__(self, zs):
        self.z, self.dp = lax.axis_index("sp"), lax.axis_index("dp")
        self.core, self.chip = self.dp % 2, self.dp // 2
        self.pair = self.at(self.z, self.dp + 1 - 2 * self.core)
        self.above, self.below = self.at(self.z - 1, self.dp), self.at(self.z + 1, self.dp)
        self.plane, self.column, self.others = [], [], []
        for d in range(1, 4):
            j = (self.chip + d) % 4
            self.plane.append((j, self.at(self.z, j * 2 + self.core)))
        for d in range(1, zs):
            j = (self.z + d) % zs
            self.column.append((j, self.at(j, self.dp)))
        self.me = self.z * 4 + self.chip
        for d in range(1, 4 * zs):
            j = (self.me + d) % (4 * zs)
            self.others.append((j, self.at(j // 4, (j % 4) * 2 + self.core)))

    def at(self, z, dp):
        return {"sp": z, "dp": dp}


class Sum:
    def __init__(self, place, zs, full, half, plane_in, z_in, send, recv, out, by_cols=False):
        self.place, self.full, self.half, self.plane_in, self.z_in = place, full, half, plane_in, z_in
        self.send, self.recv, self.out, self.by_cols = send, recv, out, by_cols
        p = place
        self.R, self.cols = half.shape
        self.rows = self.R // 4
        self.base = pl.multiple_of(p.core * self.R, self.R)
        self.other = pl.multiple_of((1 - p.core) * self.R, self.R)
        self.mine = pl.multiple_of(p.chip * self.rows, self.rows)
        self.z_rows = self.rows if by_cols else self.rows // zs
        self.z_cols = self.cols // zs if by_cols else self.cols

    def z_at(self, j, base):
        if self.by_cols:
            return (pl.ds(base, self.z_rows), pl.ds(pl.multiple_of(j * self.z_cols, self.z_cols), self.z_cols))
        return (pl.ds(pl.multiple_of(base + j * self.z_rows, self.z_rows), self.z_rows), slice(None))

    def copies(self, stage):
        p, n = self.place, len(self.place.column)
        slot = (0, 1, 4, 4 + n, 4 + 2 * n, 7 + 2 * n)[stage]

        def copy(src, dst, where, d=0):
            return remote(src, dst, self.send.at[slot + d], self.recv.at[slot + d], where)

        if stage == 0:
            return [copy(self.full.at[pl.ds(self.other, self.R)], self.half, p.pair)]
        if stage == 1:
            return [
                copy(
                    self.half.at[pl.ds(pl.multiple_of(j * self.rows, self.rows), self.rows)],
                    self.plane_in.at[d],
                    where,
                    d,
                )
                for d, (j, where) in enumerate(p.plane)
            ]
        if stage == 2:
            return [
                copy(self.half.at[self.z_at(j, self.mine)], self.z_in.at[d], where, d)
                for d, (j, where) in enumerate(p.column)
            ]
        if stage == 3:
            src, dst = self.own()
            return [copy(src, dst, where, d) for d, (_, where) in enumerate(p.column)]
        if stage == 4:
            there = self.out.at[pl.ds(pl.multiple_of(self.base + self.mine, self.rows), self.rows)]
            return [copy(there, there, where, d) for d, (_, where) in enumerate(p.plane)]
        there = self.out.at[pl.ds(self.base, self.R)]
        return [copy(there, there, p.pair)]

    def own(self):
        p = self.place
        return self.half.at[self.z_at(p.z, self.mine)], self.out.at[self.z_at(p.z, self.base + self.mine)]

    def own_copy(self):
        src, dst = self.own()
        return pltpu.make_async_copy(src, dst, self.send.at[self.send.shape[0] - 1])

    def add(self, at, parts):
        value = self.half[at].astype(f32)
        for part in parts:
            value = value + part.astype(f32)
        self.half[at] = value.astype(self.half.dtype)

    def step(self, stage):
        if stage > 0:
            for c in self.copies(stage - 1):
                c.wait_recv()
        if stage == 1:
            self.add((slice(None), slice(None)), [self.full[pl.ds(self.base, self.R), :]])
        if stage == 2:
            self.add((pl.ds(self.mine, self.rows), slice(None)), [self.plane_in[d] for d in range(3)])
        if stage == 3:
            n = len(self.place.column)
            self.add(self.z_at(self.place.z, self.mine), [self.z_in[d] for d in range(n)])
            self.own_copy().start()
        if stage == 4:
            self.own_copy().wait()
        if stage < 6:
            for c in self.copies(stage):
                c.start()
        else:
            for k in range(6):
                for c in self.copies(k):
                    c.wait_send()


class SmallSum:
    def __init__(self, place, zs, full, pair_in, rows_in, send, recv, out):
        self.place, self.full, self.pair_in, self.rows_in = place, full, pair_in, rows_in
        self.send, self.recv, self.out = send, recv, out
        p = place
        n = self.n = 4 * zs
        self.rows = full.shape[0] // n
        self.me, self.others = p.me, p.others

    def part(self, j):
        return pl.ds(pl.multiple_of(j * self.rows, self.rows), self.rows)

    def copies(self, stage):
        n = self.n
        if stage == 0:
            return [remote(self.full, self.pair_in, self.send.at[0], self.recv.at[0], self.place.pair)]
        out = []
        for d, (j, where) in enumerate(self.others):
            slot = (stage - 1) * (n - 1) + 1 + d
            if stage == 1:
                src, dst = self.full.at[self.part(j)], self.rows_in.at[d]
            else:
                src, dst = self.full.at[self.part(self.me)], self.out.at[self.part(self.me)]
            out.append(remote(src, dst, self.send.at[slot], self.recv.at[slot], where))
        return out

    def own_copy(self):
        return pltpu.make_async_copy(
            self.full.at[self.part(self.me)], self.out.at[self.part(self.me)], self.send.at[self.send.shape[0] - 1]
        )

    def step(self, stage):
        if stage > 0:
            for c in self.copies(stage - 1):
                c.wait_recv()
        if stage == 1:
            for c in self.copies(0):
                c.wait_send()
            self.full[...] += self.pair_in[...]
        if stage == 2:
            value = self.full[self.part(self.me), :]
            for d in range(self.n - 1):
                value = value + self.rows_in[d]
            self.full[self.part(self.me), :] = value
            self.own_copy().start()
        if stage < 3:
            for c in self.copies(stage):
                c.start()
        else:
            self.own_copy().wait()
            for k in (1, 2):
                for c in self.copies(k):
                    c.wait_send()


class LateSum:
    def __init__(self, place, zs, full, half, parts_in, send, recv, out):
        self.place, self.full, self.half, self.parts_in = place, full, half, parts_in
        self.send, self.recv, self.out, self.zs = send, recv, out, zs
        p = place
        n = self.n = 4 * zs
        self.R = half.shape[0]
        self.rows, self.cols = half.shape[0] // 4, half.shape[1] // zs
        self.base = pl.multiple_of(p.core * self.R, self.R)
        self.me, self.others = p.me, p.others

    def part(self, j, base):
        return (
            pl.ds(pl.multiple_of(base + (j % 4) * self.rows, self.rows), self.rows),
            pl.ds(pl.multiple_of((j // 4) * self.cols, self.cols), self.cols),
        )

    def copies(self, stage):
        p, n = self.place, self.n
        if stage == 0:
            other = pl.multiple_of((1 - p.core) * self.R, self.R)
            return [remote(self.full.at[pl.ds(other, self.R)], self.half, self.send.at[0], self.recv.at[0], p.pair)]
        if stage == 3:
            there = self.out.at[pl.ds(self.base, self.R)]
            return [remote(there, there, self.send.at[2 * n - 1], self.recv.at[2 * n - 1], p.pair)]
        out = []
        for d, (j, where) in enumerate(self.others):
            slot = (stage - 1) * (n - 1) + 1 + d
            if stage == 1:
                src, dst = self.half.at[self.part(j, 0)], self.parts_in.at[d]
            else:
                src, dst = self.half.at[self.part(self.me, 0)], self.out.at[self.part(self.me, self.base)]
            out.append(remote(src, dst, self.send.at[slot], self.recv.at[slot], where))
        return out

    def own_copy(self):
        return pltpu.make_async_copy(
            self.half.at[self.part(self.me, 0)], self.out.at[self.part(self.me, self.base)], self.send.at[2 * self.n]
        )

    def step(self, stage):
        if stage > 0:
            for c in self.copies(stage - 1):
                c.wait_recv()
        if stage == 1:
            own = self.full[pl.ds(self.base, self.R), :].astype(f32)
            self.half[...] = (self.half[...].astype(f32) + own).astype(self.half.dtype)
        if stage == 2:
            at = self.part(self.me, 0)
            value = self.half[at].astype(f32)
            for d in range(self.n - 1):
                value = value + self.parts_in[d].astype(f32)
            self.half[at] = value.astype(self.half.dtype)
            self.own_copy().start()
        if stage == 3:
            self.own_copy().wait()
        if stage < 4:
            for c in self.copies(stage):
                c.start()
        else:
            for k in range(4):
                for c in self.copies(k):
                    c.wait_send()


def backward_kernel(
    G, T, h, across, nf, steps, zs, stages,
    ext, keep, cot, sh_in, inv2, act, slope_early, slope_late, nm, fh_in, inv1, xhat, gdw_own,
    dw, vec, pw, ew, fwd_own, inv_all, taps, dwk, back,
    own_out, top_in, bot_in, gdw_out, gpw_out, gew_out, small_out,
    held, gres_s, gn_s, gr_s, acc, spec, gpw, gew, geb, small, halo_sem, *sums,
):
    step = pl.program_id(0)
    pixels = h * across
    C, HID = sh_in.shape[-1], act.shape[-1]
    HC = 512
    masks = Masks(h, across)
    place = Place(zs)
    names = ("down", "project", "early")
    outs = (gdw_out, gpw_out, gew_out.at[:, pl.ds(0, EARLY)])
    reduced = {}
    if stages is not None:
        for k, name in enumerate(names):
            buffers = list(sums[6 * k : 6 * k + 6])
            if name == "down":
                buffers[0] = gdw_own
            reduced[name] = Sum(place, zs, *buffers, outs[k], by_cols=name == "early")
        reduced["late"] = LateSum(place, zs, *sums[22:27], gew_out.at[:, pl.ds(EARLY, HID - EARLY)])
        reduced["small"] = SmallSum(place, zs, small, *sums[18:22], small_out)

    peers = [place.pair] + [w for _, w in place.others] if stages is not None else [w for _, w in place.column]

    @pl.when(step == 0)
    def _():
        barrier = pltpu.get_barrier_semaphore()
        for where in peers:
            pl.semaphore_signal(barrier, inc=1, device_id=where, device_id_type=MESH)
        for ref in (gpw, gew, geb, small, acc):
            ref[...] = jnp.zeros_like(ref)
        spec[...] = dot_exact(taps[...], tap_rows(dwk))

    @pl.when(step == 1)
    def _():
        pl.semaphore_wait(pltpu.get_barrier_semaphore(), len(peers))

    def run(at):
        for name, stage in stages.get(at, ()):
            if stage == 0 and name == "project":
                reduced[name].full[...] = gpw[...].T.astype(bf16)
            if stage == 0 and name == "early":
                reduced[name].full[...] = gew[:, :EARLY].astype(bf16)
            if stage == 0 and name == "late":
                reduced[name].full[...] = gew[:, EARLY:].astype(bf16)
            reduced[name].step(stage)

    if stages is not None:
        for at in range(4 * steps):
            if at in stages:
                pl.when(step == at)(functools.partial(run, at))

    def row(k):
        return vec[k : k + 1, :]

    def extent(b, g):
        return ext[g * G + b, 0], ext[g * G + b, 1]

    @pl.when(step < steps)
    def _():
        g = step
        coarse = lanes(stack([masks.coarse(*extent(b, g)) for b in range(G)], 0).astype(bf16), cot.shape[-1])
        up = cot[...].reshape(coarse.shape) * coarse
        gdb = total(up.astype(f32))
        for k in range(cot.shape[-1] // C):
            small[V_DB + k : V_DB + k + 1, :] += gdb[:, k * C : (k + 1) * C]
        for p in range(2):
            for q in range(2):
                k = 2 * p + q
                slab = dot_nt(up, dw[k * C : (k + 1) * C, :])
                for n in range(C // 128):
                    gr_s[n, :, p, pl.ds(q, across // 2, stride=2), :] = slab[:, n * 128 : (n + 1) * 128].reshape(
                        G * h // 2, across // 2, 128
                    )
        for team in range(G // T):
            here = pl.ds(team * T * pixels, T * pixels)
            valids = [masks.own(*extent(team * T + t, g)) for t in range(T)]
            facs = [
                valids[t] * (keep[g * G + team * T + t].astype(f32) * (1.0 / survival)) for t in range(T)
            ]
            rows = T * h // 2
            gr = stack(
                [gr_s[n, team * rows : (team + 1) * rows].reshape(T * pixels, 128) for n in range(C // 128)], 1
            )
            gr = gr * lanes(stack(valids, 0), C)
            sh = sh_in[here, :].astype(f32)
            small[V_DG : V_DG + 1, :] += total(gr * sh)
            small[V_DS : V_DS + 1, :] += total(gr)
            u = gr * row(DG)
            gres = lanes(inv2[here, :], C) * (u - mean(u) - sh * mean(u * sh))
            first = pl.multiple_of(g * (G * pixels) + team * T * pixels, T * pixels)
            gres_s[pl.ds(first, T * pixels), :] = gres.astype(bf16)
            gb = (gres * lanes(stack(facs, 0), C) * row(LS)).astype(bf16)
            for t in range(T):
                held[g * G + team * T + t, :pixels] = gb[t * pixels : (t + 1) * pixels]
            small[V_PB : V_PB + 1, :] += total(gb.astype(f32))
            gpw[...] += dot_tn(gb, act[here, :])

    def hidden_back(g, team, slope, columns):
        here = pl.ds(team * T * pixels, T * pixels)
        gb = stack([held[g * G + team * T + t, :pixels] for t in range(T)], 0)
        gn = None
        for first in range(columns.start, columns.stop, HC):
            part = slice(first, first + HC)
            own = slice(first - columns.start, first - columns.start + HC)
            gh = (dot_nt(gb, pw[part, :]) * slope[here, own].astype(f32)).astype(bf16)
            geb[:, part] += total(gh.astype(f32))
            gew[:, part] += dot_tn(nm[here, :], gh)
            term = dot_nt(gh, ew[:, part])
            gn = term if gn is None else gn + term
        return gn

    @pl.when((step >= steps) & (step < 2 * steps))
    def _():
        g = step - steps
        for team in range(G // T):
            gn = hidden_back(g, team, slope_early, slice(0, EARLY))
            gn_s[pl.ds(pl.multiple_of(g * (G * pixels) + team * T * pixels, T * pixels), T * pixels), :] = gn

    @pl.when((step >= 2 * steps) & (step < 3 * steps))
    def _():
        g = step - 2 * steps
        for team in range(G // T):
            gn = hidden_back(g, team, slope_late, slice(EARLY, HID))
            gn_s[pl.ds(pl.multiple_of(g * (G * pixels) + team * T * pixels, T * pixels), T * pixels), :] += gn

    def halo(target, g, side, where):
        part, edge = pl.ds(pl.multiple_of(g * G, G), G), 3 * across
        src = held.at[part, pl.ds(side * edge, edge)]
        return remote(src, target.at[part], halo_sem.at[0, side, g], halo_sem.at[1, side, g], where)

    def up(g):
        return halo(bot_in, g, 0, place.above)

    def down(g):
        return halo(top_in, g, 1, place.below)

    @pl.when(step >= 3 * steps)
    def _():
        g = step - 3 * steps
        edge = 3 * across
        kr, ki = lanes(spec[:nf], T * C), lanes(spec[nf:], T * C)
        for team in range(G // T):
            here = pl.ds(team * T * pixels, T * pixels)
            first = pl.multiple_of(g * (G * pixels) + team * T * pixels, T * pixels)
            gn = gn_s[pl.ds(first, T * pixels), :]
            fh = fh_in[here, :].astype(f32)
            small[V_NG : V_NG + 1, :] += total(gn * fh)
            small[V_NB : V_NB + 1, :] += total(gn)
            w = gn * row(NG)
            gm = lanes(inv1[here, :], C) * (w - mean(w) - fh * mean(w * fh))
            small[V_DWB : V_DWB + 1, :] += total(gm)
            gm = gm.astype(bf16)
            gm = stack([gm[t * pixels : (t + 1) * pixels] for t in range(T)], 1)
            hat = dot(fwd_own[...], gm)
            gr, gi = hat[:nf], hat[nf:]
            sr, si = acc[:nf], acc[nf:]
            for t in range(T):
                at = slice(t * C, (t + 1) * C)
                xr, xi = xhat[team * T + t, :nf].astype(f32), xhat[team * T + t, nf:].astype(f32)
                sr = sr + gr[:, at] * xr + gi[:, at] * xi
                si = si + gr[:, at] * xi - gi[:, at] * xr
            acc[:nf] = sr
            acc[nf:] = si
            product = jnp.concatenate(
                [(gr * kr + gi * ki).astype(bf16), (gi * kr - gr * ki).astype(bf16)], axis=0
            )
            o = dot(inv_all[...], product)
            for t in range(T):
                b = g * G + team * T + t
                each = o[:, t * C : (t + 1) * C] * lanes(masks.every(ext[b, 0], ext[b, 1]), C)
                held[b, :edge] = each[:edge].astype(bf16)
                own = gres_s[pl.ds(pl.multiple_of(b * pixels, pixels), pixels), :].astype(f32)
                own_out[team * T + t] = (each[edge : edge + pixels] + own).astype(bf16)
                held[b, edge : 2 * edge] = each[edge + pixels :].astype(bf16)
        pl.when(place.z > 0)(lambda: up(g).start())
        pl.when(place.z < zs - 1)(lambda: down(g).start())

    @pl.when(step == 4 * steps - 1)
    def _():
        small[0:56, :] = dot_exact(back[...], acc[...])
        for k in range(HID // C):
            small[V_EB + k : V_EB + k + 1, :] = geb[:, k * C : (k + 1) * C]
        if stages is not None:
            run(4 * steps)
        else:
            for k, (src, dst) in enumerate(((gpw, gpw_out), (gew, gew_out), (small, small_out))):
                c = pltpu.make_async_copy(src, dst, sums[0].at[k])
                c.start()
                c.wait()

        @pl.when(place.z > 0)
        def _():
            for g in range(steps):
                up(g).wait_send()
                down(g).wait_recv()

        @pl.when(place.z < zs - 1)
        def _():
            for g in range(steps):
                down(g).wait_send()
                up(g).wait_recv()


def schedule():
    at = {
        "down": (1, 2, 7, 10, 13),
        "project": (4, 5, 9, 12, 14),
        "early": (8, 9, 12, 14, 15),
        "late": (12, 13, 15),
    }
    table = {}
    for name, when in at.items():
        for stage, step in enumerate(when):
            table.setdefault(step, []).append((name, stage))
    d, p, e, q, s = "down", "project", "early", "late", "small"
    table[16] = [
        (s, 0), (d, 5), (s, 1), (p, 5), (e, 5), (q, 3), (s, 2), (d, 6), (p, 6), (e, 6), (q, 4), (s, 3),
    ]
    return table


def backward(fused, zs, G, T, h, across, nf, n_img, ext, keep, cot, sh, inv2, act, slope_early, slope_late, nm, fh, inv1, xhat, gdw, *consts):
    pixels, C, CO = h * across, sh.shape[-1], cot.shape[-1]
    HID = act.shape[1]
    Q, NP, steps = pixels // 4, n_img * pixels, n_img // G

    def group(first):
        return lambda t: jnp.clip(t - first, 0, steps - 1)

    def img(first, *s):
        return pl.BlockSpec((G,) + s, lambda t: (group(first)(t),) + (0,) * len(s))

    def pix(first, c):
        return pl.BlockSpec((G * pixels, c), lambda t: (group(first)(t), 0))

    any_space = pl.BlockSpec(memory_space=pl.ANY)
    smem = pl.BlockSpec(memory_space=pltpu.SMEM)
    sds = jax.ShapeDtypeStruct

    def sum_buffers(rows, cols, by_cols, dtype, full):
        half = rows // 2
        z = (half // 4, cols // zs) if by_cols else (half // 4 // zs, cols)
        n = 8 + 2 * (zs - 1)
        return [
            pltpu.VMEM((rows, cols) if full else (16, 128), dtype),
            pltpu.VMEM((half, cols), dtype),
            pltpu.VMEM((3, half // 4, cols), dtype),
            pltpu.VMEM((zs - 1,) + z, dtype),
            pltpu.SemaphoreType.DMA((n + 1,)),
            pltpu.SemaphoreType.DMA((n,)),
        ]

    if fused:
        sums = sum_buffers(4 * C, CO, False, bf16, False)
        sums += sum_buffers(HID, C, False, bf16, True)
        sums += sum_buffers(C, EARLY, True, bf16, True)
        n = 4 * zs
        sums += [
            pltpu.VMEM((SMALL, C), f32),
            pltpu.VMEM((n - 1, SMALL // n, C), f32),
            pltpu.SemaphoreType.DMA((2 * n,)),
            pltpu.SemaphoreType.DMA((2 * n - 1,)),
        ]
        late = HID - EARLY
        sums += [
            pltpu.VMEM((C, late), bf16),
            pltpu.VMEM((C // 2, late), bf16),
            pltpu.VMEM((n - 1, C // 8, late // zs), bf16),
            pltpu.SemaphoreType.DMA((2 * n + 1,)),
            pltpu.SemaphoreType.DMA((2 * n,)),
        ]
        results = [sds((4 * C, CO), bf16), sds((HID, C), bf16), sds((C, HID), bf16)]
    else:
        sums = [pltpu.SemaphoreType.DMA((3,))]
        results = [sds((16, 128), bf16), sds((C, HID), f32), sds((C, HID), f32)]
        gdw = gdw[:16, :128]
    return pl.pallas_call(
        functools.partial(backward_kernel, G, T, h, across, nf, steps, zs, schedule() if fused else None),
        grid=(4 * steps,),
        in_specs=[
            smem, smem, img(0, Q, CO), pix(0, C), pix(0, 128), pix(0, HID), pix(steps, EARLY),
            pl.BlockSpec((G * pixels, HID - EARLY), lambda t: (group(2 * steps)(t), 0)),
            pl.BlockSpec((G * pixels, C), lambda t: (jnp.clip(t - steps, 0, 2 * steps - 1) % steps, 0)), pix(3 * steps, C),
            pix(3 * steps, 128), img(3 * steps, 2 * nf, C), whole(gdw),
        ]
        + [whole(a) for a in consts],
        out_specs=[img(3 * steps, pixels, C)] + [any_space] * 6,
        out_shape=[
            sds((n_img, pixels, C), bf16), sds((n_img, 3 * across, C), bf16), sds((n_img, 3 * across, C), bf16),
        ]
        + results
        + [sds((SMALL, C), f32)],
        scratch_shapes=[
            pltpu.VMEM((n_img, max(pixels, 6 * across), C), bf16), pltpu.VMEM((NP, C), bf16), pltpu.VMEM((NP, C), f32), pltpu.VMEM((C // 128, G * h // 2, 2, across, 128), f32),
            pltpu.VMEM((2 * nf, C), f32), pltpu.VMEM((2 * nf, C), f32), pltpu.VMEM((C, HID), f32), pltpu.VMEM((C, HID), f32),
            pltpu.VMEM((1, HID), f32), pltpu.VMEM((SMALL, C), f32),
            pltpu.SemaphoreType.DMA((2, 2, steps)),
        ]
        + sums,
        compiler_params=pltpu.CompilerParams(vmem_limit_bytes=VMEM, collective_id=0, has_side_effects=True),
        name="backward",
    )(ext, keep, cot, sh, inv2, act, slope_early, slope_late, nm, fh, inv1, xhat, gdw, *consts)


def per_device(n_sp, n_dp, *arrays):
    (
        tokens, extents, keep_mask, cotangent, dw_kernel, dw_bias, norm_gain, norm_bias, expand_weight, expand_bias,
        project_weight, project_bias, layer_scale, down_gain, down_shift, down_weight, down_bias,
    ) = arrays
    n_img, h, across, C = tokens.shape
    CO, HID = cotangent.shape[-1], expand_weight.shape[1]
    pixels = h * across
    G, T = 1024 // pixels, 512 // pixels
    fused = n_sp == 4 and n_dp == 8 and n_img // G == 4
    if not fused:
        G = T
    nf, fwd, inv, fwd_own, inv_all, spectrum, back = tables(h, across)
    fwd, inv, fwd_own, inv_all = (jnp.asarray(a, bf16) for a in (fwd, inv, fwd_own, inv_all))
    taps, back = jnp.asarray(spectrum, f32), jnp.asarray(back, f32)
    z = lax.axis_index("sp")
    first = z * h
    ext = extents - jnp.stack([first, jnp.zeros_like(first)])[None, :]
    own = tokens.reshape(n_img, pixels, C)
    cot = cotangent.reshape(n_img, pixels // 4, CO)
    dw = down_weight.reshape(4 * C, CO)
    vec = jnp.zeros((16, C), f32)
    for k, v in (
        (DWB, dw_bias), (NG, norm_gain), (NB, norm_bias), (PB, project_bias), (LS, layer_scale), (DG, down_gain),
        (DS, down_shift), (DB, down_bias), (EB, expand_bias),
    ):
        rows = v.size // C
        vec = vec + jnp.pad(v.reshape(rows, C), ((k, 16 - rows - k), (0, 0)))
    out, act, slope_early, slope_late, xhat, fh, nm, inv1, sh, inv2, gdw = forward(
        bf16 if fused else f32, n_sp,
        G, T, h, across, nf, n_img, ext, keep_mask, own, cot, fwd, inv, taps, dw_kernel, vec, expand_weight, project_weight, dw,
    )
    grad, from_above, from_below, gdw_sum, gpw, gew, small = backward(
        fused, n_sp, G, T, h, across, nf, n_img, ext, keep_mask, cot, sh, inv2, act, slope_early,
        slope_late, nm, fh, inv1, xhat, gdw, dw, vec, project_weight, expand_weight, fwd_own, inv_all, taps, dw_kernel, back,
    )
    if fused:
        gdw, gpw, gew = (a.astype(f32) for a in (gdw_sum, gpw, gew))
    else:
        gdw, gpw, gew, small = lax.psum((gdw, gpw, gew, small), ("sp", "dp"))
        gpw = gpw.T
    from_above = jnp.where(z > 0, from_above, jnp.zeros_like(from_above)).reshape(n_img, 3, across, C)
    from_below = jnp.where(z < n_sp - 1, from_below, jnp.zeros_like(from_below)).reshape(n_img, 3, across, C)
    gap = ((0, 0), (0, h - 3), (0, 0), (0, 0))
    pog = ((0, 0), (h - 3, 0), (0, 0), (0, 0))
    grad = (
        grad.reshape(n_img, h, across, C).astype(f32)
        + jnp.pad(from_above, gap).astype(f32)
        + jnp.pad(from_below, pog).astype(f32)
    ).astype(bf16)
    gls = (jnp.sum(project_weight.astype(f32) * gpw, axis=0) + project_bias * small[V_PB]) / layer_scale
    gdk = small[:56].reshape(7, 8, C)[:, :7]
    geb = small[V_EB : V_EB + HID // C].reshape(HID)
    gdb = small[V_DB : V_DB + CO // C].reshape(CO)
    return (
        out.reshape(n_img, h // 2, across // 2, CO), grad, gdk, small[V_DWB], small[V_NG], small[V_NB], gew, geb, gpw,
        small[V_PB], gls, small[V_DG], small[V_DS], gdw.reshape(down_weight.shape), gdb,
    )


def solution(mesh):
    maps = P("dp", "sp", None, None)
    return jax.shard_map(
        functools.partial(per_device, mesh.shape["sp"], mesh.shape["dp"]),
        mesh=mesh,
        in_specs=(maps, P("dp", None), P("dp"), maps) + (P(),) * 13,
        out_specs=(maps, maps) + (P(),) * 13,
        check_vma=False,
    )
```

```python
import functools

import jax
import jax.numpy as jnp
import numpy as np
from jax import lax
from jax.experimental import pallas as pl
from jax.experimental.pallas import tpu as pltpu
from jax.sharding import PartitionSpec as P

bf16 = jnp.bfloat16
f32 = jnp.float32
epsilon = 1e-06
survival = 0.875
VMEM = 63 * 1024 * 1024
MESH = pl.DeviceIdType.MESH
DWB, NG, NB, PB, LS, DG, DS, DB, EB = 0, 1, 2, 3, 4, 5, 6, 7, 9
SMALL, V_DG, V_DS, V_PB, V_NG, V_NB, V_DWB, V_EB, V_DB = 128, 56, 57, 58, 59, 60, 61, 64, 72


def tables(h, across):
    nr, nc = h + 6, across + 3
    us, vs, ms = [], [], []
    for v in range(nc // 2 + 1):
        for u in range(nr):
            mu, mv = (-u) % nr, (-v) % nc
            if (mv, mu) < (v, u):
                continue
            us.append(u)
            vs.append(v)
            ms.append(1.0 if (mu, mv) == (u, v) else 2.0)
    n = len(us)
    nf = -(-n // 128) * 128
    us, vs, ms = (np.array(a + [0] * (nf - n), np.float64) for a in (us, vs, ms))
    live = (np.arange(nf) < n)[:, None]

    def angle(r, c):
        turns = (np.outer(us, r.ravel()) * nc + np.outer(vs, c.ravel()) * nr) % (nr * nc)
        return 2 * np.pi * turns / (nr * nc)

    def waves(a):
        return np.concatenate([np.cos(a) * live, -np.sin(a) * live])

    every = waves(angle(*np.meshgrid(np.arange(h + 6), np.arange(across), indexing="ij")))
    own = waves(angle(*np.meshgrid(np.arange(h), np.arange(across), indexing="ij")))
    ki, kj = np.meshgrid(np.arange(7), np.arange(8) - 3, indexing="ij")
    taps = angle(ki, kj)
    weight = (ms / (nr * nc))[:, None] * (kj.ravel() < 4)[None, :]
    spectrum = np.concatenate([np.cos(taps) * weight, np.sin(taps) * weight])
    back = np.concatenate([np.cos(taps) * weight, -np.sin(taps) * weight]).T
    return nf, every, own.T, own, every.T, spectrum, back


def dot(a, b):
    return jnp.dot(a, b, preferred_element_type=f32)


def dot_nt(a, b):
    return lax.dot_general(a, b, (((1,), (1,)), ((), ())), preferred_element_type=f32)


def dot_tn(a, b):
    return lax.dot_general(a, b, (((0,), (0,)), ((), ())), preferred_element_type=f32)


def dot_exact(a, b):
    return jnp.dot(a, b, preferred_element_type=f32, precision=lax.Precision.HIGHEST)


def mean(x):
    return jnp.sum(x, axis=-1, keepdims=True) * (1.0 / x.shape[-1])


def total(x):
    return jnp.sum(x, axis=0, keepdims=True)


def lanes(x, width):
    return jnp.concatenate([x] * (width // x.shape[1]), axis=1)


def stack(parts, axis):
    return parts[0] if len(parts) == 1 else jnp.concatenate(parts, axis=axis)


def gelu_parts(v):
    u = v * v
    p = 0.7978667366454887 + u * (
        0.03640226973029483
        + u * (-9.53235048862514e-05 + u * (-3.491248211005391e-05 + u * 1.3019431827058075e-06))
    )
    phi = 0.5 + 0.5 * jnp.tanh(v * p)
    density = jnp.exp2(u * -0.7213475204444817 - 1.3257480647361595)
    return v * phi, phi + v * density


class Masks:
    def __init__(self, h, across):
        n = lax.broadcasted_iota(jnp.int32, ((h + 6) * across, 128), 0)
        self.row, self.col = (n >> (across.bit_length() - 1)) - 3, n & (across - 1)
        self.own_rows = slice(3 * across, (3 + h) * across)
        q = lax.broadcasted_iota(jnp.int32, (h * across // 4, 128), 0)
        half = across // 2
        self.coarse_row, self.coarse_col = 2 * (q >> (half.bit_length() - 1)), 2 * (q & (half - 1))

    def every(self, rows, cols):
        return ((self.row < rows) & (self.col < cols)).astype(f32)

    def own(self, rows, cols):
        r, c = self.row[self.own_rows], self.col[self.own_rows]
        return ((r < rows) & (c < cols)).astype(f32)

    def coarse(self, rows, cols):
        return ((self.coarse_row < rows) & (self.coarse_col < cols)).astype(f32)


def remote(src, dst, send, recv, where):
    return pltpu.make_async_remote_copy(
        src_ref=src, dst_ref=dst, send_sem=send, recv_sem=recv, device_id=where, device_id_type=MESH
    )


def greet(peers):
    barrier = pltpu.get_barrier_semaphore()
    for where in peers:
        pl.semaphore_signal(barrier, inc=1, device_id=where, device_id_type=MESH)
    pl.semaphore_wait(barrier, len(peers))


def stack_vectors(vec, refs):
    C, k = vec.shape[1], 0
    for ref in refs:
        for first in range(0, ref.shape[0], C):
            vec[k : k + 1, :] = ref[first : first + C].reshape(1, C)
            k += 1


def tap_rows(dwk):
    gap = jnp.zeros((1, dwk.shape[-1]), f32)
    return jnp.concatenate([x for i in range(7) for x in (dwk[i], gap)], axis=0)


def forward_kernel(
    G, T, h, across, nf, zs, steps,
    ext, keep, tok, own, cot, fwd, inv, taps, dwk, v0, v1, v2, v3, v4, v5, v6, v7, v8, ew, pw, dw,
    out, act, slope, xhat, fh_out, nm, inv1_out, sh_out, inv2_out, gdw,
    top, bot, spec, vec, red, gdw_s, sem,
):
    g = pl.program_id(0)
    pixels = h * across
    edge = 3 * across
    C = own.shape[-1]
    z, dp = lax.axis_index("sp"), lax.axis_index("dp")
    above, below = {"sp": z - 1, "dp": dp}, {"sp": z + 1, "dp": dp}

    def halo(k, up):
        part = pl.ds(k * T, T)
        if up:
            return remote(tok.at[part, pl.ds(0, edge)], bot.at[part], sem.at[0, 0, k], sem.at[1, 0, k], above)
        return remote(tok.at[part, pl.ds(pixels - edge, edge)], top.at[part], sem.at[0, 1, k], sem.at[1, 1, k], below)

    def each(k, up_act, down_act):
        if up_act is not None:
            pl.when(z > 0)(lambda: up_act(halo(k, True)))
        if down_act is not None:
            pl.when(z < zs - 1)(lambda: down_act(halo(k, False)))

    parts = steps * G // T

    def arrive(part):
        pl.when(z < zs - 1)(lambda: halo(part, True).wait_recv())
        pl.when(z > 0)(lambda: halo(part, False).wait_recv())

    @pl.when(g == 0)
    def _():
        greet([{"sp": (z + 1) % zs, "dp": dp}, {"sp": (z + zs - 1) % zs, "dp": dp}])
        for k in range(parts):
            each(k, lambda c: c.start(), lambda c: c.start())

        @pl.when(z == 0)
        def _():
            top[...] = jnp.zeros_like(top)

        @pl.when(z == zs - 1)
        def _():
            bot[...] = jnp.zeros_like(bot)

        gdw_s[...] = jnp.zeros_like(gdw_s)
        spec[...] = dot_exact(taps[...], tap_rows(dwk))
        stack_vectors(vec, (v0, v1, v2, v3, v4, v5, v6, v7, v8))

    for k in range(1, steps):

        @pl.when(g == k)
        def _():
            for part in range(k * (G // T), (k + 1) * (G // T)):
                arrive(part)

    masks = Masks(h, across)
    kr, ki = lanes(spec[:nf], T * C), lanes(spec[nf:], T * C)
    eb = jnp.concatenate([vec[EB + k : EB + k + 1, :] for k in range(ew.shape[1] // C)], axis=1)
    db = jnp.concatenate([vec[DB + k : DB + k + 1, :] for k in range(cot.shape[-1] // C)], axis=1)
    HC = 512
    for team in range(G // T):
        pl.when(g == 0)(functools.partial(arrive, team))
        xs, fields, valids, facs = [], [], [], []
        for t in range(T):
            b = team * T + t
            rows, cols = ext[g * G + b, 0], ext[g * G + b, 1]
            x = jnp.concatenate([top[g * G + b], own[b], bot[g * G + b]], axis=0)
            every = masks.every(rows, cols)
            x = x * lanes(every.astype(bf16), C)
            xs.append(x)
            fields.append(x[masks.own_rows])
            valids.append(every[masks.own_rows])
            facs.append(valids[-1] * (keep[g * G + b].astype(f32) * (1.0 / survival)))
        hat = dot(fwd[...], stack(xs, 1))
        xr, xi = hat[:nf], hat[nf:]
        for t in range(T):
            xhat[team * T + t] = hat[:, t * C : (t + 1) * C].astype(bf16)
        product = jnp.concatenate(
            [(xr * kr - xi * ki).astype(bf16), (xr * ki + xi * kr).astype(bf16)], axis=0
        )
        mixed = dot(inv[...], product)
        mixed = stack([mixed[:, t * C : (t + 1) * C] for t in range(T)], 0) + vec[DWB : DWB + 1, :]
        here = pl.ds(team * T * pixels, T * pixels)
        d = mixed - mean(mixed)
        inv1 = lax.rsqrt(mean(d * d) + epsilon)
        fh = d * inv1
        fh_out[here, :] = fh.astype(bf16)
        inv1_out[here, :] = jnp.broadcast_to(inv1, (T * pixels, 128))
        normed = (fh * vec[NG : NG + 1, :] + vec[NB : NB + 1, :]).astype(bf16)
        nm[here, :] = normed
        branch = vec[PB : PB + 1, :]
        for k in range(ew.shape[1] // HC):
            part = slice(k * HC, (k + 1) * HC)
            a, s = gelu_parts(dot(normed, ew[:, part]) + eb[:, part])
            a = a.astype(bf16)
            act[here, part] = a
            slope[here, part] = s.astype(bf16)
            branch = branch + dot(a, pw[part, :])
        valid, fac = stack(valids, 0), stack(facs, 0)
        res = stack(fields, 0).astype(f32) + lanes(fac, C) * (branch * vec[LS : LS + 1, :])
        d = res - mean(res)
        inv2 = lax.rsqrt(mean(d * d) + epsilon)
        sh = d * inv2
        sh_out[here, :] = sh.astype(bf16)
        inv2_out[here, :] = jnp.broadcast_to(inv2, (T * pixels, 128))
        reduced = (sh * vec[DG : DG + 1, :] + vec[DS : DS + 1, :]) * lanes(valid, C)
        rows_here = T * h // 2
        for k in range(C // 128):
            slab = reduced[:, k * 128 : (k + 1) * 128].reshape(rows_here, 2, across, 128)
            red[k, team * rows_here : (team + 1) * rows_here] = slab
    patch = jnp.concatenate(
        [
            red[k, :, p, pl.ds(q, across // 2, stride=2), :].reshape(G * pixels // 4, 128).astype(bf16)
            for p in range(2)
            for q in range(2)
            for k in range(C // 128)
        ],
        axis=1,
    )
    coarse = stack([masks.coarse(ext[g * G + b, 0], ext[g * G + b, 1]) for b in range(G)], 0)
    coarse = lanes(coarse, cot.shape[-1])
    up = cot[...].reshape(coarse.shape) * coarse.astype(bf16)
    out[...] = ((dot(patch, dw[...]) + db) * coarse).astype(bf16).reshape(out.shape)
    gdw_s[...] += dot_tn(patch, up)

    @pl.when(g == steps - 1)
    def _():
        gdw[...] = gdw_s[...].astype(gdw.dtype)
        for k in range(parts):
            each(k, lambda c: c.wait_send(), lambda c: c.wait_send())


def whole(a):
    return pl.BlockSpec(a.shape, lambda t: (0,) * a.ndim, pipeline_mode=pl.Buffered(1))


def forward(sum_type, zs, G, T, h, across, nf, n_img, ext, keep, own, cot, *consts):
    pixels, C, CO = h * across, own.shape[-1], cot.shape[-1]
    HID = consts[-3].shape[1]
    Q, NP, steps = pixels // 4, n_img * pixels, n_img // G

    def img(*s):
        return pl.BlockSpec((G,) + s, lambda g: (g,) + (0,) * len(s))

    def pix(c):
        return pl.BlockSpec((G * pixels, c), lambda g: (g, 0))

    smem = pl.BlockSpec(memory_space=pltpu.SMEM)
    sds = jax.ShapeDtypeStruct
    return pl.pallas_call(
        functools.partial(forward_kernel, G, T, h, across, nf, zs, steps),
        grid=(steps,),
        in_specs=[smem, smem, pl.BlockSpec(memory_space=pl.ANY), img(pixels, C), img(Q, CO)] + [whole(a) for a in consts],
        out_specs=[
            img(Q, CO), pix(HID), pix(HID), img(2 * nf, C), pix(C), pix(C), pix(128), pix(C), pix(128),
            pl.BlockSpec((4 * C, CO), lambda g: (0, 0)),
        ],
        out_shape=[
            sds((n_img, Q, CO), bf16), sds((NP, HID), bf16), sds((NP, HID), bf16), sds((n_img, 2 * nf, C), bf16),
            sds((NP, C), bf16), sds((NP, C), bf16), sds((NP, 128), f32), sds((NP, C), bf16), sds((NP, 128), f32),
            sds((4 * C, CO), sum_type),
        ],
        scratch_shapes=[
            pltpu.VMEM((n_img, 3 * across, C), bf16), pltpu.VMEM((n_img, 3 * across, C), bf16),
            pltpu.VMEM((2 * nf, C), f32), pltpu.VMEM((16, C), f32), pltpu.VMEM((C // 128, G * h // 2, 2, across, 128), f32),
            pltpu.VMEM((4 * C, CO), f32),
            pltpu.SemaphoreType.DMA((2, 2, n_img // T)),
        ],
        compiler_params=pltpu.CompilerParams(vmem_limit_bytes=VMEM, collective_id=1, has_side_effects=True),
        name="forward",
    )(ext, keep, own, own, cot, *consts)


class Place:
    def __init__(self, zs):
        self.z, self.dp = lax.axis_index("sp"), lax.axis_index("dp")
        self.core, self.chip = self.dp % 2, self.dp // 2
        self.pair = self.at(self.z, self.dp + 1 - 2 * self.core)
        self.above, self.below = self.at(self.z - 1, self.dp), self.at(self.z + 1, self.dp)
        self.plane, self.column, self.others = [], [], []
        for d in range(1, 4):
            j = (self.chip + d) % 4
            self.plane.append((j, self.at(self.z, j * 2 + self.core)))
        for d in range(1, zs):
            j = (self.z + d) % zs
            self.column.append((j, self.at(j, self.dp)))
        self.me = self.z * 4 + self.chip
        for d in range(1, 4 * zs):
            j = (self.me + d) % (4 * zs)
            self.others.append((j, self.at(j // 4, (j % 4) * 2 + self.core)))

    def at(self, z, dp):
        return {"sp": z, "dp": dp}


class Sum:
    def __init__(self, place, zs, full, half, plane_in, z_in, send, recv, out, by_cols=False):
        self.place, self.full, self.half, self.plane_in, self.z_in = place, full, half, plane_in, z_in
        self.send, self.recv, self.out, self.by_cols = send, recv, out, by_cols
        p = place
        self.R, self.cols = half.shape
        self.rows = self.R // 4
        self.base = pl.multiple_of(p.core * self.R, self.R)
        self.other = pl.multiple_of((1 - p.core) * self.R, self.R)
        self.mine = pl.multiple_of(p.chip * self.rows, self.rows)
        self.z_rows = self.rows if by_cols else self.rows // zs
        self.z_cols = self.cols // zs if by_cols else self.cols

    def z_at(self, j, base):
        if self.by_cols:
            return (pl.ds(base, self.z_rows), pl.ds(pl.multiple_of(j * self.z_cols, self.z_cols), self.z_cols))
        return (pl.ds(pl.multiple_of(base + j * self.z_rows, self.z_rows), self.z_rows), slice(None))

    def copies(self, stage):
        p, n = self.place, len(self.place.column)
        slot = (0, 1, 4, 4 + n, 4 + 2 * n, 7 + 2 * n)[stage]

        def copy(src, dst, where, d=0):
            return remote(src, dst, self.send.at[slot + d], self.recv.at[slot + d], where)

        if stage == 0:
            return [copy(self.full.at[pl.ds(self.other, self.R)], self.half, p.pair)]
        if stage == 1:
            return [
                copy(
                    self.half.at[pl.ds(pl.multiple_of(j * self.rows, self.rows), self.rows)],
                    self.plane_in.at[d],
                    where,
                    d,
                )
                for d, (j, where) in enumerate(p.plane)
            ]
        if stage == 2:
            return [
                copy(self.half.at[self.z_at(j, self.mine)], self.z_in.at[d], where, d)
                for d, (j, where) in enumerate(p.column)
            ]
        if stage == 3:
            src, dst = self.own()
            return [copy(src, dst, where, d) for d, (_, where) in enumerate(p.column)]
        if stage == 4:
            there = self.out.at[pl.ds(pl.multiple_of(self.base + self.mine, self.rows), self.rows)]
            return [copy(there, there, where, d) for d, (_, where) in enumerate(p.plane)]
        there = self.out.at[pl.ds(self.base, self.R)]
        return [copy(there, there, p.pair)]

    def own(self):
        p = self.place
        return self.half.at[self.z_at(p.z, self.mine)], self.out.at[self.z_at(p.z, self.base + self.mine)]

    def own_copy(self):
        src, dst = self.own()
        return pltpu.make_async_copy(src, dst, self.send.at[self.send.shape[0] - 1])

    def add(self, at, parts):
        value = self.half[at].astype(f32)
        for part in parts:
            value = value + part.astype(f32)
        self.half[at] = value.astype(self.half.dtype)

    def step(self, stage):
        if stage > 0:
            for c in self.copies(stage - 1):
                c.wait_recv()
        if stage == 1:
            self.add((slice(None), slice(None)), [self.full[pl.ds(self.base, self.R), :]])
        if stage == 2:
            self.add((pl.ds(self.mine, self.rows), slice(None)), [self.plane_in[d] for d in range(3)])
        if stage == 3:
            n = len(self.place.column)
            self.add(self.z_at(self.place.z, self.mine), [self.z_in[d] for d in range(n)])
            self.own_copy().start()
        if stage == 4:
            self.own_copy().wait()
        if stage < 6:
            for c in self.copies(stage):
                c.start()
        else:
            for k in range(6):
                for c in self.copies(k):
                    c.wait_send()


class SmallSum:
    def __init__(self, place, zs, full, pair_in, rows_in, send, recv, out):
        self.place, self.full, self.pair_in, self.rows_in = place, full, pair_in, rows_in
        self.send, self.recv, self.out = send, recv, out
        p = place
        n = self.n = 4 * zs
        self.rows = full.shape[0] // n
        self.me, self.others = p.me, p.others

    def part(self, j):
        return pl.ds(pl.multiple_of(j * self.rows, self.rows), self.rows)

    def copies(self, stage):
        n = self.n
        if stage == 0:
            return [remote(self.full, self.pair_in, self.send.at[0], self.recv.at[0], self.place.pair)]
        out = []
        for d, (j, where) in enumerate(self.others):
            slot = (stage - 1) * (n - 1) + 1 + d
            if stage == 1:
                src, dst = self.full.at[self.part(j)], self.rows_in.at[d]
            else:
                src, dst = self.full.at[self.part(self.me)], self.out.at[self.part(self.me)]
            out.append(remote(src, dst, self.send.at[slot], self.recv.at[slot], where))
        return out

    def own_copy(self):
        return pltpu.make_async_copy(
            self.full.at[self.part(self.me)], self.out.at[self.part(self.me)], self.send.at[self.send.shape[0] - 1]
        )

    def step(self, stage):
        if stage > 0:
            for c in self.copies(stage - 1):
                c.wait_recv()
        if stage == 1:
            for c in self.copies(0):
                c.wait_send()
            self.full[...] += self.pair_in[...]
        if stage == 2:
            value = self.full[self.part(self.me), :]
            for d in range(self.n - 1):
                value = value + self.rows_in[d]
            self.full[self.part(self.me), :] = value
            self.own_copy().start()
        if stage < 3:
            for c in self.copies(stage):
                c.start()
        else:
            self.own_copy().wait()
            for k in (1, 2):
                for c in self.copies(k):
                    c.wait_send()


def backward_kernel(
    G, T, h, across, nf, steps, zs, stages,
    ext, keep, cot, sh_in, inv2, act, slope, nm, fh_in, inv1, xhat, gdw_own,
    dw, v0, v1, v2, v3, v4, v5, v6, v7, v8, pw, ew, fwd_own, inv_all, taps, dwk, back,
    own_out, top_in, bot_in, gdw_out, gpw_out, gew_out, small_out,
    held, gres_s, gn_s, gr_s, acc, spec, vec, gpw, gew, geb, small, halo_sem, *sums,
):
    step = pl.program_id(0)
    pixels = h * across
    C, HID = sh_in.shape[-1], act.shape[-1]
    HC = 512
    masks = Masks(h, across)
    place = Place(zs)
    reduced = {}
    if stages is not None:
        wide = gdw_own.shape[1] // 2
        for k, name in enumerate(("down0", "down1", "project", "expand")):
            buffers, out = list(sums[6 * k : 6 * k + 6]), {2: gpw_out, 3: gew_out}.get(k)
            if k < 2:
                columns = pl.ds(k * wide, wide)
                buffers[0], out = gdw_own.at[:, columns], gdw_out.at[:, columns]
            reduced[name] = Sum(place, zs, *buffers, out, by_cols=name == "expand")
        reduced["small"] = SmallSum(place, zs, small, *sums[24:28], small_out)

    peers = [place.pair] + [w for _, w in place.others] if stages is not None else [w for _, w in place.column]

    @pl.when(step == 0)
    def _():
        barrier = pltpu.get_barrier_semaphore()
        for where in peers:
            pl.semaphore_signal(barrier, inc=1, device_id=where, device_id_type=MESH)
        for ref in (gpw, gew, geb, small, acc):
            ref[...] = jnp.zeros_like(ref)
        spec[...] = dot_exact(taps[...], tap_rows(dwk))
        stack_vectors(vec, (v0, v1, v2, v3, v4, v5, v6, v7, v8))

    @pl.when(step == 1)
    def _():
        pl.semaphore_wait(pltpu.get_barrier_semaphore(), len(peers))

    def run(at):
        for name, stage in stages.get(at, ()):
            if stage == 0 and name == "project":
                reduced[name].full[...] = gpw[...].T.astype(bf16)
            if stage == 0 and name == "expand":
                reduced[name].full[...] = gew[...].astype(bf16)
            reduced[name].step(stage)

    if stages is not None:
        for at in range(3 * steps):
            if at in stages:
                pl.when(step == at)(functools.partial(run, at))

    def row(k):
        return vec[k : k + 1, :]

    def extent(b, g):
        return ext[g * G + b, 0], ext[g * G + b, 1]

    @pl.when(step < steps)
    def _():
        g = step
        coarse = lanes(stack([masks.coarse(*extent(b, g)) for b in range(G)], 0).astype(bf16), cot.shape[-1])
        up = cot[...].reshape(coarse.shape) * coarse
        gdb = total(up.astype(f32))
        for k in range(cot.shape[-1] // C):
            small[V_DB + k : V_DB + k + 1, :] += gdb[:, k * C : (k + 1) * C]
        for p in range(2):
            for q in range(2):
                k = 2 * p + q
                slab = dot_nt(up, dw[k * C : (k + 1) * C, :])
                for n in range(C // 128):
                    gr_s[n, :, p, pl.ds(q, across // 2, stride=2), :] = slab[:, n * 128 : (n + 1) * 128].reshape(
                        G * h // 2, across // 2, 128
                    )
        for team in range(G // T):
            here = pl.ds(team * T * pixels, T * pixels)
            valids = [masks.own(*extent(team * T + t, g)) for t in range(T)]
            facs = [
                valids[t] * (keep[g * G + team * T + t].astype(f32) * (1.0 / survival)) for t in range(T)
            ]
            rows = T * h // 2
            gr = stack(
                [gr_s[n, team * rows : (team + 1) * rows].reshape(T * pixels, 128) for n in range(C // 128)], 1
            )
            gr = gr * lanes(stack(valids, 0), C)
            sh = sh_in[here, :].astype(f32)
            small[V_DG : V_DG + 1, :] += total(gr * sh)
            small[V_DS : V_DS + 1, :] += total(gr)
            u = gr * row(DG)
            gres = lanes(inv2[here, :], C) * (u - mean(u) - sh * mean(u * sh))
            first = pl.multiple_of(g * (G * pixels) + team * T * pixels, T * pixels)
            gres_s[pl.ds(first, T * pixels), :] = gres.astype(bf16)
            gb = (gres * lanes(stack(facs, 0), C) * row(LS)).astype(bf16)
            for t in range(T):
                held[g * G + team * T + t, :pixels] = gb[t * pixels : (t + 1) * pixels]
            small[V_PB : V_PB + 1, :] += total(gb.astype(f32))
            gpw[...] += dot_tn(gb, act[here, :])

    @pl.when((step >= steps) & (step < 2 * steps))
    def _():
        g = step - steps
        for team in range(G // T):
            here = pl.ds(team * T * pixels, T * pixels)
            gb = stack([held[g * G + team * T + t, :pixels] for t in range(T)], 0)
            gn = None
            for k in range(HID // HC):
                part = slice(k * HC, (k + 1) * HC)
                gh = (dot_nt(gb, pw[part, :]) * slope[here, part].astype(f32)).astype(bf16)
                geb[:, part] += total(gh.astype(f32))
                gew[:, part] += dot_tn(nm[here, :], gh)
                term = dot_nt(gh, ew[:, part])
                gn = term if gn is None else gn + term
            gn_s[pl.ds(pl.multiple_of(g * (G * pixels) + team * T * pixels, T * pixels), T * pixels), :] = gn

    def halo(target, g, side, where):
        part, edge = pl.ds(pl.multiple_of(g * G, G), G), 3 * across
        src = held.at[part, pl.ds(side * edge, edge)]
        return remote(src, target.at[part], halo_sem.at[0, side, g], halo_sem.at[1, side, g], where)

    def up(g):
        return halo(bot_in, g, 0, place.above)

    def down(g):
        return halo(top_in, g, 1, place.below)

    @pl.when(step >= 2 * steps)
    def _():
        g = step - 2 * steps
        edge = 3 * across
        kr, ki = lanes(spec[:nf], T * C), lanes(spec[nf:], T * C)
        for team in range(G // T):
            here = pl.ds(team * T * pixels, T * pixels)
            first = pl.multiple_of(g * (G * pixels) + team * T * pixels, T * pixels)
            gn = gn_s[pl.ds(first, T * pixels), :]
            fh = fh_in[here, :].astype(f32)
            small[V_NG : V_NG + 1, :] += total(gn * fh)
            small[V_NB : V_NB + 1, :] += total(gn)
            w = gn * row(NG)
            gm = lanes(inv1[here, :], C) * (w - mean(w) - fh * mean(w * fh))
            small[V_DWB : V_DWB + 1, :] += total(gm)
            gm = gm.astype(bf16)
            gm = stack([gm[t * pixels : (t + 1) * pixels] for t in range(T)], 1)
            hat = dot(fwd_own[...], gm)
            gr, gi = hat[:nf], hat[nf:]
            sr, si = acc[:nf], acc[nf:]
            for t in range(T):
                at = slice(t * C, (t + 1) * C)
                xr, xi = xhat[team * T + t, :nf].astype(f32), xhat[team * T + t, nf:].astype(f32)
                sr = sr + gr[:, at] * xr + gi[:, at] * xi
                si = si + gr[:, at] * xi - gi[:, at] * xr
            acc[:nf] = sr
            acc[nf:] = si
            product = jnp.concatenate(
                [(gr * kr + gi * ki).astype(bf16), (gi * kr - gr * ki).astype(bf16)], axis=0
            )
            o = dot(inv_all[...], product)
            for t in range(T):
                b = g * G + team * T + t
                each = o[:, t * C : (t + 1) * C] * lanes(masks.every(ext[b, 0], ext[b, 1]), C)
                held[b, :edge] = each[:edge].astype(bf16)
                own = gres_s[pl.ds(pl.multiple_of(b * pixels, pixels), pixels), :].astype(f32)
                own_out[team * T + t] = (each[edge : edge + pixels] + own).astype(bf16)
                held[b, edge : 2 * edge] = each[edge + pixels :].astype(bf16)
        pl.when(place.z > 0)(lambda: up(g).start())
        pl.when(place.z < zs - 1)(lambda: down(g).start())

    @pl.when(step == 3 * steps - 1)
    def _():
        small[0:56, :] = dot_exact(back[...], acc[...])
        for k in range(HID // C):
            small[V_EB + k : V_EB + k + 1, :] = geb[:, k * C : (k + 1) * C]
        if stages is not None:
            run(3 * steps)
        else:
            for k, (src, dst) in enumerate(((gpw, gpw_out), (gew, gew_out), (small, small_out))):
                c = pltpu.make_async_copy(src, dst, sums[0].at[k])
                c.start()
                c.wait()

        @pl.when(place.z > 0)
        def _():
            for g in range(steps):
                up(g).wait_send()
                down(g).wait_recv()

        @pl.when(place.z < zs - 1)
        def _():
            for g in range(steps):
                down(g).wait_send()
                up(g).wait_recv()


def schedule():
    return {
        1: [("down0", 0)],
        2: [("down0", 1), ("down1", 0)],
        3: [("down1", 1)],
        4: [("project", 0)],
        5: [("down0", 2), ("project", 1)],
        6: [("down0", 3), ("down1", 2)],
        7: [("down1", 3), ("project", 2)],
        8: [("project", 3), ("expand", 0)],
        9: [("expand", 1)],
        10: [("down1", 4), ("expand", 2)],
        11: [("down0", 4), ("project", 4), ("expand", 3)],
        12: [
            ("small", 0), ("down1", 5), ("small", 1), ("down0", 5), ("project", 5), ("expand", 4), ("small", 2), ("expand", 5),
            ("down0", 6), ("down1", 6), ("project", 6), ("small", 3), ("expand", 6),
        ],
    }


def backward(fused, zs, G, T, h, across, nf, n_img, ext, keep, cot, sh, inv2, act, slope, nm, fh, inv1, xhat, gdw, *consts):
    pixels, C, CO = h * across, sh.shape[-1], cot.shape[-1]
    HID = act.shape[1]
    Q, NP, steps = pixels // 4, n_img * pixels, n_img // G

    def group(first):
        return lambda t: jnp.clip(t - first, 0, steps - 1)

    def img(first, *s):
        return pl.BlockSpec((G,) + s, lambda t: (group(first)(t),) + (0,) * len(s))

    def pix(first, c):
        return pl.BlockSpec((G * pixels, c), lambda t: (group(first)(t), 0))

    any_space = pl.BlockSpec(memory_space=pl.ANY)
    smem = pl.BlockSpec(memory_space=pltpu.SMEM)
    sds = jax.ShapeDtypeStruct

    def sum_buffers(rows, cols, by_cols, dtype, full):
        half = rows // 2
        z = (half // 4, cols // zs) if by_cols else (half // 4 // zs, cols)
        n = 8 + 2 * (zs - 1)
        return [
            pltpu.VMEM((rows, cols) if full else (16, 128), dtype),
            pltpu.VMEM((half, cols), dtype),
            pltpu.VMEM((3, half // 4, cols), dtype),
            pltpu.VMEM((zs - 1,) + z, dtype),
            pltpu.SemaphoreType.DMA((n + 1,)),
            pltpu.SemaphoreType.DMA((n,)),
        ]

    if fused:
        sums = sum_buffers(4 * C, CO // 2, False, bf16, False) * 2
        sums += sum_buffers(HID, C, False, bf16, True)
        sums += sum_buffers(C, HID, True, bf16, True)
        n = 4 * zs
        sums += [
            pltpu.VMEM((SMALL, C), f32),
            pltpu.VMEM((n - 1, SMALL // n, C), f32),
            pltpu.SemaphoreType.DMA((2 * n,)),
            pltpu.SemaphoreType.DMA((2 * n - 1,)),
        ]
        results = [sds((4 * C, CO), bf16), sds((HID, C), bf16), sds((C, HID), bf16)]
    else:
        sums = [pltpu.SemaphoreType.DMA((3,))]
        results = [sds((16, 128), bf16), sds((C, HID), f32), sds((C, HID), f32)]
        gdw = gdw[:16, :128]
    return pl.pallas_call(
        functools.partial(backward_kernel, G, T, h, across, nf, steps, zs, schedule() if fused else None),
        grid=(3 * steps,),
        in_specs=[
            smem, smem, img(0, Q, CO), pix(0, C), pix(0, 128), pix(0, HID), pix(steps, HID), pix(steps, C), pix(2 * steps, C),
            pix(2 * steps, 128), img(2 * steps, 2 * nf, C), whole(gdw),
        ]
        + [whole(a) for a in consts],
        out_specs=[img(2 * steps, pixels, C)] + [any_space] * 6,
        out_shape=[
            sds((n_img, pixels, C), bf16), sds((n_img, 3 * across, C), bf16), sds((n_img, 3 * across, C), bf16),
        ]
        + results
        + [sds((SMALL, C), f32)],
        scratch_shapes=[
            pltpu.VMEM((n_img, max(pixels, 6 * across), C), bf16), pltpu.VMEM((NP, C), bf16), pltpu.VMEM((NP, C), f32), pltpu.VMEM((C // 128, G * h // 2, 2, across, 128), f32),
            pltpu.VMEM((2 * nf, C), f32), pltpu.VMEM((2 * nf, C), f32), pltpu.VMEM((16, C), f32), pltpu.VMEM((C, HID), f32), pltpu.VMEM((C, HID), f32),
            pltpu.VMEM((1, HID), f32), pltpu.VMEM((SMALL, C), f32),
            pltpu.SemaphoreType.DMA((2, 2, steps)),
        ]
        + sums,
        compiler_params=pltpu.CompilerParams(vmem_limit_bytes=VMEM, collective_id=0, has_side_effects=True),
        name="backward",
    )(ext, keep, cot, sh, inv2, act, slope, nm, fh, inv1, xhat, gdw, *consts)


def per_device(n_sp, n_dp, *arrays):
    (
        tokens, extents, keep_mask, cotangent, dw_kernel, dw_bias, norm_gain, norm_bias, expand_weight, expand_bias,
        project_weight, project_bias, layer_scale, down_gain, down_shift, down_weight, down_bias,
    ) = arrays
    n_img, h, across, C = tokens.shape
    CO, HID = cotangent.shape[-1], expand_weight.shape[1]
    pixels = h * across
    G, T = 1024 // pixels, 512 // pixels
    fused = n_sp == 4 and n_dp == 8 and n_img // G == 4
    if not fused:
        G = T
    nf, fwd, inv, fwd_own, inv_all, spectrum, back = tables(h, across)
    fwd, inv, fwd_own, inv_all = (jnp.asarray(a, bf16) for a in (fwd, inv, fwd_own, inv_all))
    taps, back = jnp.asarray(spectrum, f32), jnp.asarray(back, f32)
    z = lax.axis_index("sp")
    first = z * h
    ext = extents - jnp.stack([first, jnp.zeros_like(first)])[None, :]
    own = tokens.reshape(n_img, pixels, C)
    cot = cotangent.reshape(n_img, pixels // 4, CO)
    dw = down_weight.reshape(4 * C, CO)
    vectors = (
        dw_bias, norm_gain, norm_bias, project_bias, layer_scale, down_gain, down_shift, down_bias, expand_bias
    )
    out, act, slope, xhat, fh, nm, inv1, sh, inv2, gdw = forward(
        bf16 if fused else f32, n_sp,
        G, T, h, across, nf, n_img, ext, keep_mask, own, cot, fwd, inv, taps, dw_kernel, *vectors, expand_weight, project_weight, dw,
    )
    grad, from_above, from_below, gdw_sum, gpw, gew, small = backward(
        fused, n_sp, G, T, h, across, nf, n_img, ext, keep_mask, cot, sh, inv2, act, slope,
        nm, fh, inv1, xhat, gdw, dw, *vectors, project_weight, expand_weight, fwd_own, inv_all, taps, dw_kernel, back,
    )
    if fused:
        gdw, gpw, gew = (a.astype(f32) for a in (gdw_sum, gpw, gew))
    else:
        gdw, gpw, gew, small = lax.psum((gdw, gpw, gew, small), ("sp", "dp"))
        gpw = gpw.T
    from_above = jnp.where(z > 0, from_above, jnp.zeros_like(from_above))
    from_below = jnp.where(z < n_sp - 1, from_below, jnp.zeros_like(from_below))
    gap = ((0, 0), (0, h - 3), (0, 0), (0, 0))
    pog = ((0, 0), (h - 3, 0), (0, 0), (0, 0))
    grad = (
        grad.reshape(n_img, h, across, C).astype(f32)
        + jnp.pad(from_above.reshape(n_img, 3, across, C), gap).astype(f32)
        + jnp.pad(from_below.reshape(n_img, 3, across, C), pog).astype(f32)
    ).astype(bf16)
    gls = (jnp.sum(project_weight.astype(f32) * gpw, axis=0) + project_bias * small[V_PB]) / layer_scale
    gdk = small[:56].reshape(7, 8, C)[:, :7]
    geb = small[V_EB : V_EB + HID // C].reshape(HID)
    gdb = small[V_DB : V_DB + CO // C].reshape(CO)
    return (
        out.reshape(n_img, h // 2, across // 2, CO), grad, gdk, small[V_DWB], small[V_NG], small[V_NB], gew, geb, gpw,
        small[V_PB], gls, small[V_DG], small[V_DS], gdw.reshape(down_weight.shape), gdb,
    )


def solution(mesh):
    maps = P("dp", "sp", None, None)
    return jax.shard_map(
        functools.partial(per_device, mesh.shape["sp"], mesh.shape["dp"]),
        mesh=mesh,
        in_specs=(maps, P("dp", None), P("dp"), maps) + (P(),) * 13,
        out_specs=(maps, maps) + (P(),) * 13,
        check_vma=False,
    )
```

```python
import functools

import jax
import jax.numpy as jnp
import numpy as np
from jax import lax
from jax.experimental import pallas as pl
from jax.experimental.pallas import tpu as pltpu
from jax.sharding import PartitionSpec as P

bf16 = jnp.bfloat16
f32 = jnp.float32
epsilon = 1e-06
survival = 0.875
VMEM = 63 * 1024 * 1024
MESH = pl.DeviceIdType.MESH
DWB, NG, NB, PB, LS, DG, DS, DB, EB = 0, 1, 2, 3, 4, 5, 6, 7, 9
V_DG, V_DS, V_PB, V_NG, V_NB, V_DWB, V_DB = 0, 1, 2, 3, 4, 5, 6
SMALL, S_VEC, S_EB = (64, 512), 0, 24


def tables(h, across):
    nr, nc = h + 6, across + 3
    us, vs, ms = [], [], []
    for v in range(nc // 2 + 1):
        for u in range(nr):
            mu, mv = (-u) % nr, (-v) % nc
            if (mv, mu) < (v, u):
                continue
            us.append(u)
            vs.append(v)
            ms.append(1.0 if (mu, mv) == (u, v) else 2.0)
    n = len(us)
    nf = -(-n // 128) * 128
    us, vs, ms = (np.array(a + [0] * (nf - n), np.float64) for a in (us, vs, ms))
    live = (np.arange(nf) < n)[:, None]

    def angle(r, c):
        turns = (np.outer(us, r.ravel()) * nc + np.outer(vs, c.ravel()) * nr) % (nr * nc)
        return 2 * np.pi * turns / (nr * nc)

    def waves(a):
        return np.concatenate([np.cos(a) * live, -np.sin(a) * live])

    every = waves(angle(*np.meshgrid(np.arange(h + 6), np.arange(across), indexing="ij")))
    own = waves(angle(*np.meshgrid(np.arange(h), np.arange(across), indexing="ij")))
    ki, kj = np.meshgrid(np.arange(7), np.arange(8) - 3, indexing="ij")
    taps = angle(ki, kj)
    weight = (ms / (nr * nc))[:, None] * (kj.ravel() < 4)[None, :]
    spectrum = np.concatenate([np.cos(taps) * weight, np.sin(taps) * weight])
    back = np.concatenate([np.cos(taps) * weight, -np.sin(taps) * weight]).T
    return nf, every, own.T, own, every.T, spectrum, back


def dot(a, b):
    return jnp.dot(a, b, preferred_element_type=f32)


def dot_nt(a, b):
    return lax.dot_general(a, b, (((1,), (1,)), ((), ())), preferred_element_type=f32)


def dot_tn(a, b):
    return lax.dot_general(a, b, (((0,), (0,)), ((), ())), preferred_element_type=f32)


def dot_exact(a, b):
    return jnp.dot(a, b, preferred_element_type=f32, precision=lax.Precision.HIGHEST)


def mean(x):
    return jnp.sum(x, axis=-1, keepdims=True) * (1.0 / x.shape[-1])


def total(x):
    return jnp.sum(x, axis=0, keepdims=True)


def lanes(x, width):
    return jnp.concatenate([x] * (width // x.shape[1]), axis=1)


def stack(parts, axis):
    return parts[0] if len(parts) == 1 else jnp.concatenate(parts, axis=axis)


def gelu_parts(v):
    u = v * v
    p = 0.7978667366454887 + u * (
        0.03640226973029483
        + u * (-9.53235048862514e-05 + u * (-3.491248211005391e-05 + u * 1.3019431827058075e-06))
    )
    phi = 0.5 + 0.5 * jnp.tanh(v * p)
    density = jnp.exp2(u * -0.7213475204444817 - 1.3257480647361595)
    return v * phi, phi + v * density


class Masks:
    def __init__(self, h, across):
        n = lax.broadcasted_iota(jnp.int32, ((h + 6) * across, 128), 0)
        self.row, self.col = (n >> (across.bit_length() - 1)) - 3, n & (across - 1)
        self.own_rows = slice(3 * across, (3 + h) * across)
        q = lax.broadcasted_iota(jnp.int32, (h * across // 4, 128), 0)
        half = across // 2
        self.coarse_row, self.coarse_col = 2 * (q >> (half.bit_length() - 1)), 2 * (q & (half - 1))

    def every(self, rows, cols):
        return ((self.row < rows) & (self.col < cols)).astype(f32)

    def own(self, rows, cols):
        r, c = self.row[self.own_rows], self.col[self.own_rows]
        return ((r < rows) & (c < cols)).astype(f32)

    def coarse(self, rows, cols):
        return ((self.coarse_row < rows) & (self.coarse_col < cols)).astype(f32)


def remote(src, dst, send, recv, where):
    return pltpu.make_async_remote_copy(
        src_ref=src, dst_ref=dst, send_sem=send, recv_sem=recv, device_id=where, device_id_type=MESH
    )


def greet(peers):
    barrier = pltpu.get_barrier_semaphore()
    for where in peers:
        pl.semaphore_signal(barrier, inc=1, device_id=where, device_id_type=MESH)
    pl.semaphore_wait(barrier, len(peers))


def stack_vectors(vec, refs):
    C, k = vec.shape[1], 0
    for ref in refs:
        for first in range(0, ref.shape[0], C):
            vec[k : k + 1, :] = ref[first : first + C].reshape(1, C)
            k += 1


def tap_rows(dwk):
    gap = jnp.zeros((1, dwk.shape[-1]), f32)
    return jnp.concatenate([x for i in range(7) for x in (dwk[i], gap)], axis=0)


def forward_kernel(
    G, T, h, across, nf, zs, steps,
    ext, keep, tok, own, cot, fwd, inv, taps, dwk, v0, v1, v2, v3, v4, v5, v6, v7, v8, ew_far, pw_far, dw_far,
    out, act, slope, xhat, fh_out, nm, inv1_out, sh_out, inv2_out, gdw,
    top, bot, spec, vec, red, gdw_s, ew, pw, dw, sem, weight_sem,
):
    g = pl.program_id(0)
    pixels = h * across
    edge = 3 * across
    C = own.shape[-1]
    z, dp = lax.axis_index("sp"), lax.axis_index("dp")
    above, below = {"sp": z - 1, "dp": dp}, {"sp": z + 1, "dp": dp}

    def halo(k, up):
        part = pl.ds(k * T, T)
        if up:
            return remote(tok.at[part, pl.ds(0, edge)], bot.at[part], sem.at[0, 0, k], sem.at[1, 0, k], above)
        return remote(tok.at[part, pl.ds(pixels - edge, edge)], top.at[part], sem.at[0, 1, k], sem.at[1, 1, k], below)

    def each(k, up_act, down_act):
        if up_act is not None:
            pl.when(z > 0)(lambda: up_act(halo(k, True)))
        if down_act is not None:
            pl.when(z < zs - 1)(lambda: down_act(halo(k, False)))

    parts = steps * G // T

    def arrive(part):
        pl.when(z < zs - 1)(lambda: halo(part, True).wait_recv())
        pl.when(z > 0)(lambda: halo(part, False).wait_recv())

    weights = [
        pltpu.make_async_copy(src, dst, weight_sem.at[k])
        for k, (src, dst) in enumerate(((ew_far, ew), (pw_far, pw), (dw_far, dw)))
    ]

    @pl.when(g == 0)
    def _():
        for c in weights:
            c.start()
        greet([{"sp": (z + 1) % zs, "dp": dp}, {"sp": (z + zs - 1) % zs, "dp": dp}])
        for k in range(parts):
            each(k, lambda c: c.start(), lambda c: c.start())

        @pl.when(z == 0)
        def _():
            top[...] = jnp.zeros_like(top)

        @pl.when(z == zs - 1)
        def _():
            bot[...] = jnp.zeros_like(bot)

        gdw_s[...] = jnp.zeros_like(gdw_s)
        spec[...] = dot_exact(taps[...], tap_rows(dwk))
        stack_vectors(vec, (v0, v1, v2, v3, v4, v5, v6, v7, v8))
        for c in weights:
            c.wait()

    for k in range(1, steps):

        @pl.when(g == k)
        def _():
            for part in range(k * (G // T), (k + 1) * (G // T)):
                arrive(part)

    masks = Masks(h, across)
    kr, ki = lanes(spec[:nf], T * C), lanes(spec[nf:], T * C)
    eb = jnp.concatenate([vec[EB + k : EB + k + 1, :] for k in range(ew.shape[1] // C)], axis=1)
    db = jnp.concatenate([vec[DB + k : DB + k + 1, :] for k in range(cot.shape[-1] // C)], axis=1)
    HC = 256
    for team in range(G // T):
        pl.when(g == 0)(functools.partial(arrive, team))
        xs, fields, valids, facs = [], [], [], []
        for t in range(T):
            b = team * T + t
            rows, cols = ext[g * G + b, 0], ext[g * G + b, 1]
            x = jnp.concatenate([top[g * G + b], own[b], bot[g * G + b]], axis=0)
            every = masks.every(rows, cols)
            x = x * lanes(every.astype(bf16), C)
            xs.append(x)
            fields.append(x[masks.own_rows])
            valids.append(every[masks.own_rows])
            facs.append(valids[-1] * (keep[g * G + b].astype(f32) * (1.0 / survival)))
        hat = dot(fwd[...], stack(xs, 1))
        xr, xi = hat[:nf], hat[nf:]
        for t in range(T):
            xhat[team * T + t] = hat[:, t * C : (t + 1) * C].astype(bf16)
        product = jnp.concatenate(
            [(xr * kr - xi * ki).astype(bf16), (xr * ki + xi * kr).astype(bf16)], axis=0
        )
        mixed = dot(inv[...], product)
        mixed = stack([mixed[:, t * C : (t + 1) * C] for t in range(T)], 0) + vec[DWB : DWB + 1, :]
        here = pl.ds(team * T * pixels, T * pixels)
        d = mixed - mean(mixed)
        inv1 = lax.rsqrt(mean(d * d) + epsilon)
        fh = d * inv1
        fh_out[here, :] = fh.astype(bf16)
        inv1_out[here, :] = jnp.broadcast_to(inv1, (T * pixels, 128))
        normed = (fh * vec[NG : NG + 1, :] + vec[NB : NB + 1, :]).astype(bf16)
        nm[here, :] = normed
        branch = vec[PB : PB + 1, :]
        for k in range(ew.shape[1] // HC):
            part = slice(k * HC, (k + 1) * HC)
            a, s = gelu_parts(dot(normed, ew[:, part]) + eb[:, part])
            a = a.astype(bf16)
            act[here, part] = a
            slope[here, part] = s.astype(bf16)
            branch = branch + dot(a, pw[part, :])
        valid, fac = stack(valids, 0), stack(facs, 0)
        res = stack(fields, 0).astype(f32) + lanes(fac, C) * (branch * vec[LS : LS + 1, :])
        d = res - mean(res)
        inv2 = lax.rsqrt(mean(d * d) + epsilon)
        sh = d * inv2
        sh_out[here, :] = sh.astype(bf16)
        inv2_out[here, :] = jnp.broadcast_to(inv2, (T * pixels, 128))
        reduced = (sh * vec[DG : DG + 1, :] + vec[DS : DS + 1, :]) * lanes(valid, C)
        rows_here = T * h // 2
        for k in range(C // 128):
            slab = reduced[:, k * 128 : (k + 1) * 128].reshape(rows_here, 2, across, 128)
            red[k, team * rows_here : (team + 1) * rows_here] = slab
    patch = jnp.concatenate(
        [
            red[k, :, p, pl.ds(q, across // 2, stride=2), :].reshape(G * pixels // 4, 128).astype(bf16)
            for p in range(2)
            for q in range(2)
            for k in range(C // 128)
        ],
        axis=1,
    )
    coarse = stack([masks.coarse(ext[g * G + b, 0], ext[g * G + b, 1]) for b in range(G)], 0)
    coarse = lanes(coarse, cot.shape[-1])
    up = cot[...].reshape(coarse.shape) * coarse.astype(bf16)
    out[...] = ((dot(patch, dw[...]) + db) * coarse).astype(bf16).reshape(out.shape)
    gdw_s[...] += dot_tn(patch, up)

    @pl.when(g == steps - 1)
    def _():
        gdw[...] = gdw_s[...].astype(gdw.dtype)
        for k in range(parts):
            each(k, lambda c: c.wait_send(), lambda c: c.wait_send())


def whole(a):
    return pl.BlockSpec(a.shape, lambda t: (0,) * a.ndim, pipeline_mode=pl.Buffered(1))


def forward(sum_type, zs, G, T, h, across, nf, n_img, ext, keep, own, cot, *consts):
    pixels, C, CO = h * across, own.shape[-1], cot.shape[-1]
    HID = consts[-3].shape[1]
    Q, NP, steps = pixels // 4, n_img * pixels, n_img // G

    def img(*s):
        return pl.BlockSpec((G,) + s, lambda g: (g,) + (0,) * len(s))

    def pix(c):
        return pl.BlockSpec((G * pixels, c), lambda g: (g, 0))

    smem = pl.BlockSpec(memory_space=pltpu.SMEM)
    far = pl.BlockSpec(memory_space=pl.ANY)
    sds = jax.ShapeDtypeStruct
    return pl.pallas_call(
        functools.partial(forward_kernel, G, T, h, across, nf, zs, steps),
        grid=(steps,),
        in_specs=[smem, smem, far, img(pixels, C), img(Q, CO)] + [whole(a) for a in consts[:-3]] + [far] * 3,
        out_specs=[
            img(Q, CO), pix(HID), pix(HID), img(2 * nf, C), pix(C), pix(C), pix(128), pix(C), pix(128),
            pl.BlockSpec((4 * C, CO), lambda g: (0, 0)),
        ],
        out_shape=[
            sds((n_img, Q, CO), bf16), sds((NP, HID), bf16), sds((NP, HID), bf16), sds((n_img, 2 * nf, C), bf16),
            sds((NP, C), bf16), sds((NP, C), bf16), sds((NP, 128), f32), sds((NP, C), bf16), sds((NP, 128), f32),
            sds((4 * C, CO), sum_type),
        ],
        scratch_shapes=[
            pltpu.VMEM((n_img, 3 * across, C), bf16), pltpu.VMEM((n_img, 3 * across, C), bf16),
            pltpu.VMEM((2 * nf, C), f32), pltpu.VMEM((16, C), f32), pltpu.VMEM((C // 128, G * h // 2, 2, across, 128), f32),
            pltpu.VMEM((4 * C, CO), f32), pltpu.VMEM((C, HID), bf16), pltpu.VMEM((HID, C), bf16), pltpu.VMEM((4 * C, CO), bf16),
            pltpu.SemaphoreType.DMA((2, 2, n_img // T)), pltpu.SemaphoreType.DMA((3,)),
        ],
        compiler_params=pltpu.CompilerParams(vmem_limit_bytes=VMEM, collective_id=1, has_side_effects=True),
        name="forward",
    )(ext, keep, own, own, cot, *consts)


class Place:
    def __init__(self, zs):
        self.z, self.dp = lax.axis_index("sp"), lax.axis_index("dp")
        self.core, self.chip = self.dp % 2, self.dp // 2
        self.pair = self.at(self.z, self.dp + 1 - 2 * self.core)
        self.above, self.below = self.at(self.z - 1, self.dp), self.at(self.z + 1, self.dp)
        self.plane, self.column, self.others = [], [], []
        for d in range(1, 4):
            j = (self.chip + d) % 4
            self.plane.append((j, self.at(self.z, j * 2 + self.core)))
        for d in range(1, zs):
            j = (self.z + d) % zs
            self.column.append((j, self.at(j, self.dp)))
        self.me = self.z * 4 + self.chip
        for d in range(1, 4 * zs):
            j = (self.me + d) % (4 * zs)
            self.others.append((j, self.at(j // 4, (j % 4) * 2 + self.core)))

    def at(self, z, dp):
        return {"sp": z, "dp": dp}


class Sum:
    def __init__(self, place, zs, full, half, plane_in, z_in, send, recv, out, by_cols=False):
        self.place, self.full, self.half, self.plane_in, self.z_in = place, full, half, plane_in, z_in
        self.send, self.recv, self.out, self.by_cols = send, recv, out, by_cols
        p = place
        self.R, self.cols = half.shape
        self.rows = self.R // 4
        self.base = pl.multiple_of(p.core * self.R, self.R)
        self.other = pl.multiple_of((1 - p.core) * self.R, self.R)
        self.mine = pl.multiple_of(p.chip * self.rows, self.rows)
        self.z_rows = self.rows if by_cols else self.rows // zs
        self.z_cols = self.cols // zs if by_cols else self.cols

    def z_at(self, j, base):
        if self.by_cols:
            return (pl.ds(base, self.z_rows), pl.ds(pl.multiple_of(j * self.z_cols, self.z_cols), self.z_cols))
        return (pl.ds(pl.multiple_of(base + j * self.z_rows, self.z_rows), self.z_rows), slice(None))

    def copies(self, stage):
        p, n = self.place, len(self.place.column)
        slot = (0, 1, 4, 4 + n, 4 + 2 * n, 7 + 2 * n)[stage]

        def copy(src, dst, where, d=0):
            return remote(src, dst, self.send.at[slot + d], self.recv.at[slot + d], where)

        if stage == 0:
            return [copy(self.full.at[pl.ds(self.other, self.R)], self.half, p.pair)]
        if stage == 1:
            return [
                copy(
                    self.half.at[pl.ds(pl.multiple_of(j * self.rows, self.rows), self.rows)],
                    self.plane_in.at[d],
                    where,
                    d,
                )
                for d, (j, where) in enumerate(p.plane)
            ]
        if stage == 2:
            return [
                copy(self.half.at[self.z_at(j, self.mine)], self.z_in.at[d], where, d)
                for d, (j, where) in enumerate(p.column)
            ]
        if stage == 3:
            src, dst = self.own()
            return [copy(src, dst, where, d) for d, (_, where) in enumerate(p.column)]
        if stage == 4:
            there = self.out.at[pl.ds(pl.multiple_of(self.base + self.mine, self.rows), self.rows)]
            return [copy(there, there, where, d) for d, (_, where) in enumerate(p.plane)]
        there = self.out.at[pl.ds(self.base, self.R)]
        return [copy(there, there, p.pair)]

    def own(self):
        p = self.place
        return self.half.at[self.z_at(p.z, self.mine)], self.out.at[self.z_at(p.z, self.base + self.mine)]

    def own_copy(self):
        src, dst = self.own()
        return pltpu.make_async_copy(src, dst, self.send.at[self.send.shape[0] - 1])

    def add(self, at, parts):
        value = self.half[at].astype(f32)
        for part in parts:
            value = value + part.astype(f32)
        self.half[at] = value.astype(self.half.dtype)

    def step(self, stage):
        if stage > 0:
            for c in self.copies(stage - 1):
                c.wait_recv()
        if stage == 1:
            self.add((slice(None), slice(None)), [self.full[pl.ds(self.base, self.R), :]])
        if stage == 2:
            self.add((pl.ds(self.mine, self.rows), slice(None)), [self.plane_in[d] for d in range(3)])
        if stage == 3:
            n = len(self.place.column)
            self.add(self.z_at(self.place.z, self.mine), [self.z_in[d] for d in range(n)])
            self.own_copy().start()
        if stage == 4:
            self.own_copy().wait()
        if stage < 6:
            for c in self.copies(stage):
                c.start()
        else:
            for k in range(6):
                for c in self.copies(k):
                    c.wait_send()


class SmallSum:
    def __init__(self, place, zs, full, pair_in, tiles_in, send, recv, out):
        self.place, self.full, self.pair_in, self.tiles_in = place, full, pair_in, tiles_in
        self.send, self.recv, self.out, self.n = send, recv, out, 4 * zs

    def tile(self, chip):
        p = self.place
        lane = p.core * 256 + (chip % 2) * 128
        return (pl.ds(pl.multiple_of((chip // 2) * 8, 8), 8), pl.ds(pl.multiple_of(lane, 128), 128))

    def copies(self, stage):
        p, n = self.place, self.n
        if stage == 0:
            return [remote(self.full, self.pair_in, self.send.at[0], self.recv.at[0], p.pair)]
        if stage == 3:
            there = self.out.at[:, pl.ds(pl.multiple_of(p.core * 256, 256), 256)]
            return [remote(there, there, self.send.at[2 * n - 1], self.recv.at[2 * n - 1], p.pair)]
        out = []
        for d, (j, where) in enumerate(p.others):
            slot = (stage - 1) * (n - 1) + 1 + d
            if stage == 1:
                src, dst = self.full.at[self.tile(j)], self.tiles_in.at[d]
            else:
                src, dst = self.full.at[self.tile(p.me)], self.out.at[self.tile(p.me)]
            out.append(remote(src, dst, self.send.at[slot], self.recv.at[slot], where))
        return out

    def own_copy(self):
        at = self.tile(self.place.me)
        return pltpu.make_async_copy(self.full.at[at], self.out.at[at], self.send.at[2 * self.n])

    def step(self, stage):
        if stage > 0:
            for c in self.copies(stage - 1):
                c.wait_recv()
        if stage == 1:
            for c in self.copies(0):
                c.wait_send()
            self.full[...] += self.pair_in[...]
        if stage == 2:
            at = self.tile(self.place.me)
            value = self.full[at]
            for d in range(self.n - 1):
                value = value + self.tiles_in[d]
            self.full[at] = value
            self.own_copy().start()
        if stage == 3:
            self.own_copy().wait()
        if stage < 4:
            for c in self.copies(stage):
                c.start()
        else:
            for k in (1, 2, 3):
                for c in self.copies(k):
                    c.wait_send()


def backward_kernel(
    G, T, h, across, nf, steps, zs, stages,
    ext, keep, cot, sh_in, inv2, act, slope, nm, fh_in, inv1, xhat, gdw_far,
    dw_far, v0, v1, v2, v3, v4, v5, v6, v7, v8, pw_far, ew_far, fwd_own, inv_all, taps, dwk, back,
    own_out, top_in, bot_in, gdw_out, gpw_out, gew_out, small_out,
    held, gres_s, gn_s, gr_s, acc, spec, vec, gpw, gew, geb, vsum, small, gdw_own, dw, pw, ew, weight_sem, halo_sem, *sums,
):
    step = pl.program_id(0)
    pixels = h * across
    C, HID = sh_in.shape[-1], act.shape[-1]
    HC = 512
    masks = Masks(h, across)
    place = Place(zs)
    reduced = {}
    if stages is not None:
        wide = gdw_own.shape[1] // 2
        for k, name in enumerate(("down0", "down1", "project", "expand")):
            buffers, out = list(sums[6 * k : 6 * k + 6]), {2: gpw_out, 3: gew_out}.get(k)
            if k < 2:
                columns = pl.ds(k * wide, wide)
                buffers[0], out = gdw_own.at[:, columns], gdw_out.at[:, columns]
            reduced[name] = Sum(place, zs, *buffers, out, by_cols=name == "expand")
        reduced["small"] = SmallSum(place, zs, small, *sums[24:28], small_out)

    peers = [place.pair] + [w for _, w in place.others] if stages is not None else [w for _, w in place.column]

    weights = [
        pltpu.make_async_copy(src, dst, weight_sem.at[k])
        for k, (src, dst) in enumerate(((dw_far, dw), (gdw_far, gdw_own), (pw_far, pw), (ew_far, ew)))
    ]

    @pl.when(step == 0)
    def _():
        for c in weights:
            c.start()
        barrier = pltpu.get_barrier_semaphore()
        for where in peers:
            pl.semaphore_signal(barrier, inc=1, device_id=where, device_id_type=MESH)
        for ref in (gpw, gew, geb, vsum, acc):
            ref[...] = jnp.zeros_like(ref)
        spec[...] = dot_exact(taps[...], tap_rows(dwk))
        stack_vectors(vec, (v0, v1, v2, v3, v4, v5, v6, v7, v8))
        weights[0].wait()

    @pl.when(step == 1)
    def _():
        for c in weights[1:]:
            c.wait()
        pl.semaphore_wait(pltpu.get_barrier_semaphore(), len(peers))

    def run(at):
        for name, stage in stages.get(at, ()):
            if stage == 0 and name == "project":
                reduced[name].full[...] = gpw[...].T.astype(bf16)
            if stage == 0 and name == "expand":
                reduced[name].full[...] = gew[...].astype(bf16)
            reduced[name].step(stage)

    if stages is not None:
        for at in range(3 * steps):
            if at in stages:
                pl.when(step == at)(functools.partial(run, at))

    def row(k):
        return vec[k : k + 1, :]

    def extent(b, g):
        return ext[g * G + b, 0], ext[g * G + b, 1]

    @pl.when(step < steps)
    def _():
        g = step
        coarse = lanes(stack([masks.coarse(*extent(b, g)) for b in range(G)], 0).astype(bf16), cot.shape[-1])
        up = cot[...].reshape(coarse.shape) * coarse
        gdb = total(up.astype(f32))
        for k in range(cot.shape[-1] // C):
            vsum[V_DB + k : V_DB + k + 1, :] += gdb[:, k * C : (k + 1) * C]
        for p in range(2):
            for q in range(2):
                k = 2 * p + q
                slab = dot_nt(up, dw[k * C : (k + 1) * C, :])
                for n in range(C // 128):
                    gr_s[n, :, p, pl.ds(q, across // 2, stride=2), :] = slab[:, n * 128 : (n + 1) * 128].reshape(
                        G * h // 2, across // 2, 128
                    )
        for team in range(G // T):
            here = pl.ds(team * T * pixels, T * pixels)
            valids = [masks.own(*extent(team * T + t, g)) for t in range(T)]
            facs = [
                valids[t] * (keep[g * G + team * T + t].astype(f32) * (1.0 / survival)) for t in range(T)
            ]
            rows = T * h // 2
            gr = stack(
                [gr_s[n, team * rows : (team + 1) * rows].reshape(T * pixels, 128) for n in range(C // 128)], 1
            )
            gr = gr * lanes(stack(valids, 0), C)
            sh = sh_in[here, :].astype(f32)
            vsum[V_DG : V_DG + 1, :] += total(gr * sh)
            vsum[V_DS : V_DS + 1, :] += total(gr)
            u = gr * row(DG)
            gres = lanes(inv2[here, :], C) * (u - mean(u) - sh * mean(u * sh))
            first = pl.multiple_of(g * (G * pixels) + team * T * pixels, T * pixels)
            gres_s[pl.ds(first, T * pixels), :] = gres.astype(bf16)
            gb = (gres * lanes(stack(facs, 0), C) * row(LS)).astype(bf16)
            for t in range(T):
                held[g * G + team * T + t, :pixels] = gb[t * pixels : (t + 1) * pixels]
            vsum[V_PB : V_PB + 1, :] += total(gb.astype(f32))
            gpw[...] += dot_tn(gb, act[here, :])

    @pl.when((step >= steps) & (step < 2 * steps))
    def _():
        g = step - steps
        for team in range(G // T):
            here = pl.ds(team * T * pixels, T * pixels)
            gb = stack([held[g * G + team * T + t, :pixels] for t in range(T)], 0)
            gn = None
            for k in range(HID // HC):
                part = slice(k * HC, (k + 1) * HC)
                gh = (dot_nt(gb, pw[part, :]) * slope[here, part].astype(f32)).astype(bf16)
                geb[:, part] += total(gh.astype(f32))
                gew[:, part] += dot_tn(nm[here, :], gh)
                term = dot_nt(gh, ew[:, part])
                gn = term if gn is None else gn + term
            gn_s[pl.ds(pl.multiple_of(g * (G * pixels) + team * T * pixels, T * pixels), T * pixels), :] = gn

    def halo(target, g, side, where):
        part, edge = pl.ds(pl.multiple_of(g * G, G), G), 3 * across
        src = held.at[part, pl.ds(side * edge, edge)]
        return remote(src, target.at[part], halo_sem.at[0, side, g], halo_sem.at[1, side, g], where)

    def up(g):
        return halo(bot_in, g, 0, place.above)

    def down(g):
        return halo(top_in, g, 1, place.below)

    @pl.when(step >= 2 * steps)
    def _():
        g = step - 2 * steps
        edge = 3 * across
        kr, ki = lanes(spec[:nf], T * C), lanes(spec[nf:], T * C)
        for team in range(G // T):
            here = pl.ds(team * T * pixels, T * pixels)
            first = pl.multiple_of(g * (G * pixels) + team * T * pixels, T * pixels)
            gn = gn_s[pl.ds(first, T * pixels), :]
            fh = fh_in[here, :].astype(f32)
            vsum[V_NG : V_NG + 1, :] += total(gn * fh)
            vsum[V_NB : V_NB + 1, :] += total(gn)
            w = gn * row(NG)
            gm = lanes(inv1[here, :], C) * (w - mean(w) - fh * mean(w * fh))
            vsum[V_DWB : V_DWB + 1, :] += total(gm)
            gm = gm.astype(bf16)
            gm = stack([gm[t * pixels : (t + 1) * pixels] for t in range(T)], 1)
            hat = dot(fwd_own[...], gm)
            gr, gi = hat[:nf], hat[nf:]
            sr, si = acc[:nf], acc[nf:]
            for t in range(T):
                at = slice(t * C, (t + 1) * C)
                xr, xi = xhat[team * T + t, :nf].astype(f32), xhat[team * T + t, nf:].astype(f32)
                sr = sr + gr[:, at] * xr + gi[:, at] * xi
                si = si + gr[:, at] * xi - gi[:, at] * xr
            acc[:nf] = sr
            acc[nf:] = si
            product = jnp.concatenate(
                [(gr * kr + gi * ki).astype(bf16), (gi * kr - gr * ki).astype(bf16)], axis=0
            )
            o = dot(inv_all[...], product)
            for t in range(T):
                b = g * G + team * T + t
                each = o[:, t * C : (t + 1) * C] * lanes(masks.every(ext[b, 0], ext[b, 1]), C)
                held[b, :edge] = each[:edge].astype(bf16)
                own = gres_s[pl.ds(pl.multiple_of(b * pixels, pixels), pixels), :].astype(f32)
                own_out[team * T + t] = (each[edge : edge + pixels] + own).astype(bf16)
                held[b, edge : 2 * edge] = each[edge + pixels :].astype(bf16)
        pl.when(place.z > 0)(lambda: up(g).start())
        pl.when(place.z < zs - 1)(lambda: down(g).start())

    @pl.when(step == 3 * steps - 1)
    def _():
        small[...] = jnp.zeros_like(small)
        small[0:56, 0:C] = dot_exact(back[...], acc[...])
        for k in range(8 * C // 128):
            v, at = divmod(k, C // 128)
            small[S_VEC + k : S_VEC + k + 1, C:] = vsum[v : v + 1, at * 128 : (at + 1) * 128]
        for k in range(HID // 128):
            small[S_EB + k : S_EB + k + 1, C:] = geb[:, k * 128 : (k + 1) * 128]
        if stages is not None:
            run(3 * steps)
        else:
            for k, (src, dst) in enumerate(((gpw, gpw_out), (gew, gew_out), (small, small_out))):
                c = pltpu.make_async_copy(src, dst, sums[0].at[k])
                c.start()
                c.wait()

        @pl.when(place.z > 0)
        def _():
            for g in range(steps):
                up(g).wait_send()
                down(g).wait_recv()

        @pl.when(place.z < zs - 1)
        def _():
            for g in range(steps):
                down(g).wait_send()
                up(g).wait_recv()


def schedule():
    return {
        1: [("down1", 0)],
        2: [("down1", 1), ("down0", 0)],
        3: [("down0", 1)],
        4: [("project", 0)],
        5: [("down1", 2), ("project", 1)],
        6: [("down0", 2), ("down1", 3)],
        7: [("down0", 3), ("project", 2)],
        8: [("expand", 0), ("project", 3)],
        9: [("down0", 4), ("expand", 1)],
        10: [("project", 4), ("expand", 2)],
        11: [("down1", 4), ("expand", 3)],
        12: [
            ("small", 0), ("down0", 5), ("small", 1), ("project", 5), ("expand", 4), ("down1", 5), ("small", 2), ("expand", 5),
            ("small", 3), ("down0", 6), ("project", 6), ("down1", 6), ("small", 4), ("expand", 6),
        ],
    }


def backward(fused, zs, G, T, h, across, nf, n_img, ext, keep, cot, sh, inv2, act, slope, nm, fh, inv1, xhat, gdw, *consts):
    pixels, C, CO = h * across, sh.shape[-1], cot.shape[-1]
    HID = act.shape[1]
    Q, NP, steps = pixels // 4, n_img * pixels, n_img // G

    def group(first):
        return lambda t: jnp.clip(t - first, 0, steps - 1)

    def img(first, *s):
        return pl.BlockSpec((G,) + s, lambda t: (group(first)(t),) + (0,) * len(s))

    def pix(first, c):
        return pl.BlockSpec((G * pixels, c), lambda t: (group(first)(t), 0))

    any_space = pl.BlockSpec(memory_space=pl.ANY)
    smem = pl.BlockSpec(memory_space=pltpu.SMEM)
    sds = jax.ShapeDtypeStruct

    def sum_buffers(rows, cols, by_cols, dtype, full):
        half = rows // 2
        z = (half // 4, cols // zs) if by_cols else (half // 4 // zs, cols)
        n = 8 + 2 * (zs - 1)
        return [
            pltpu.VMEM((rows, cols) if full else (16, 128), dtype),
            pltpu.VMEM((half, cols), dtype),
            pltpu.VMEM((3, half // 4, cols), dtype),
            pltpu.VMEM((zs - 1,) + z, dtype),
            pltpu.SemaphoreType.DMA((n + 1,)),
            pltpu.SemaphoreType.DMA((n,)),
        ]

    if fused:
        sums = sum_buffers(4 * C, CO // 2, False, bf16, False) * 2
        sums += sum_buffers(HID, C, False, bf16, True)
        sums += sum_buffers(C, HID, True, bf16, True)
        n = 4 * zs
        sums += [
            pltpu.VMEM(SMALL, f32),
            pltpu.VMEM((n - 1, 8, 128), f32),
            pltpu.SemaphoreType.DMA((2 * n + 1,)),
            pltpu.SemaphoreType.DMA((2 * n,)),
        ]
        results = [sds((4 * C, CO), bf16), sds((HID, C), bf16), sds((C, HID), bf16)]
    else:
        sums = [pltpu.SemaphoreType.DMA((3,))]
        results = [sds((16, 128), bf16), sds((C, HID), f32), sds((C, HID), f32)]
        gdw = gdw[:16, :128]
    return pl.pallas_call(
        functools.partial(backward_kernel, G, T, h, across, nf, steps, zs, schedule() if fused else None),
        grid=(3 * steps,),
        in_specs=[
            smem, smem, img(0, Q, CO), pix(0, C), pix(0, 128), pix(0, HID), pix(steps, HID), pix(steps, C), pix(2 * steps, C),
            pix(2 * steps, 128), img(2 * steps, 2 * nf, C), any_space, any_space,
        ]
        + [whole(a) for a in consts[1:10]]
        + [any_space] * 2
        + [whole(a) for a in consts[12:]],
        out_specs=[img(2 * steps, pixels, C)] + [any_space] * 6,
        out_shape=[
            sds((n_img, pixels, C), bf16), sds((n_img, 3 * across, C), bf16), sds((n_img, 3 * across, C), bf16),
        ]
        + results
        + [sds(SMALL, f32)],
        scratch_shapes=[
            pltpu.VMEM((n_img, max(pixels, 6 * across), C), bf16), pltpu.VMEM((NP, C), bf16), pltpu.VMEM((NP, C), f32), pltpu.VMEM((C // 128, G * h // 2, 2, across, 128), f32),
            pltpu.VMEM((2 * nf, C), f32), pltpu.VMEM((2 * nf, C), f32), pltpu.VMEM((16, C), f32), pltpu.VMEM((C, HID), f32), pltpu.VMEM((C, HID), f32),
            pltpu.VMEM((1, HID), f32), pltpu.VMEM((8, C), f32), pltpu.VMEM(SMALL, f32),
            pltpu.VMEM(gdw.shape, gdw.dtype), pltpu.VMEM((4 * C, CO), bf16), pltpu.VMEM((HID, C), bf16), pltpu.VMEM((C, HID), bf16),
            pltpu.SemaphoreType.DMA((4,)), pltpu.SemaphoreType.DMA((2, 2, steps)),
        ]
        + sums,
        compiler_params=pltpu.CompilerParams(vmem_limit_bytes=VMEM, collective_id=0, has_side_effects=True),
        name="backward",
    )(ext, keep, cot, sh, inv2, act, slope, nm, fh, inv1, xhat, gdw, *consts)


def per_device(n_sp, n_dp, *arrays):
    (
        tokens, extents, keep_mask, cotangent, dw_kernel, dw_bias, norm_gain, norm_bias, expand_weight, expand_bias,
        project_weight, project_bias, layer_scale, down_gain, down_shift, down_weight, down_bias,
    ) = arrays
    n_img, h, across, C = tokens.shape
    CO, HID = cotangent.shape[-1], expand_weight.shape[1]
    pixels = h * across
    G, T = 1024 // pixels, 512 // pixels
    fused = n_sp == 4 and n_dp == 8 and n_img // G == 4
    if not fused:
        G = T
    nf, fwd, inv, fwd_own, inv_all, spectrum, back = tables(h, across)
    fwd, inv, fwd_own, inv_all = (jnp.asarray(a, bf16) for a in (fwd, inv, fwd_own, inv_all))
    taps, back = jnp.asarray(spectrum, f32), jnp.asarray(back, f32)
    z = lax.axis_index("sp")
    first = z * h
    ext = extents - jnp.stack([first, jnp.zeros_like(first)])[None, :]
    own = tokens.reshape(n_img, pixels, C)
    cot = cotangent.reshape(n_img, pixels // 4, CO)
    dw = down_weight.reshape(4 * C, CO)
    vectors = (
        dw_bias, norm_gain, norm_bias, project_bias, layer_scale, down_gain, down_shift, down_bias, expand_bias
    )
    out, act, slope, xhat, fh, nm, inv1, sh, inv2, gdw = forward(
        bf16 if fused else f32, n_sp,
        G, T, h, across, nf, n_img, ext, keep_mask, own, cot, fwd, inv, taps, dw_kernel, *vectors, expand_weight, project_weight, dw,
    )
    grad, from_above, from_below, gdw_sum, gpw, gew, small = backward(
        fused, n_sp, G, T, h, across, nf, n_img, ext, keep_mask, cot, sh, inv2, act, slope,
        nm, fh, inv1, xhat, gdw, dw, *vectors, project_weight, expand_weight, fwd_own, inv_all, taps, dw_kernel, back,
    )
    if fused:
        gdw, gpw, gew = (a.astype(f32) for a in (gdw_sum, gpw, gew))
    else:
        gdw, gpw, gew, small = lax.psum((gdw, gpw, gew, small), ("sp", "dp"))
        gpw = gpw.T
    from_above = jnp.where(z > 0, from_above, jnp.zeros_like(from_above))
    from_below = jnp.where(z < n_sp - 1, from_below, jnp.zeros_like(from_below))
    gap = ((0, 0), (0, h - 3), (0, 0), (0, 0))
    pog = ((0, 0), (h - 3, 0), (0, 0), (0, 0))
    grad = (
        grad.reshape(n_img, h, across, C).astype(f32)
        + jnp.pad(from_above.reshape(n_img, 3, across, C), gap).astype(f32)
        + jnp.pad(from_below.reshape(n_img, 3, across, C), pog).astype(f32)
    ).astype(bf16)
    vectors = small[:, C:].reshape(-1)

    def vector(first, size):
        return vectors[first * 128 : first * 128 + size]

    gdg, gds, gpb, gng, gnb, gdwb = (vector(S_VEC + k * C // 128, C) for k in range(6))
    gdb, geb = vector(S_VEC + V_DB * C // 128, CO), vector(S_EB, HID)
    gls = (jnp.sum(project_weight.astype(f32) * gpw, axis=0) + project_bias * gpb) / layer_scale
    gdk = small[:56, :C].reshape(7, 8, C)[:, :7]
    return (
        out.reshape(n_img, h // 2, across // 2, CO), grad, gdk, gdwb, gng, gnb, gew, geb, gpw, gpb, gls, gdg, gds,
        gdw.reshape(down_weight.shape), gdb,
    )


def solution(mesh):
    maps = P("dp", "sp", None, None)
    return jax.shard_map(
        functools.partial(per_device, mesh.shape["sp"], mesh.shape["dp"]),
        mesh=mesh,
        in_specs=(maps, P("dp", None), P("dp"), maps) + (P(),) * 13,
        out_specs=(maps, maps) + (P(),) * 13,
        check_vma=False,
    )
```

```python
import functools

import jax
import jax.numpy as jnp
import numpy as np
from jax import lax
from jax.experimental import pallas as pl
from jax.experimental.pallas import tpu as pltpu
from jax.sharding import PartitionSpec as P

bf16 = jnp.bfloat16
f32 = jnp.float32
epsilon = 1e-06
survival = 0.875
VMEM = 63 * 1024 * 1024
MESH = pl.DeviceIdType.MESH
DWB, NG, NB, PB, LS, DG, DS, DB, EB = 0, 1, 2, 3, 4, 5, 6, 7, 9
V_DG, V_DS, V_PB, V_NG, V_NB, V_DWB, V_DB = 0, 1, 2, 3, 4, 5, 6
SMALL, S_VEC, S_EB = (64, 512), 0, 24


def tables(h, across):
    nr, nc = h + 6, across + 3
    us, vs, ms = [], [], []
    for v in range(nc // 2 + 1):
        for u in range(nr):
            mu, mv = (-u) % nr, (-v) % nc
            if (mv, mu) < (v, u):
                continue
            us.append(u)
            vs.append(v)
            ms.append(1.0 if (mu, mv) == (u, v) else 2.0)
    n = len(us)
    nf = -(-n // 128) * 128
    us, vs, ms = (np.array(a + [0] * (nf - n), np.float64) for a in (us, vs, ms))
    live = (np.arange(nf) < n)[:, None]

    def angle(r, c):
        turns = (np.outer(us, r.ravel()) * nc + np.outer(vs, c.ravel()) * nr) % (nr * nc)
        return 2 * np.pi * turns / (nr * nc)

    def waves(a):
        return np.concatenate([np.cos(a) * live, -np.sin(a) * live])

    every = waves(angle(*np.meshgrid(np.arange(h + 6), np.arange(across), indexing="ij")))
    own = waves(angle(*np.meshgrid(np.arange(h), np.arange(across), indexing="ij")))
    ki, kj = np.meshgrid(np.arange(7), np.arange(8) - 3, indexing="ij")
    taps = angle(ki, kj)
    weight = (ms / (nr * nc))[:, None] * (kj.ravel() < 4)[None, :]
    spectrum = np.concatenate([np.cos(taps) * weight, np.sin(taps) * weight])
    back = np.concatenate([np.cos(taps) * weight, -np.sin(taps) * weight]).T
    return nf, every, own.T, own, every.T, spectrum, back


def dot(a, b):
    return jnp.dot(a, b, preferred_element_type=f32)


def dot_nt(a, b):
    return lax.dot_general(a, b, (((1,), (1,)), ((), ())), preferred_element_type=f32)


def dot_tn(a, b):
    return lax.dot_general(a, b, (((0,), (0,)), ((), ())), preferred_element_type=f32)


def dot_exact(a, b):
    return jnp.dot(a, b, preferred_element_type=f32, precision=lax.Precision.HIGHEST)


def mean(x):
    return jnp.sum(x, axis=-1, keepdims=True) * (1.0 / x.shape[-1])


def total(x):
    return jnp.sum(x, axis=0, keepdims=True)


def lanes(x, width):
    return jnp.concatenate([x] * (width // x.shape[1]), axis=1)


def stack(parts, axis):
    return parts[0] if len(parts) == 1 else jnp.concatenate(parts, axis=axis)


def gelu_parts(v):
    u = v * v
    p = 0.7978667366454887 + u * (
        0.03640226973029483
        + u * (-9.53235048862514e-05 + u * (-3.491248211005391e-05 + u * 1.3019431827058075e-06))
    )
    phi = 0.5 + 0.5 * jnp.tanh(v * p)
    density = jnp.exp2(u * -0.7213475204444817 - 1.3257480647361595)
    return v * phi, phi + v * density


class Masks:
    def __init__(self, h, across):
        n = lax.broadcasted_iota(jnp.int32, ((h + 6) * across, 128), 0)
        self.row, self.col = (n >> (across.bit_length() - 1)) - 3, n & (across - 1)
        self.own_rows = slice(3 * across, (3 + h) * across)
        q = lax.broadcasted_iota(jnp.int32, (h * across // 4, 128), 0)
        half = across // 2
        self.coarse_row, self.coarse_col = 2 * (q >> (half.bit_length() - 1)), 2 * (q & (half - 1))

    def every(self, rows, cols):
        return ((self.row < rows) & (self.col < cols)).astype(f32)

    def own(self, rows, cols):
        r, c = self.row[self.own_rows], self.col[self.own_rows]
        return ((r < rows) & (c < cols)).astype(f32)

    def coarse(self, rows, cols):
        return ((self.coarse_row < rows) & (self.coarse_col < cols)).astype(f32)


def remote(src, dst, send, recv, where):
    return pltpu.make_async_remote_copy(
        src_ref=src, dst_ref=dst, send_sem=send, recv_sem=recv, device_id=where, device_id_type=MESH
    )


def greet(peers):
    barrier = pltpu.get_barrier_semaphore()
    for where in peers:
        pl.semaphore_signal(barrier, inc=1, device_id=where, device_id_type=MESH)
    pl.semaphore_wait(barrier, len(peers))


def stack_vectors(vec, refs):
    C, k = vec.shape[1], 0
    for ref in refs:
        for first in range(0, ref.shape[0], C):
            vec[k : k + 1, :] = ref[first : first + C].reshape(1, C)
            k += 1


def tap_rows(dwk):
    gap = jnp.zeros((1, dwk.shape[-1]), f32)
    return jnp.concatenate([x for i in range(7) for x in (dwk[i], gap)], axis=0)


def forward_kernel(
    G, T, h, across, nf, zs, steps,
    ext, keep, tok, own, cot, fwd, inv, taps, dwk, v0, v1, v2, v3, v4, v5, v6, v7, v8, ew_far, pw_far, dw_far,
    out, act, slope, xhat, fh_out, nm, inv1_out, sh_out, inv2_out, gdw,
    top, bot, spec, vec, red, gdw_s, ew, pw, dw, sem, weight_sem,
):
    g = pl.program_id(0)
    pixels = h * across
    edge = 3 * across
    C = own.shape[-1]
    z, dp = lax.axis_index("sp"), lax.axis_index("dp")
    above, below = {"sp": z - 1, "dp": dp}, {"sp": z + 1, "dp": dp}

    def halo(k, up):
        part = pl.ds(k * T, T)
        if up:
            return remote(tok.at[part, pl.ds(0, edge)], bot.at[part], sem.at[0, 0, k], sem.at[1, 0, k], above)
        return remote(tok.at[part, pl.ds(pixels - edge, edge)], top.at[part], sem.at[0, 1, k], sem.at[1, 1, k], below)

    def each(k, up_act, down_act):
        if up_act is not None:
            pl.when(z > 0)(lambda: up_act(halo(k, True)))
        if down_act is not None:
            pl.when(z < zs - 1)(lambda: down_act(halo(k, False)))

    parts = steps * G // T

    def arrive(part):
        pl.when(z < zs - 1)(lambda: halo(part, True).wait_recv())
        pl.when(z > 0)(lambda: halo(part, False).wait_recv())

    weights = [
        pltpu.make_async_copy(src, dst, weight_sem.at[k])
        for k, (src, dst) in enumerate(((ew_far, ew), (pw_far, pw), (dw_far, dw)))
    ]

    @pl.when(g == 0)
    def _():
        for c in weights:
            c.start()
        greet([{"sp": (z + 1) % zs, "dp": dp}, {"sp": (z + zs - 1) % zs, "dp": dp}])
        for k in range(parts):
            each(k, lambda c: c.start(), lambda c: c.start())

        @pl.when(z == 0)
        def _():
            top[...] = jnp.zeros_like(top)

        @pl.when(z == zs - 1)
        def _():
            bot[...] = jnp.zeros_like(bot)

        gdw_s[...] = jnp.zeros_like(gdw_s)
        spec[...] = dot_exact(taps[...], tap_rows(dwk))
        stack_vectors(vec, (v0, v1, v2, v3, v4, v5, v6, v7, v8))
        for c in weights:
            c.wait()

    for k in range(1, steps):

        @pl.when(g == k)
        def _():
            for part in range(k * (G // T), (k + 1) * (G // T)):
                arrive(part)

    masks = Masks(h, across)
    kr, ki = lanes(spec[:nf], T * C), lanes(spec[nf:], T * C)
    eb = jnp.concatenate([vec[EB + k : EB + k + 1, :] for k in range(ew.shape[1] // C)], axis=1)
    db = jnp.concatenate([vec[DB + k : DB + k + 1, :] for k in range(cot.shape[-1] // C)], axis=1)
    HC = 256
    for team in range(G // T):
        pl.when(g == 0)(functools.partial(arrive, team))
        xs, fields, valids, facs = [], [], [], []
        for t in range(T):
            b = team * T + t
            rows, cols = ext[g * G + b, 0], ext[g * G + b, 1]
            x = jnp.concatenate([top[g * G + b], own[b], bot[g * G + b]], axis=0)
            every = masks.every(rows, cols)
            x = x * lanes(every.astype(bf16), C)
            xs.append(x)
            fields.append(x[masks.own_rows])
            valids.append(every[masks.own_rows])
            facs.append(valids[-1] * (keep[g * G + b].astype(f32) * (1.0 / survival)))
        hat = dot(fwd[...], stack(xs, 1))
        xr, xi = hat[:nf], hat[nf:]
        for t in range(T):
            xhat[team * T + t] = hat[:, t * C : (t + 1) * C].astype(bf16)
        product = jnp.concatenate(
            [(xr * kr - xi * ki).astype(bf16), (xr * ki + xi * kr).astype(bf16)], axis=0
        )
        mixed = dot(inv[...], product)
        mixed = stack([mixed[:, t * C : (t + 1) * C] for t in range(T)], 0) + vec[DWB : DWB + 1, :]
        here = pl.ds(team * T * pixels, T * pixels)
        d = mixed - mean(mixed)
        inv1 = lax.rsqrt(mean(d * d) + epsilon)
        fh = d * inv1
        fh_out[here, :] = fh.astype(bf16)
        inv1_out[here, :] = jnp.broadcast_to(inv1, (T * pixels, 128))
        normed = (fh * vec[NG : NG + 1, :] + vec[NB : NB + 1, :]).astype(bf16)
        nm[here, :] = normed
        branch = vec[PB : PB + 1, :]
        for k in range(ew.shape[1] // HC):
            part = slice(k * HC, (k + 1) * HC)
            a, s = gelu_parts(dot(normed, ew[:, part]) + eb[:, part])
            a = a.astype(bf16)
            act[here, part] = a
            slope[here, part] = s.astype(bf16)
            branch = branch + dot(a, pw[part, :])
        valid, fac = stack(valids, 0), stack(facs, 0)
        res = stack(fields, 0).astype(f32) + lanes(fac, C) * (branch * vec[LS : LS + 1, :])
        d = res - mean(res)
        inv2 = lax.rsqrt(mean(d * d) + epsilon)
        sh = d * inv2
        sh_out[here, :] = sh.astype(bf16)
        inv2_out[here, :] = jnp.broadcast_to(inv2, (T * pixels, 128))
        reduced = (sh * vec[DG : DG + 1, :] + vec[DS : DS + 1, :]) * lanes(valid, C)
        rows_here = T * h // 2
        for k in range(C // 128):
            slab = reduced[:, k * 128 : (k + 1) * 128].reshape(rows_here, 2, across, 128)
            red[k, team * rows_here : (team + 1) * rows_here] = slab
    patch = jnp.concatenate(
        [
            red[k, :, p, pl.ds(q, across // 2, stride=2), :].reshape(G * pixels // 4, 128).astype(bf16)
            for p in range(2)
            for q in range(2)
            for k in range(C // 128)
        ],
        axis=1,
    )
    coarse = stack([masks.coarse(ext[g * G + b, 0], ext[g * G + b, 1]) for b in range(G)], 0)
    coarse = lanes(coarse, cot.shape[-1])
    up = cot[...].reshape(coarse.shape) * coarse.astype(bf16)
    out[...] = ((dot(patch, dw[...]) + db) * coarse).astype(bf16).reshape(out.shape)
    gdw_s[...] += dot_tn(patch, up)

    @pl.when(g == steps - 1)
    def _():
        gdw[...] = gdw_s[...].astype(gdw.dtype)
        for k in range(parts):
            each(k, lambda c: c.wait_send(), lambda c: c.wait_send())


def whole(a):
    return pl.BlockSpec(a.shape, lambda t: (0,) * a.ndim, pipeline_mode=pl.Buffered(1))


def forward(sum_type, zs, G, T, h, across, nf, n_img, ext, keep, own, cot, *consts):
    pixels, C, CO = h * across, own.shape[-1], cot.shape[-1]
    HID = consts[-3].shape[1]
    Q, NP, steps = pixels // 4, n_img * pixels, n_img // G

    def img(*s):
        return pl.BlockSpec((G,) + s, lambda g: (g,) + (0,) * len(s))

    def pix(c):
        return pl.BlockSpec((G * pixels, c), lambda g: (g, 0))

    smem = pl.BlockSpec(memory_space=pltpu.SMEM)
    far = pl.BlockSpec(memory_space=pl.ANY)
    sds = jax.ShapeDtypeStruct
    return pl.pallas_call(
        functools.partial(forward_kernel, G, T, h, across, nf, zs, steps),
        grid=(steps,),
        in_specs=[smem, smem, far, img(pixels, C), img(Q, CO)] + [whole(a) for a in consts[:-3]] + [far] * 3,
        out_specs=[
            img(Q, CO), pix(HID), pix(HID), img(2 * nf, C), pix(C), pix(C), pix(128), pix(C), pix(128),
            pl.BlockSpec((4 * C, CO), lambda g: (0, 0)),
        ],
        out_shape=[
            sds((n_img, Q, CO), bf16), sds((NP, HID), bf16), sds((NP, HID), bf16), sds((n_img, 2 * nf, C), bf16),
            sds((NP, C), bf16), sds((NP, C), bf16), sds((NP, 128), f32), sds((NP, C), bf16), sds((NP, 128), f32),
            sds((4 * C, CO), sum_type),
        ],
        scratch_shapes=[
            pltpu.VMEM((n_img, 3 * across, C), bf16), pltpu.VMEM((n_img, 3 * across, C), bf16),
            pltpu.VMEM((2 * nf, C), f32), pltpu.VMEM((16, C), f32), pltpu.VMEM((C // 128, G * h // 2, 2, across, 128), f32),
            pltpu.VMEM((4 * C, CO), f32), pltpu.VMEM((C, HID), bf16), pltpu.VMEM((HID, C), bf16), pltpu.VMEM((4 * C, CO), bf16),
            pltpu.SemaphoreType.DMA((2, 2, n_img // T)), pltpu.SemaphoreType.DMA((3,)),
        ],
        compiler_params=pltpu.CompilerParams(vmem_limit_bytes=VMEM, collective_id=1, has_side_effects=True),
        name="forward",
    )(ext, keep, own, own, cot, *consts)


class Place:
    def __init__(self, zs):
        self.z, self.dp = lax.axis_index("sp"), lax.axis_index("dp")
        self.core, self.chip = self.dp % 2, self.dp // 2
        self.pair = self.at(self.z, self.dp + 1 - 2 * self.core)
        self.above, self.below = self.at(self.z - 1, self.dp), self.at(self.z + 1, self.dp)
        self.plane, self.column, self.others = [], [], []
        for d in range(1, 4):
            j = (self.chip + d) % 4
            self.plane.append((j, self.at(self.z, j * 2 + self.core)))
        for d in range(1, zs):
            j = (self.z + d) % zs
            self.column.append((j, self.at(j, self.dp)))
        self.me = self.z * 4 + self.chip
        for d in range(1, 4 * zs):
            j = (self.me + d) % (4 * zs)
            self.others.append((j, self.at(j // 4, (j % 4) * 2 + self.core)))

    def at(self, z, dp):
        return {"sp": z, "dp": dp}


class Sum:
    def __init__(self, place, zs, full, half, plane_in, z_in, send, recv, out, by_cols=False):
        self.place, self.full, self.half, self.plane_in, self.z_in = place, full, half, plane_in, z_in
        self.send, self.recv, self.out, self.by_cols = send, recv, out, by_cols
        p = place
        self.R, self.cols = half.shape
        self.rows = self.R // 4
        self.base = pl.multiple_of(p.core * self.R, self.R)
        self.other = pl.multiple_of((1 - p.core) * self.R, self.R)
        self.mine = pl.multiple_of(p.chip * self.rows, self.rows)
        self.z_rows = self.rows if by_cols else self.rows // zs
        self.z_cols = self.cols // zs if by_cols else self.cols

    def z_at(self, j, base):
        if self.by_cols:
            return (pl.ds(base, self.z_rows), pl.ds(pl.multiple_of(j * self.z_cols, self.z_cols), self.z_cols))
        return (pl.ds(pl.multiple_of(base + j * self.z_rows, self.z_rows), self.z_rows), slice(None))

    def copies(self, stage):
        p, n = self.place, len(self.place.column)
        slot = (0, 1, 4, 4 + n, 4 + 2 * n, 7 + 2 * n)[stage]

        def copy(src, dst, where, d=0):
            return remote(src, dst, self.send.at[slot + d], self.recv.at[slot + d], where)

        if stage == 0:
            return [copy(self.full.at[pl.ds(self.other, self.R)], self.half, p.pair)]
        if stage == 1:
            return [
                copy(
                    self.half.at[pl.ds(pl.multiple_of(j * self.rows, self.rows), self.rows)],
                    self.plane_in.at[d],
                    where,
                    d,
                )
                for d, (j, where) in enumerate(p.plane)
            ]
        if stage == 2:
            return [
                copy(self.half.at[self.z_at(j, self.mine)], self.z_in.at[d], where, d)
                for d, (j, where) in enumerate(p.column)
            ]
        if stage == 3:
            src, dst = self.own()
            return [copy(src, dst, where, d) for d, (_, where) in enumerate(p.column)]
        if stage == 4:
            there = self.out.at[pl.ds(pl.multiple_of(self.base + self.mine, self.rows), self.rows)]
            return [copy(there, there, where, d) for d, (_, where) in enumerate(p.plane)]
        there = self.out.at[pl.ds(self.base, self.R)]
        return [copy(there, there, p.pair)]

    def own(self):
        p = self.place
        return self.half.at[self.z_at(p.z, self.mine)], self.out.at[self.z_at(p.z, self.base + self.mine)]

    def own_copy(self):
        src, dst = self.own()
        return pltpu.make_async_copy(src, dst, self.send.at[self.send.shape[0] - 1])

    def add(self, at, parts):
        value = self.half[at].astype(f32)
        for part in parts:
            value = value + part.astype(f32)
        self.half[at] = value.astype(self.half.dtype)

    def step(self, stage):
        if stage > 0:
            for c in self.copies(stage - 1):
                c.wait_recv()
        if stage == 1:
            self.add((slice(None), slice(None)), [self.full[pl.ds(self.base, self.R), :]])
        if stage == 2:
            self.add((pl.ds(self.mine, self.rows), slice(None)), [self.plane_in[d] for d in range(3)])
        if stage == 3:
            n = len(self.place.column)
            self.add(self.z_at(self.place.z, self.mine), [self.z_in[d] for d in range(n)])
            self.own_copy().start()
        if stage == 4:
            self.own_copy().wait()
        if stage < 6:
            for c in self.copies(stage):
                c.start()
        else:
            for k in range(6):
                for c in self.copies(k):
                    c.wait_send()


class SmallSum:
    def __init__(self, place, zs, full, pair_in, tiles_in, send, recv, out):
        self.place, self.full, self.pair_in, self.tiles_in = place, full, pair_in, tiles_in
        self.send, self.recv, self.out, self.n = send, recv, out, 4 * zs

    def tile(self, chip):
        p = self.place
        lane = p.core * 256 + (chip % 2) * 128
        return (pl.ds(pl.multiple_of((chip // 2) * 8, 8), 8), pl.ds(pl.multiple_of(lane, 128), 128))

    def copies(self, stage):
        p, n = self.place, self.n
        if stage == 0:
            return [remote(self.full, self.pair_in, self.send.at[0], self.recv.at[0], p.pair)]
        if stage == 3:
            there = self.out.at[:, pl.ds(pl.multiple_of(p.core * 256, 256), 256)]
            return [remote(there, there, self.send.at[2 * n - 1], self.recv.at[2 * n - 1], p.pair)]
        out = []
        for d, (j, where) in enumerate(p.others):
            slot = (stage - 1) * (n - 1) + 1 + d
            if stage == 1:
                src, dst = self.full.at[self.tile(j)], self.tiles_in.at[d]
            else:
                src, dst = self.full.at[self.tile(p.me)], self.out.at[self.tile(p.me)]
            out.append(remote(src, dst, self.send.at[slot], self.recv.at[slot], where))
        return out

    def own_copy(self):
        at = self.tile(self.place.me)
        return pltpu.make_async_copy(self.full.at[at], self.out.at[at], self.send.at[2 * self.n])

    def step(self, stage):
        if stage > 0:
            for c in self.copies(stage - 1):
                c.wait_recv()
        if stage == 1:
            for c in self.copies(0):
                c.wait_send()
            self.full[...] += self.pair_in[...]
        if stage == 2:
            at = self.tile(self.place.me)
            value = self.full[at]
            for d in range(self.n - 1):
                value = value + self.tiles_in[d]
            self.full[at] = value
            self.own_copy().start()
        if stage == 3:
            self.own_copy().wait()
        if stage < 4:
            for c in self.copies(stage):
                c.start()
        else:
            for k in (1, 2, 3):
                for c in self.copies(k):
                    c.wait_send()


def backward_kernel(
    G, T, h, across, nf, steps, zs, stages,
    ext, keep, cot, sh_in, inv2, act, slope, nm, fh_in, inv1, xhat, gdw_far,
    dw_far, v0, v1, v2, v3, v4, v5, v6, v7, v8, pw_far, ew_far, fwd_own, inv_all, taps, dwk, back,
    own_out, top_in, bot_in, gdw_out, gpw_out, gew_out, small_out,
    held, gres_s, gn_s, gr_s, acc, spec, vec, gpw, gew, geb, vsum, small, gdw_own, dw, pw, ew, weight_sem, halo_sem, *sums,
):
    step = pl.program_id(0)
    pixels = h * across
    C, HID = sh_in.shape[-1], act.shape[-1]
    HC = 768
    masks = Masks(h, across)
    place = Place(zs)
    reduced = {}
    if stages is not None:
        wide = gdw_own.shape[1] // 2
        for k, name in enumerate(("down0", "down1", "project", "expand")):
            buffers, out = list(sums[6 * k : 6 * k + 6]), {2: gpw_out, 3: gew_out}.get(k)
            if k < 2:
                columns = pl.ds(k * wide, wide)
                buffers[0], out = gdw_own.at[:, columns], gdw_out.at[:, columns]
            reduced[name] = Sum(place, zs, *buffers, out, by_cols=name == "expand")
        reduced["small"] = SmallSum(place, zs, small, *sums[24:28], small_out)

    peers = [place.pair] + [w for _, w in place.others] if stages is not None else [w for _, w in place.column]

    weights = [
        pltpu.make_async_copy(src, dst, weight_sem.at[k])
        for k, (src, dst) in enumerate(((dw_far, dw), (gdw_far, gdw_own), (pw_far, pw), (ew_far, ew)))
    ]

    @pl.when(step == 0)
    def _():
        for c in weights:
            c.start()
        barrier = pltpu.get_barrier_semaphore()
        for where in peers:
            pl.semaphore_signal(barrier, inc=1, device_id=where, device_id_type=MESH)
        for ref in (gpw, gew, geb, vsum, acc):
            ref[...] = jnp.zeros_like(ref)
        spec[...] = dot_exact(taps[...], tap_rows(dwk))
        stack_vectors(vec, (v0, v1, v2, v3, v4, v5, v6, v7, v8))
        weights[0].wait()

    @pl.when(step == 1)
    def _():
        for c in weights[1:]:
            c.wait()
        pl.semaphore_wait(pltpu.get_barrier_semaphore(), len(peers))

    def run(at):
        for name, stage in stages.get(at, ()):
            if stage == 0 and name == "project":
                reduced[name].full[...] = gpw[...].T.astype(bf16)
            if stage == 0 and name == "expand":
                reduced[name].full[...] = gew[...].astype(bf16)
            reduced[name].step(stage)

    if stages is not None:
        for at in range(3 * steps):
            if at in stages:
                pl.when(step == at)(functools.partial(run, at))

    def row(k):
        return vec[k : k + 1, :]

    def extent(b, g):
        return ext[g * G + b, 0], ext[g * G + b, 1]

    @pl.when(step < steps)
    def _():
        g = step
        coarse = lanes(stack([masks.coarse(*extent(b, g)) for b in range(G)], 0).astype(bf16), cot.shape[-1])
        up = cot[...].reshape(coarse.shape) * coarse
        gdb = total(up.astype(f32))
        for k in range(cot.shape[-1] // C):
            vsum[V_DB + k : V_DB + k + 1, :] += gdb[:, k * C : (k + 1) * C]
        for p in range(2):
            for q in range(2):
                k = 2 * p + q
                slab = dot_nt(up, dw[k * C : (k + 1) * C, :])
                for n in range(C // 128):
                    gr_s[n, :, p, pl.ds(q, across // 2, stride=2), :] = slab[:, n * 128 : (n + 1) * 128].reshape(
                        G * h // 2, across // 2, 128
                    )
        for team in range(G // T):
            here = pl.ds(team * T * pixels, T * pixels)
            valids = [masks.own(*extent(team * T + t, g)) for t in range(T)]
            facs = [
                valids[t] * (keep[g * G + team * T + t].astype(f32) * (1.0 / survival)) for t in range(T)
            ]
            rows = T * h // 2
            gr = stack(
                [gr_s[n, team * rows : (team + 1) * rows].reshape(T * pixels, 128) for n in range(C // 128)], 1
            )
            gr = gr * lanes(stack(valids, 0), C)
            sh = sh_in[here, :].astype(f32)
            vsum[V_DG : V_DG + 1, :] += total(gr * sh)
            vsum[V_DS : V_DS + 1, :] += total(gr)
            u = gr * row(DG)
            gres = lanes(inv2[here, :], C) * (u - mean(u) - sh * mean(u * sh))
            first = pl.multiple_of(g * (G * pixels) + team * T * pixels, T * pixels)
            gres_s[pl.ds(first, T * pixels), :] = gres.astype(bf16)
            gb = (gres * lanes(stack(facs, 0), C) * row(LS)).astype(bf16)
            for t in range(T):
                held[g * G + team * T + t, :pixels] = gb[t * pixels : (t + 1) * pixels]
            vsum[V_PB : V_PB + 1, :] += total(gb.astype(f32))
            gpw[...] += dot_tn(gb, act[here, :])

    @pl.when((step >= steps) & (step < 2 * steps))
    def _():
        g = step - steps
        for team in range(G // T):
            here = pl.ds(team * T * pixels, T * pixels)
            gb = stack([held[g * G + team * T + t, :pixels] for t in range(T)], 0)
            gn = None
            for k in range(HID // HC):
                part = slice(k * HC, (k + 1) * HC)
                gh = (dot_nt(gb, pw[part, :]) * slope[here, part].astype(f32)).astype(bf16)
                geb[:, part] += total(gh.astype(f32))
                gew[:, part] += dot_tn(nm[here, :], gh)
                term = dot_nt(gh, ew[:, part])
                gn = term if gn is None else gn + term
            gn_s[pl.ds(pl.multiple_of(g * (G * pixels) + team * T * pixels, T * pixels), T * pixels), :] = gn

    def halo(target, g, side, where):
        part, edge = pl.ds(pl.multiple_of(g * G, G), G), 3 * across
        src = held.at[part, pl.ds(side * edge, edge)]
        return remote(src, target.at[part], halo_sem.at[0, side, g], halo_sem.at[1, side, g], where)

    def up(g):
        return halo(bot_in, g, 0, place.above)

    def down(g):
        return halo(top_in, g, 1, place.below)

    @pl.when(step >= 2 * steps)
    def _():
        g = step - 2 * steps
        edge = 3 * across
        kr, ki = lanes(spec[:nf], T * C), lanes(spec[nf:], T * C)
        for team in range(G // T):
            here = pl.ds(team * T * pixels, T * pixels)
            first = pl.multiple_of(g * (G * pixels) + team * T * pixels, T * pixels)
            gn = gn_s[pl.ds(first, T * pixels), :]
            fh = fh_in[here, :].astype(f32)
            vsum[V_NG : V_NG + 1, :] += total(gn * fh)
            vsum[V_NB : V_NB + 1, :] += total(gn)
            w = gn * row(NG)
            gm = lanes(inv1[here, :], C) * (w - mean(w) - fh * mean(w * fh))
            vsum[V_DWB : V_DWB + 1, :] += total(gm)
            gm = gm.astype(bf16)
            gm = stack([gm[t * pixels : (t + 1) * pixels] for t in range(T)], 1)
            hat = dot(fwd_own[...], gm)
            gr, gi = hat[:nf], hat[nf:]
            sr, si = acc[:nf], acc[nf:]
            for t in range(T):
                at = slice(t * C, (t + 1) * C)
                xr, xi = xhat[team * T + t, :nf].astype(f32), xhat[team * T + t, nf:].astype(f32)
                sr = sr + gr[:, at] * xr + gi[:, at] * xi
                si = si + gr[:, at] * xi - gi[:, at] * xr
            acc[:nf] = sr
            acc[nf:] = si
            product = jnp.concatenate(
                [(gr * kr + gi * ki).astype(bf16), (gi * kr - gr * ki).astype(bf16)], axis=0
            )
            o = dot(inv_all[...], product)
            for t in range(T):
                b = g * G + team * T + t
                each = o[:, t * C : (t + 1) * C] * lanes(masks.every(ext[b, 0], ext[b, 1]), C)
                held[b, :edge] = each[:edge].astype(bf16)
                own = gres_s[pl.ds(pl.multiple_of(b * pixels, pixels), pixels), :].astype(f32)
                own_out[team * T + t] = (each[edge : edge + pixels] + own).astype(bf16)
                held[b, edge : 2 * edge] = each[edge + pixels :].astype(bf16)
        pl.when(place.z > 0)(lambda: up(g).start())
        pl.when(place.z < zs - 1)(lambda: down(g).start())

    @pl.when(step == 3 * steps - 1)
    def _():
        small[...] = jnp.zeros_like(small)
        small[0:56, 0:C] = dot_exact(back[...], acc[...])
        for k in range(8 * C // 128):
            v, at = divmod(k, C // 128)
            small[S_VEC + k : S_VEC + k + 1, C:] = vsum[v : v + 1, at * 128 : (at + 1) * 128]
        for k in range(HID // 128):
            small[S_EB + k : S_EB + k + 1, C:] = geb[:, k * 128 : (k + 1) * 128]
        if stages is not None:
            run(3 * steps)
        else:
            for k, (src, dst) in enumerate(((gpw, gpw_out), (gew, gew_out), (small, small_out))):
                c = pltpu.make_async_copy(src, dst, sums[0].at[k])
                c.start()
                c.wait()

        @pl.when(place.z > 0)
        def _():
            for g in range(steps):
                up(g).wait_send()
                down(g).wait_recv()

        @pl.when(place.z < zs - 1)
        def _():
            for g in range(steps):
                down(g).wait_send()
                up(g).wait_recv()


def schedule():
    return {
        1: [('down0', 0)],
        2: [('down0', 1), ('down1', 0)],
        3: [('down1', 1)],
        4: [('project', 0)],
        5: [('down0', 2), ('project', 1)],
        6: [('down0', 3), ('down1', 2)],
        7: [('down1', 3), ('project', 2)],
        8: [('project', 3), ('expand', 0)],
        9: [('expand', 1)],
        10: [('down1', 4), ('expand', 2)],
        11: [('down0', 4), ('project', 4), ('expand', 3)],
        12: [('small', 0), ('down1', 5), ('small', 1), ('down0', 5), ('project', 5), ('expand', 4), ('small', 2), ('expand', 5), ('small', 3), ('down0', 6), ('down1', 6), ('project', 6), ('small', 4), ('expand', 6)],
    }


def backward(fused, zs, G, T, h, across, nf, n_img, ext, keep, cot, sh, inv2, act, slope, nm, fh, inv1, xhat, gdw, *consts):
    pixels, C, CO = h * across, sh.shape[-1], cot.shape[-1]
    HID = act.shape[1]
    Q, NP, steps = pixels // 4, n_img * pixels, n_img // G

    def group(first):
        return lambda t: jnp.clip(t - first, 0, steps - 1)

    def img(first, *s):
        return pl.BlockSpec((G,) + s, lambda t: (group(first)(t),) + (0,) * len(s))

    def pix(first, c):
        return pl.BlockSpec((G * pixels, c), lambda t: (group(first)(t), 0))

    any_space = pl.BlockSpec(memory_space=pl.ANY)
    smem = pl.BlockSpec(memory_space=pltpu.SMEM)
    sds = jax.ShapeDtypeStruct

    def sum_buffers(rows, cols, by_cols, dtype, full):
        half = rows // 2
        z = (half // 4, cols // zs) if by_cols else (half // 4 // zs, cols)
        n = 8 + 2 * (zs - 1)
        return [
            pltpu.VMEM((rows, cols) if full else (16, 128), dtype),
            pltpu.VMEM((half, cols), dtype),
            pltpu.VMEM((3, half // 4, cols), dtype),
            pltpu.VMEM((zs - 1,) + z, dtype),
            pltpu.SemaphoreType.DMA((n + 1,)),
            pltpu.SemaphoreType.DMA((n,)),
        ]

    if fused:
        sums = sum_buffers(4 * C, CO // 2, False, bf16, False) * 2
        sums += sum_buffers(HID, C, False, bf16, True)
        sums += sum_buffers(C, HID, True, bf16, True)
        n = 4 * zs
        sums += [
            pltpu.VMEM(SMALL, f32),
            pltpu.VMEM((n - 1, 8, 128), f32),
            pltpu.SemaphoreType.DMA((2 * n + 1,)),
            pltpu.SemaphoreType.DMA((2 * n,)),
        ]
        results = [sds((4 * C, CO), bf16), sds((HID, C), bf16), sds((C, HID), bf16)]
    else:
        sums = [pltpu.SemaphoreType.DMA((3,))]
        results = [sds((16, 128), bf16), sds((C, HID), f32), sds((C, HID), f32)]
        gdw = gdw[:16, :128]
    return pl.pallas_call(
        functools.partial(backward_kernel, G, T, h, across, nf, steps, zs, schedule() if fused else None),
        grid=(3 * steps,),
        in_specs=[
            smem, smem, img(0, Q, CO), pix(0, C), pix(0, 128), pix(0, HID), pix(steps, HID), pix(steps, C), pix(2 * steps, C),
            pix(2 * steps, 128), img(2 * steps, 2 * nf, C), any_space, any_space,
        ]
        + [whole(a) for a in consts[1:10]]
        + [any_space] * 2
        + [whole(a) for a in consts[12:]],
        out_specs=[img(2 * steps, pixels, C)] + [any_space] * 6,
        out_shape=[
            sds((n_img, pixels, C), bf16), sds((n_img, 3 * across, C), bf16), sds((n_img, 3 * across, C), bf16),
        ]
        + results
        + [sds(SMALL, f32)],
        scratch_shapes=[
            pltpu.VMEM((n_img, max(pixels, 6 * across), C), bf16), pltpu.VMEM((NP, C), bf16), pltpu.VMEM((NP, C), f32), pltpu.VMEM((C // 128, G * h // 2, 2, across, 128), f32),
            pltpu.VMEM((2 * nf, C), f32), pltpu.VMEM((2 * nf, C), f32), pltpu.VMEM((16, C), f32), pltpu.VMEM((C, HID), f32), pltpu.VMEM((C, HID), f32),
            pltpu.VMEM((1, HID), f32), pltpu.VMEM((8, C), f32), pltpu.VMEM(SMALL, f32),
            pltpu.VMEM(gdw.shape, gdw.dtype), pltpu.VMEM((4 * C, CO), bf16), pltpu.VMEM((HID, C), bf16), pltpu.VMEM((C, HID), bf16),
            pltpu.SemaphoreType.DMA((4,)), pltpu.SemaphoreType.DMA((2, 2, steps)),
        ]
        + sums,
        compiler_params=pltpu.CompilerParams(vmem_limit_bytes=VMEM, collective_id=0, has_side_effects=True),
        name="backward",
    )(ext, keep, cot, sh, inv2, act, slope, nm, fh, inv1, xhat, gdw, *consts)


def per_device(n_sp, n_dp, *arrays):
    (
        tokens, extents, keep_mask, cotangent, dw_kernel, dw_bias, norm_gain, norm_bias, expand_weight, expand_bias,
        project_weight, project_bias, layer_scale, down_gain, down_shift, down_weight, down_bias,
    ) = arrays
    n_img, h, across, C = tokens.shape
    CO, HID = cotangent.shape[-1], expand_weight.shape[1]
    pixels = h * across
    G, T = 1024 // pixels, 512 // pixels
    fused = n_sp == 4 and n_dp == 8 and n_img // G == 4
    if not fused:
        G = T
    nf, fwd, inv, fwd_own, inv_all, spectrum, back = tables(h, across)
    fwd, inv, fwd_own, inv_all = (jnp.asarray(a, bf16) for a in (fwd, inv, fwd_own, inv_all))
    taps, back = jnp.asarray(spectrum, f32), jnp.asarray(back, f32)
    z = lax.axis_index("sp")
    first = z * h
    ext = extents - jnp.stack([first, jnp.zeros_like(first)])[None, :]
    own = tokens.reshape(n_img, pixels, C)
    cot = cotangent.reshape(n_img, pixels // 4, CO)
    dw = down_weight.reshape(4 * C, CO)
    vectors = (
        dw_bias, norm_gain, norm_bias, project_bias, layer_scale, down_gain, down_shift, down_bias, expand_bias
    )
    out, act, slope, xhat, fh, nm, inv1, sh, inv2, gdw = forward(
        bf16 if fused else f32, n_sp,
        G, T, h, across, nf, n_img, ext, keep_mask, own, cot, fwd, inv, taps, dw_kernel, *vectors, expand_weight, project_weight, dw,
    )
    grad, from_above, from_below, gdw_sum, gpw, gew, small = backward(
        fused, n_sp, G, T, h, across, nf, n_img, ext, keep_mask, cot, sh, inv2, act, slope,
        nm, fh, inv1, xhat, gdw, dw, *vectors, project_weight, expand_weight, fwd_own, inv_all, taps, dw_kernel, back,
    )
    if fused:
        gdw, gpw, gew = (a.astype(f32) for a in (gdw_sum, gpw, gew))
    else:
        gdw, gpw, gew, small = lax.psum((gdw, gpw, gew, small), ("sp", "dp"))
        gpw = gpw.T
    from_above = jnp.where(z > 0, from_above, jnp.zeros_like(from_above))
    from_below = jnp.where(z < n_sp - 1, from_below, jnp.zeros_like(from_below))
    gap = ((0, 0), (0, h - 3), (0, 0), (0, 0))
    pog = ((0, 0), (h - 3, 0), (0, 0), (0, 0))
    grad = (
        grad.reshape(n_img, h, across, C).astype(f32)
        + jnp.pad(from_above.reshape(n_img, 3, across, C), gap).astype(f32)
        + jnp.pad(from_below.reshape(n_img, 3, across, C), pog).astype(f32)
    ).astype(bf16)
    vectors = small[:, C:].reshape(-1)

    def vector(first, size):
        return vectors[first * 128 : first * 128 + size]

    gdg, gds, gpb, gng, gnb, gdwb = (vector(S_VEC + k * C // 128, C) for k in range(6))
    gdb, geb = vector(S_VEC + V_DB * C // 128, CO), vector(S_EB, HID)
    gls = (jnp.sum(project_weight.astype(f32) * gpw, axis=0) + project_bias * gpb) / layer_scale
    gdk = small[:56, :C].reshape(7, 8, C)[:, :7]
    return (
        out.reshape(n_img, h // 2, across // 2, CO), grad, gdk, gdwb, gng, gnb, gew, geb, gpw, gpb, gls, gdg, gds,
        gdw.reshape(down_weight.shape), gdb,
    )


def solution(mesh):
    maps = P("dp", "sp", None, None)
    return jax.shard_map(
        functools.partial(per_device, mesh.shape["sp"], mesh.shape["dp"]),
        mesh=mesh,
        in_specs=(maps, P("dp", None), P("dp"), maps) + (P(),) * 13,
        out_specs=(maps, maps) + (P(),) * 13,
        check_vma=False,
    )
```

```python
import functools

import jax
import jax.numpy as jnp
import numpy as np
from jax import lax
from jax.experimental import pallas as pl
from jax.experimental.pallas import tpu as pltpu
from jax.sharding import PartitionSpec as P

bf16 = jnp.bfloat16
f32 = jnp.float32
epsilon = 1e-06
survival = 0.875
VMEM = 63 * 1024 * 1024
MESH = pl.DeviceIdType.MESH
DWB, NG, NB, PB, LS, DG, DS, DB, EB = 0, 1, 2, 3, 4, 5, 6, 7, 9
V_DG, V_DS, V_PB, V_NG, V_NB, V_DWB, V_DB = 0, 1, 2, 3, 4, 5, 6
SMALL, S_VEC, S_EB = (64, 512), 0, 24


def tables(h, across):
    nr, nc = h + 6, across + 3
    us, vs, ms = [], [], []
    for v in range(nc // 2 + 1):
        for u in range(nr):
            mu, mv = (-u) % nr, (-v) % nc
            if (mv, mu) < (v, u):
                continue
            us.append(u)
            vs.append(v)
            ms.append(1.0 if (mu, mv) == (u, v) else 2.0)
    n = len(us)
    nf = -(-n // 128) * 128
    us, vs, ms = (np.array(a + [0] * (nf - n), np.float64) for a in (us, vs, ms))
    live = (np.arange(nf) < n)[:, None]

    def angle(r, c):
        turns = (np.outer(us, r.ravel()) * nc + np.outer(vs, c.ravel()) * nr) % (nr * nc)
        return 2 * np.pi * turns / (nr * nc)

    def waves(a):
        return np.concatenate([np.cos(a) * live, -np.sin(a) * live])

    every = waves(angle(*np.meshgrid(np.arange(h + 6), np.arange(across), indexing="ij")))
    own = waves(angle(*np.meshgrid(np.arange(h), np.arange(across), indexing="ij")))
    ki, kj = np.meshgrid(np.arange(7), np.arange(8) - 3, indexing="ij")
    taps = angle(ki, kj)
    weight = (ms / (nr * nc))[:, None] * (kj.ravel() < 4)[None, :]
    spectrum = np.concatenate([np.cos(taps) * weight, np.sin(taps) * weight])
    back = np.concatenate([np.cos(taps) * weight, -np.sin(taps) * weight]).T
    return nf, every, own.T, own, every.T, spectrum, back


def dot(a, b):
    return jnp.dot(a, b, preferred_element_type=f32)


def dot_nt(a, b):
    return lax.dot_general(a, b, (((1,), (1,)), ((), ())), preferred_element_type=f32)


def dot_tn(a, b):
    return lax.dot_general(a, b, (((0,), (0,)), ((), ())), preferred_element_type=f32)


def dot_exact(a, b):
    return jnp.dot(a, b, preferred_element_type=f32, precision=lax.Precision.HIGHEST)


def mean(x):
    return jnp.sum(x, axis=-1, keepdims=True) * (1.0 / x.shape[-1])


def total(x):
    return jnp.sum(x, axis=0, keepdims=True)


def lanes(x, width):
    return jnp.concatenate([x] * (width // x.shape[1]), axis=1)


def stack(parts, axis):
    return parts[0] if len(parts) == 1 else jnp.concatenate(parts, axis=axis)


def gelu_parts(v):
    u = v * v
    p = 0.7978667366454887 + u * (
        0.03640226973029483
        + u * (-9.53235048862514e-05 + u * (-3.491248211005391e-05 + u * 1.3019431827058075e-06))
    )
    phi = 0.5 + 0.5 * jnp.tanh(v * p)
    density = jnp.exp2(u * -0.7213475204444817 - 1.3257480647361595)
    return v * phi, phi + v * density


class Masks:
    def __init__(self, h, across):
        n = lax.broadcasted_iota(jnp.int32, ((h + 6) * across, 128), 0)
        self.row, self.col = (n >> (across.bit_length() - 1)) - 3, n & (across - 1)
        self.own_rows = slice(3 * across, (3 + h) * across)
        q = lax.broadcasted_iota(jnp.int32, (h * across // 4, 128), 0)
        half = across // 2
        self.coarse_row, self.coarse_col = 2 * (q >> (half.bit_length() - 1)), 2 * (q & (half - 1))

    def every(self, rows, cols):
        return ((self.row < rows) & (self.col < cols)).astype(f32)

    def own(self, rows, cols):
        r, c = self.row[self.own_rows], self.col[self.own_rows]
        return ((r < rows) & (c < cols)).astype(f32)

    def coarse(self, rows, cols):
        return ((self.coarse_row < rows) & (self.coarse_col < cols)).astype(f32)


def remote(src, dst, send, recv, where):
    return pltpu.make_async_remote_copy(
        src_ref=src, dst_ref=dst, send_sem=send, recv_sem=recv, device_id=where, device_id_type=MESH
    )


def greet(peers):
    barrier = pltpu.get_barrier_semaphore()
    for where in peers:
        pl.semaphore_signal(barrier, inc=1, device_id=where, device_id_type=MESH)
    pl.semaphore_wait(barrier, len(peers))


def stack_vectors(vec, refs):
    C, k = vec.shape[1], 0
    for ref in refs:
        for first in range(0, ref.shape[0], C):
            vec[k : k + 1, :] = ref[first : first + C].reshape(1, C)
            k += 1


def tap_rows(dwk):
    gap = jnp.zeros((1, dwk.shape[-1]), f32)
    return jnp.concatenate([x for i in range(7) for x in (dwk[i], gap)], axis=0)


def forward_kernel(
    G, T, h, across, nf, zs, steps,
    ext, keep, tok, own, cot, fwd, inv, taps, dwk, v0, v1, v2, v3, v4, v5, v6, v7, v8, ew_far, pw_far, dw_far,
    out, act, slope, xhat, fh_out, nm, inv1_out, sh_out, inv2_out, gdw, spec,
    top, bot, vec, red, gdw_s, ew, pw, dw, sem, weight_sem,
):
    g = pl.program_id(0)
    pixels = h * across
    edge = 3 * across
    C = own.shape[-1]
    z, dp = lax.axis_index("sp"), lax.axis_index("dp")
    above, below = {"sp": z - 1, "dp": dp}, {"sp": z + 1, "dp": dp}

    def halo(k, up):
        part = pl.ds(k * T, T)
        if up:
            return remote(tok.at[part, pl.ds(0, edge)], bot.at[part], sem.at[0, 0, k], sem.at[1, 0, k], above)
        return remote(tok.at[part, pl.ds(pixels - edge, edge)], top.at[part], sem.at[0, 1, k], sem.at[1, 1, k], below)

    def each(k, up_act, down_act):
        if up_act is not None:
            pl.when(z > 0)(lambda: up_act(halo(k, True)))
        if down_act is not None:
            pl.when(z < zs - 1)(lambda: down_act(halo(k, False)))

    parts = steps * G // T

    def arrive(part):
        pl.when(z < zs - 1)(lambda: halo(part, True).wait_recv())
        pl.when(z > 0)(lambda: halo(part, False).wait_recv())

    weights = [
        pltpu.make_async_copy(src, dst, weight_sem.at[k])
        for k, (src, dst) in enumerate(((ew_far, ew), (pw_far, pw), (dw_far, dw)))
    ]

    @pl.when(g == 0)
    def _():
        for c in weights:
            c.start()
        greet([{"sp": (z + 1) % zs, "dp": dp}, {"sp": (z + zs - 1) % zs, "dp": dp}])
        for k in range(parts):
            each(k, lambda c: c.start(), lambda c: c.start())

        @pl.when(z == 0)
        def _():
            top[...] = jnp.zeros_like(top)

        @pl.when(z == zs - 1)
        def _():
            bot[...] = jnp.zeros_like(bot)

        gdw_s[...] = jnp.zeros_like(gdw_s)
        spec[...] = dot_exact(taps[...], tap_rows(dwk))
        stack_vectors(vec, (v0, v1, v2, v3, v4, v5, v6, v7, v8))
        for c in weights:
            c.wait()

    for k in range(1, steps):

        @pl.when(g == k)
        def _():
            for part in range(k * (G // T), (k + 1) * (G // T)):
                arrive(part)

    masks = Masks(h, across)
    kr, ki = lanes(spec[:nf], T * C), lanes(spec[nf:], T * C)
    eb = jnp.concatenate([vec[EB + k : EB + k + 1, :] for k in range(ew.shape[1] // C)], axis=1)
    db = jnp.concatenate([vec[DB + k : DB + k + 1, :] for k in range(cot.shape[-1] // C)], axis=1)
    HC = 256
    for team in range(G // T):
        pl.when(g == 0)(functools.partial(arrive, team))
        xs, fields, valids, facs = [], [], [], []
        for t in range(T):
            b = team * T + t
            rows, cols = ext[g * G + b, 0], ext[g * G + b, 1]
            x = jnp.concatenate([top[g * G + b], own[b], bot[g * G + b]], axis=0)
            every = masks.every(rows, cols)
            x = x * lanes(every.astype(bf16), C)
            xs.append(x)
            fields.append(x[masks.own_rows])
            valids.append(every[masks.own_rows])
            facs.append(valids[-1] * (keep[g * G + b].astype(f32) * (1.0 / survival)))
        hat = dot(fwd[...], stack(xs, 1))
        xr, xi = hat[:nf], hat[nf:]
        for t in range(T):
            xhat[team * T + t] = hat[:, t * C : (t + 1) * C].astype(bf16)
        product = jnp.concatenate(
            [(xr * kr - xi * ki).astype(bf16), (xr * ki + xi * kr).astype(bf16)], axis=0
        )
        mixed = dot(inv[...], product)
        mixed = stack([mixed[:, t * C : (t + 1) * C] for t in range(T)], 0) + vec[DWB : DWB + 1, :]
        here = pl.ds(team * T * pixels, T * pixels)
        d = mixed - mean(mixed)
        inv1 = lax.rsqrt(mean(d * d) + epsilon)
        fh = d * inv1
        fh_out[here, :] = fh.astype(bf16)
        inv1_out[here, :] = jnp.broadcast_to(inv1, (T * pixels, 128))
        normed = (fh * vec[NG : NG + 1, :] + vec[NB : NB + 1, :]).astype(bf16)
        nm[here, :] = normed
        branch = vec[PB : PB + 1, :]
        for k in range(ew.shape[1] // HC):
            part = slice(k * HC, (k + 1) * HC)
            a, s = gelu_parts(dot(normed, ew[:, part]) + eb[:, part])
            a = a.astype(bf16)
            act[here, part] = a
            slope[here, part] = s.astype(bf16)
            branch = branch + dot(a, pw[part, :])
        valid, fac = stack(valids, 0), stack(facs, 0)
        res = stack(fields, 0).astype(f32) + lanes(fac, C) * (branch * vec[LS : LS + 1, :])
        d = res - mean(res)
        inv2 = lax.rsqrt(mean(d * d) + epsilon)
        sh = d * inv2
        sh_out[here, :] = sh.astype(bf16)
        inv2_out[here, :] = jnp.broadcast_to(inv2, (T * pixels, 128))
        reduced = (sh * vec[DG : DG + 1, :] + vec[DS : DS + 1, :]) * lanes(valid, C)
        rows_here = T * h // 2
        for k in range(C // 128):
            slab = reduced[:, k * 128 : (k + 1) * 128].reshape(rows_here, 2, across, 128)
            red[k, team * rows_here : (team + 1) * rows_here] = slab
    patch = jnp.concatenate(
        [
            red[k, :, p, pl.ds(q, across // 2, stride=2), :].reshape(G * pixels // 4, 128).astype(bf16)
            for p in range(2)
            for q in range(2)
            for k in range(C // 128)
        ],
        axis=1,
    )
    coarse = stack([masks.coarse(ext[g * G + b, 0], ext[g * G + b, 1]) for b in range(G)], 0)
    coarse = lanes(coarse, cot.shape[-1])
    up = cot[...].reshape(coarse.shape) * coarse.astype(bf16)
    out[...] = ((dot(patch, dw[...]) + db) * coarse).astype(bf16).reshape(out.shape)
    gdw_s[...] += dot_tn(patch, up)

    @pl.when(g == steps - 1)
    def _():
        gdw[...] = gdw_s[...].astype(gdw.dtype)
        for k in range(parts):
            each(k, lambda c: c.wait_send(), lambda c: c.wait_send())


def whole(a):
    return pl.BlockSpec(a.shape, lambda t: (0,) * a.ndim, pipeline_mode=pl.Buffered(1))


def forward(sum_type, zs, G, T, h, across, nf, n_img, ext, keep, own, cot, *consts):
    pixels, C, CO = h * across, own.shape[-1], cot.shape[-1]
    HID = consts[-3].shape[1]
    Q, NP, steps = pixels // 4, n_img * pixels, n_img // G

    def img(*s):
        return pl.BlockSpec((G,) + s, lambda g: (g,) + (0,) * len(s))

    def pix(c):
        return pl.BlockSpec((G * pixels, c), lambda g: (g, 0))

    smem = pl.BlockSpec(memory_space=pltpu.SMEM)
    far = pl.BlockSpec(memory_space=pl.ANY)
    sds = jax.ShapeDtypeStruct
    return pl.pallas_call(
        functools.partial(forward_kernel, G, T, h, across, nf, zs, steps),
        grid=(steps,),
        in_specs=[smem, smem, far, img(pixels, C), img(Q, CO)] + [whole(a) for a in consts[:-3]] + [far] * 3,
        out_specs=[
            img(Q, CO), pix(HID), pix(HID), img(2 * nf, C), pix(C), pix(C), pix(128), pix(C), pix(128),
            pl.BlockSpec((4 * C, CO), lambda g: (0, 0)), pl.BlockSpec((2 * nf, C), lambda g: (0, 0)),
        ],
        out_shape=[
            sds((n_img, Q, CO), bf16), sds((NP, HID), bf16), sds((NP, HID), bf16), sds((n_img, 2 * nf, C), bf16),
            sds((NP, C), bf16), sds((NP, C), bf16), sds((NP, 128), f32), sds((NP, C), bf16), sds((NP, 128), f32),
            sds((4 * C, CO), sum_type), sds((2 * nf, C), f32),
        ],
        scratch_shapes=[
            pltpu.VMEM((n_img, 3 * across, C), bf16), pltpu.VMEM((n_img, 3 * across, C), bf16),
            pltpu.VMEM((16, C), f32), pltpu.VMEM((C // 128, G * h // 2, 2, across, 128), f32),
            pltpu.VMEM((4 * C, CO), f32), pltpu.VMEM((C, HID), bf16), pltpu.VMEM((HID, C), bf16), pltpu.VMEM((4 * C, CO), bf16),
            pltpu.SemaphoreType.DMA((2, 2, n_img // T)), pltpu.SemaphoreType.DMA((3,)),
        ],
        compiler_params=pltpu.CompilerParams(vmem_limit_bytes=VMEM, collective_id=1, has_side_effects=True),
        name="forward",
    )(ext, keep, own, own, cot, *consts)


class Place:
    def __init__(self, zs):
        self.z, self.dp = lax.axis_index("sp"), lax.axis_index("dp")
        self.core, self.chip = self.dp % 2, self.dp // 2
        self.pair = self.at(self.z, self.dp + 1 - 2 * self.core)
        self.above, self.below = self.at(self.z - 1, self.dp), self.at(self.z + 1, self.dp)
        self.plane, self.column, self.others = [], [], []
        for d in range(1, 4):
            j = (self.chip + d) % 4
            self.plane.append((j, self.at(self.z, j * 2 + self.core)))
        for d in range(1, zs):
            j = (self.z + d) % zs
            self.column.append((j, self.at(j, self.dp)))
        self.me = self.z * 4 + self.chip
        for d in range(1, 4 * zs):
            j = (self.me + d) % (4 * zs)
            self.others.append((j, self.at(j // 4, (j % 4) * 2 + self.core)))

    def at(self, z, dp):
        return {"sp": z, "dp": dp}


class Sum:
    def __init__(self, place, zs, full, half, plane_in, z_in, send, recv, out, by_cols=False):
        self.place, self.full, self.half, self.plane_in, self.z_in = place, full, half, plane_in, z_in
        self.send, self.recv, self.out, self.by_cols = send, recv, out, by_cols
        p = place
        self.R, self.cols = half.shape
        self.rows = self.R // 4
        self.base = pl.multiple_of(p.core * self.R, self.R)
        self.other = pl.multiple_of((1 - p.core) * self.R, self.R)
        self.mine = pl.multiple_of(p.chip * self.rows, self.rows)
        self.z_rows = self.rows if by_cols else self.rows // zs
        self.z_cols = self.cols // zs if by_cols else self.cols

    def z_at(self, j, base):
        if self.by_cols:
            return (pl.ds(base, self.z_rows), pl.ds(pl.multiple_of(j * self.z_cols, self.z_cols), self.z_cols))
        return (pl.ds(pl.multiple_of(base + j * self.z_rows, self.z_rows), self.z_rows), slice(None))

    def copies(self, stage):
        p, n = self.place, len(self.place.column)
        slot = (0, 1, 4, 4 + n, 4 + 2 * n, 7 + 2 * n)[stage]

        def copy(src, dst, where, d=0):
            return remote(src, dst, self.send.at[slot + d], self.recv.at[slot + d], where)

        if stage == 0:
            return [copy(self.full.at[pl.ds(self.other, self.R)], self.half, p.pair)]
        if stage == 1:
            return [
                copy(
                    self.half.at[pl.ds(pl.multiple_of(j * self.rows, self.rows), self.rows)],
                    self.plane_in.at[d],
                    where,
                    d,
                )
                for d, (j, where) in enumerate(p.plane)
            ]
        if stage == 2:
            return [
                copy(self.half.at[self.z_at(j, self.mine)], self.z_in.at[d], where, d)
                for d, (j, where) in enumerate(p.column)
            ]
        if stage == 3:
            src, dst = self.own()
            return [copy(src, dst, where, d) for d, (_, where) in enumerate(p.column)]
        if stage == 4:
            there = self.out.at[pl.ds(pl.multiple_of(self.base + self.mine, self.rows), self.rows)]
            return [copy(there, there, where, d) for d, (_, where) in enumerate(p.plane)]
        there = self.out.at[pl.ds(self.base, self.R)]
        return [copy(there, there, p.pair)]

    def own(self):
        p = self.place
        return self.half.at[self.z_at(p.z, self.mine)], self.out.at[self.z_at(p.z, self.base + self.mine)]

    def own_copy(self):
        src, dst = self.own()
        return pltpu.make_async_copy(src, dst, self.send.at[self.send.shape[0] - 1])

    def add(self, at, parts):
        value = self.half[at].astype(f32)
        for part in parts:
            value = value + part.astype(f32)
        self.half[at] = value.astype(self.half.dtype)

    def step(self, stage):
        if stage > 0:
            for c in self.copies(stage - 1):
                c.wait_recv()
        if stage == 1:
            self.add((slice(None), slice(None)), [self.full[pl.ds(self.base, self.R), :]])
        if stage == 2:
            self.add((pl.ds(self.mine, self.rows), slice(None)), [self.plane_in[d] for d in range(3)])
        if stage == 3:
            n = len(self.place.column)
            self.add(self.z_at(self.place.z, self.mine), [self.z_in[d] for d in range(n)])
            self.own_copy().start()
        if stage == 4:
            self.own_copy().wait()
        if stage < 6:
            for c in self.copies(stage):
                c.start()
        else:
            for k in range(6):
                for c in self.copies(k):
                    c.wait_send()


class SmallSum:
    def __init__(self, place, zs, full, pair_in, tiles_in, send, recv, out):
        self.place, self.full, self.pair_in, self.tiles_in = place, full, pair_in, tiles_in
        self.send, self.recv, self.out, self.n = send, recv, out, 4 * zs

    def tile(self, chip):
        p = self.place
        lane = p.core * 256 + (chip % 2) * 128
        return (pl.ds(pl.multiple_of((chip // 2) * 8, 8), 8), pl.ds(pl.multiple_of(lane, 128), 128))

    def copies(self, stage):
        p, n = self.place, self.n
        if stage == 0:
            return [remote(self.full, self.pair_in, self.send.at[0], self.recv.at[0], p.pair)]
        if stage == 3:
            there = self.out.at[:, pl.ds(pl.multiple_of(p.core * 256, 256), 256)]
            return [remote(there, there, self.send.at[2 * n - 1], self.recv.at[2 * n - 1], p.pair)]
        out = []
        for d, (j, where) in enumerate(p.others):
            slot = (stage - 1) * (n - 1) + 1 + d
            if stage == 1:
                src, dst = self.full.at[self.tile(j)], self.tiles_in.at[d]
            else:
                src, dst = self.full.at[self.tile(p.me)], self.out.at[self.tile(p.me)]
            out.append(remote(src, dst, self.send.at[slot], self.recv.at[slot], where))
        return out

    def own_copy(self):
        at = self.tile(self.place.me)
        return pltpu.make_async_copy(self.full.at[at], self.out.at[at], self.send.at[2 * self.n])

    def step(self, stage):
        if stage > 0:
            for c in self.copies(stage - 1):
                c.wait_recv()
        if stage == 1:
            for c in self.copies(0):
                c.wait_send()
            self.full[...] += self.pair_in[...]
        if stage == 2:
            at = self.tile(self.place.me)
            value = self.full[at]
            for d in range(self.n - 1):
                value = value + self.tiles_in[d]
            self.full[at] = value
            self.own_copy().start()
        if stage == 3:
            self.own_copy().wait()
        if stage < 4:
            for c in self.copies(stage):
                c.start()
        else:
            for k in (1, 2, 3):
                for c in self.copies(k):
                    c.wait_send()


def backward_kernel(
    G, T, h, across, nf, steps, zs, stages,
    ext, keep, cot, sh_in, inv2, act, slope, nm, fh_in, inv1, xhat, gdw_far,
    dw_far, v0, v1, v2, v3, v4, v5, v6, v7, v8, pw_far, ew_far, fwd_own, inv_all, spec_far, back,
    own_out, top_in, bot_in, gdw_out, gpw_out, gew_out, small_out,
    held, gres_s, gn_s, gr_s, acc, spec, vec, gpw, gew, geb, vsum, small, gdw_own, dw, pw, ew, weight_sem, halo_sem, *sums,
):
    step = pl.program_id(0)
    pixels = h * across
    C, HID = sh_in.shape[-1], act.shape[-1]
    HC = 768
    masks = Masks(h, across)
    place = Place(zs)
    reduced = {}
    if stages is not None:
        wide = gdw_own.shape[1] // 2
        for k, name in enumerate(("down0", "down1", "project", "expand")):
            buffers, out = list(sums[6 * k : 6 * k + 6]), {2: gpw_out, 3: gew_out}.get(k)
            if k < 2:
                columns = pl.ds(k * wide, wide)
                buffers[0], out = gdw_own.at[:, columns], gdw_out.at[:, columns]
            reduced[name] = Sum(place, zs, *buffers, out, by_cols=name == "expand")
        reduced["small"] = SmallSum(place, zs, small, *sums[24:28], small_out)

    peers = [place.pair] + [w for _, w in place.others] if stages is not None else [w for _, w in place.column]

    weights = [
        pltpu.make_async_copy(src, dst, weight_sem.at[k])
        for k, (src, dst) in enumerate(((dw_far, dw), (gdw_far, gdw_own), (pw_far, pw), (ew_far, ew), (spec_far, spec)))
    ]

    @pl.when(step == 0)
    def _():
        for c in weights:
            c.start()
        barrier = pltpu.get_barrier_semaphore()
        for where in peers:
            pl.semaphore_signal(barrier, inc=1, device_id=where, device_id_type=MESH)
        for ref in (gpw, gew, geb, vsum, acc):
            ref[...] = jnp.zeros_like(ref)
        stack_vectors(vec, (v0, v1, v2, v3, v4, v5, v6, v7, v8))
        weights[0].wait()

    @pl.when(step == 1)
    def _():
        for c in weights[1:]:
            c.wait()
        pl.semaphore_wait(pltpu.get_barrier_semaphore(), len(peers))

    def run(at):
        for name, stage in stages.get(at, ()):
            if stage == 0 and name == "project":
                reduced[name].full[...] = gpw[...].T.astype(bf16)
            if stage == 0 and name == "expand":
                reduced[name].full[...] = gew[...].astype(bf16)
            reduced[name].step(stage)

    if stages is not None:
        for at in range(3 * steps):
            if at in stages:
                pl.when(step == at)(functools.partial(run, at))

    def row(k):
        return vec[k : k + 1, :]

    def extent(b, g):
        return ext[g * G + b, 0], ext[g * G + b, 1]

    @pl.when(step < steps)
    def _():
        g = step
        coarse = lanes(stack([masks.coarse(*extent(b, g)) for b in range(G)], 0).astype(bf16), cot.shape[-1])
        up = cot[...].reshape(coarse.shape) * coarse
        gdb = total(up.astype(f32))
        for k in range(cot.shape[-1] // C):
            vsum[V_DB + k : V_DB + k + 1, :] += gdb[:, k * C : (k + 1) * C]
        for p in range(2):
            for q in range(2):
                k = 2 * p + q
                slab = dot_nt(up, dw[k * C : (k + 1) * C, :])
                for n in range(C // 128):
                    gr_s[n, :, p, pl.ds(q, across // 2, stride=2), :] = slab[:, n * 128 : (n + 1) * 128].reshape(
                        G * h // 2, across // 2, 128
                    )
        for team in range(G // T):
            here = pl.ds(team * T * pixels, T * pixels)
            valids = [masks.own(*extent(team * T + t, g)) for t in range(T)]
            facs = [
                valids[t] * (keep[g * G + team * T + t].astype(f32) * (1.0 / survival)) for t in range(T)
            ]
            rows = T * h // 2
            gr = stack(
                [gr_s[n, team * rows : (team + 1) * rows].reshape(T * pixels, 128) for n in range(C // 128)], 1
            )
            gr = gr * lanes(stack(valids, 0), C)
            sh = sh_in[here, :].astype(f32)
            vsum[V_DG : V_DG + 1, :] += total(gr * sh)
            vsum[V_DS : V_DS + 1, :] += total(gr)
            u = gr * row(DG)
            gres = lanes(inv2[here, :], C) * (u - mean(u) - sh * mean(u * sh))
            first = pl.multiple_of(g * (G * pixels) + team * T * pixels, T * pixels)
            gres_s[pl.ds(first, T * pixels), :] = gres.astype(bf16)
            gb = (gres * lanes(stack(facs, 0), C) * row(LS)).astype(bf16)
            for t in range(T):
                held[g * G + team * T + t, :pixels] = gb[t * pixels : (t + 1) * pixels]
            vsum[V_PB : V_PB + 1, :] += total(gb.astype(f32))
            gpw[...] += dot_tn(gb, act[here, :])

    @pl.when((step >= steps) & (step < 2 * steps))
    def _():
        g = step - steps
        for team in range(G // T):
            here = pl.ds(team * T * pixels, T * pixels)
            gb = stack([held[g * G + team * T + t, :pixels] for t in range(T)], 0)
            gn = None
            for k in range(HID // HC):
                part = slice(k * HC, (k + 1) * HC)
                gh = (dot_nt(gb, pw[part, :]) * slope[here, part].astype(f32)).astype(bf16)
                geb[:, part] += total(gh.astype(f32))
                gew[:, part] += dot_tn(nm[here, :], gh)
                term = dot_nt(gh, ew[:, part])
                gn = term if gn is None else gn + term
            gn_s[pl.ds(pl.multiple_of(g * (G * pixels) + team * T * pixels, T * pixels), T * pixels), :] = gn

    def halo(target, n, side, where):
        part, edge = pl.ds(pl.multiple_of(n * T, T), T), 3 * across
        src = held.at[part, pl.ds(side * edge, edge)]
        return remote(src, target.at[part], halo_sem.at[0, side, n], halo_sem.at[1, side, n], where)

    def up(g):
        return halo(bot_in, g, 0, place.above)

    def down(g):
        return halo(top_in, g, 1, place.below)

    @pl.when(step >= 2 * steps)
    def _():
        g = step - 2 * steps
        edge = 3 * across
        kr, ki = lanes(spec[:nf], T * C), lanes(spec[nf:], T * C)
        for team in range(G // T):
            here = pl.ds(team * T * pixels, T * pixels)
            first = pl.multiple_of(g * (G * pixels) + team * T * pixels, T * pixels)
            gn = gn_s[pl.ds(first, T * pixels), :]
            fh = fh_in[here, :].astype(f32)
            vsum[V_NG : V_NG + 1, :] += total(gn * fh)
            vsum[V_NB : V_NB + 1, :] += total(gn)
            w = gn * row(NG)
            gm = lanes(inv1[here, :], C) * (w - mean(w) - fh * mean(w * fh))
            vsum[V_DWB : V_DWB + 1, :] += total(gm)
            gm = gm.astype(bf16)
            gm = stack([gm[t * pixels : (t + 1) * pixels] for t in range(T)], 1)
            hat = dot(fwd_own[...], gm)
            gr, gi = hat[:nf], hat[nf:]
            sr, si = acc[:nf], acc[nf:]
            for t in range(T):
                at = slice(t * C, (t + 1) * C)
                xr, xi = xhat[team * T + t, :nf].astype(f32), xhat[team * T + t, nf:].astype(f32)
                sr = sr + gr[:, at] * xr + gi[:, at] * xi
                si = si + gr[:, at] * xi - gi[:, at] * xr
            acc[:nf] = sr
            acc[nf:] = si
            product = jnp.concatenate(
                [(gr * kr + gi * ki).astype(bf16), (gi * kr - gr * ki).astype(bf16)], axis=0
            )
            o = dot(inv_all[...], product)
            for t in range(T):
                b = g * G + team * T + t
                each = o[:, t * C : (t + 1) * C] * lanes(masks.every(ext[b, 0], ext[b, 1]), C)
                held[b, :edge] = each[:edge].astype(bf16)
                own = gres_s[pl.ds(pl.multiple_of(b * pixels, pixels), pixels), :].astype(f32)
                own_out[team * T + t] = (each[edge : edge + pixels] + own).astype(bf16)
                held[b, edge : 2 * edge] = each[edge + pixels :].astype(bf16)
            n = g * (G // T) + team
            pl.when(place.z > 0)(lambda n=n: up(n).start())
            pl.when(place.z < zs - 1)(lambda n=n: down(n).start())

    @pl.when(step == 3 * steps - 1)
    def _():
        small[...] = jnp.zeros_like(small)
        small[0:56, 0:C] = dot_exact(back[...], acc[...])
        for k in range(8 * C // 128):
            v, at = divmod(k, C // 128)
            small[S_VEC + k : S_VEC + k + 1, C:] = vsum[v : v + 1, at * 128 : (at + 1) * 128]
        for k in range(HID // 128):
            small[S_EB + k : S_EB + k + 1, C:] = geb[:, k * 128 : (k + 1) * 128]
        if stages is not None:
            run(3 * steps)
        else:
            for k, (src, dst) in enumerate(((gpw, gpw_out), (gew, gew_out), (small, small_out))):
                c = pltpu.make_async_copy(src, dst, sums[0].at[k])
                c.start()
                c.wait()

        @pl.when(place.z > 0)
        def _():
            for g in range(steps * (G // T)):
                up(g).wait_send()
                down(g).wait_recv()

        @pl.when(place.z < zs - 1)
        def _():
            for g in range(steps * (G // T)):
                down(g).wait_send()
                up(g).wait_recv()


def schedule():
    return {
        1: [('down0', 0)],
        2: [('down0', 1), ('down1', 0)],
        3: [('down1', 1)],
        4: [('project', 0)],
        5: [('down0', 2), ('project', 1)],
        6: [('down0', 3), ('down1', 2)],
        7: [('down1', 3), ('project', 2)],
        8: [('project', 3), ('expand', 0)],
        9: [('expand', 1)],
        10: [('down1', 4), ('expand', 2)],
        11: [('down0', 4), ('project', 4), ('expand', 3)],
        12: [('small', 0), ('down1', 5), ('small', 1), ('down0', 5), ('project', 5), ('expand', 4), ('small', 2), ('expand', 5), ('small', 3), ('down0', 6), ('down1', 6), ('project', 6), ('small', 4), ('expand', 6)],
    }


def backward(fused, zs, G, T, h, across, nf, n_img, ext, keep, cot, sh, inv2, act, slope, nm, fh, inv1, xhat, gdw, *consts):
    pixels, C, CO = h * across, sh.shape[-1], cot.shape[-1]
    HID = act.shape[1]
    Q, NP, steps = pixels // 4, n_img * pixels, n_img // G

    def group(first):
        return lambda t: jnp.clip(t - first, 0, steps - 1)

    def img(first, *s):
        return pl.BlockSpec((G,) + s, lambda t: (group(first)(t),) + (0,) * len(s))

    def pix(first, c):
        return pl.BlockSpec((G * pixels, c), lambda t: (group(first)(t), 0))

    any_space = pl.BlockSpec(memory_space=pl.ANY)
    smem = pl.BlockSpec(memory_space=pltpu.SMEM)
    sds = jax.ShapeDtypeStruct

    def sum_buffers(rows, cols, by_cols, dtype, full):
        half = rows // 2
        z = (half // 4, cols // zs) if by_cols else (half // 4 // zs, cols)
        n = 8 + 2 * (zs - 1)
        return [
            pltpu.VMEM((rows, cols) if full else (16, 128), dtype),
            pltpu.VMEM((half, cols), dtype),
            pltpu.VMEM((3, half // 4, cols), dtype),
            pltpu.VMEM((zs - 1,) + z, dtype),
            pltpu.SemaphoreType.DMA((n + 1,)),
            pltpu.SemaphoreType.DMA((n,)),
        ]

    if fused:
        sums = sum_buffers(4 * C, CO // 2, False, bf16, False) * 2
        sums += sum_buffers(HID, C, False, bf16, True)
        sums += sum_buffers(C, HID, True, bf16, True)
        n = 4 * zs
        sums += [
            pltpu.VMEM(SMALL, f32),
            pltpu.VMEM((n - 1, 8, 128), f32),
            pltpu.SemaphoreType.DMA((2 * n + 1,)),
            pltpu.SemaphoreType.DMA((2 * n,)),
        ]
        results = [sds((4 * C, CO), bf16), sds((HID, C), bf16), sds((C, HID), bf16)]
    else:
        sums = [pltpu.SemaphoreType.DMA((3,))]
        results = [sds((16, 128), bf16), sds((C, HID), f32), sds((C, HID), f32)]
        gdw = gdw[:16, :128]
    return pl.pallas_call(
        functools.partial(backward_kernel, G, T, h, across, nf, steps, zs, schedule() if fused else None),
        grid=(3 * steps,),
        in_specs=[
            smem, smem, img(0, Q, CO), pix(0, C), pix(0, 128), pix(0, HID), pix(steps, HID), pix(steps, C), pix(2 * steps, C),
            pix(2 * steps, 128), img(2 * steps, 2 * nf, C), any_space, any_space,
        ]
        + [whole(a) for a in consts[1:10]]
        + [any_space] * 2
        + [whole(a) for a in consts[12:14]]
        + [any_space, whole(consts[15])],
        out_specs=[img(2 * steps, pixels, C)] + [any_space] * 6,
        out_shape=[
            sds((n_img, pixels, C), bf16), sds((n_img, 3 * across, C), bf16), sds((n_img, 3 * across, C), bf16),
        ]
        + results
        + [sds(SMALL, f32)],
        scratch_shapes=[
            pltpu.VMEM((n_img, max(pixels, 6 * across), C), bf16), pltpu.VMEM((NP, C), bf16), pltpu.VMEM((NP, C), f32), pltpu.VMEM((C // 128, G * h // 2, 2, across, 128), f32),
            pltpu.VMEM((2 * nf, C), f32), pltpu.VMEM((2 * nf, C), f32), pltpu.VMEM((16, C), f32), pltpu.VMEM((C, HID), f32), pltpu.VMEM((C, HID), f32),
            pltpu.VMEM((1, HID), f32), pltpu.VMEM((8, C), f32), pltpu.VMEM(SMALL, f32),
            pltpu.VMEM(gdw.shape, gdw.dtype), pltpu.VMEM((4 * C, CO), bf16), pltpu.VMEM((HID, C), bf16), pltpu.VMEM((C, HID), bf16),
            pltpu.SemaphoreType.DMA((5,)), pltpu.SemaphoreType.DMA((2, 2, n_img // T)),
        ]
        + sums,
        compiler_params=pltpu.CompilerParams(vmem_limit_bytes=VMEM, collective_id=0, has_side_effects=True),
        name="backward",
    )(ext, keep, cot, sh, inv2, act, slope, nm, fh, inv1, xhat, gdw, *consts)


def per_device(n_sp, n_dp, *arrays):
    (
        tokens, extents, keep_mask, cotangent, dw_kernel, dw_bias, norm_gain, norm_bias, expand_weight, expand_bias,
        project_weight, project_bias, layer_scale, down_gain, down_shift, down_weight, down_bias,
    ) = arrays
    n_img, h, across, C = tokens.shape
    CO, HID = cotangent.shape[-1], expand_weight.shape[1]
    pixels = h * across
    G, T = 1024 // pixels, 512 // pixels
    fused = n_sp == 4 and n_dp == 8 and n_img // G == 4
    if not fused:
        G = T
    nf, fwd, inv, fwd_own, inv_all, spectrum, back = tables(h, across)
    fwd, inv, fwd_own, inv_all = (jnp.asarray(a, bf16) for a in (fwd, inv, fwd_own, inv_all))
    taps, back = jnp.asarray(spectrum, f32), jnp.asarray(back, f32)
    z = lax.axis_index("sp")
    first = z * h
    ext = extents - jnp.stack([first, jnp.zeros_like(first)])[None, :]
    own = tokens.reshape(n_img, pixels, C)
    cot = cotangent.reshape(n_img, pixels // 4, CO)
    dw = down_weight.reshape(4 * C, CO)
    vectors = (
        dw_bias, norm_gain, norm_bias, project_bias, layer_scale, down_gain, down_shift, down_bias, expand_bias
    )
    out, act, slope, xhat, fh, nm, inv1, sh, inv2, gdw, spec = forward(
        bf16 if fused else f32, n_sp,
        G, T, h, across, nf, n_img, ext, keep_mask, own, cot, fwd, inv, taps, dw_kernel, *vectors, expand_weight, project_weight, dw,
    )
    grad, from_above, from_below, gdw_sum, gpw, gew, small = backward(
        fused, n_sp, G, T, h, across, nf, n_img, ext, keep_mask, cot, sh, inv2, act, slope,
        nm, fh, inv1, xhat, gdw, dw, *vectors, project_weight, expand_weight, fwd_own, inv_all, spec, back,
    )
    if fused:
        gdw, gpw, gew = (a.astype(f32) for a in (gdw_sum, gpw, gew))
    else:
        gdw, gpw, gew, small = lax.psum((gdw, gpw, gew, small), ("sp", "dp"))
        gpw = gpw.T
    from_above = jnp.where(z > 0, from_above, jnp.zeros_like(from_above))
    from_below = jnp.where(z < n_sp - 1, from_below, jnp.zeros_like(from_below))
    gap = ((0, 0), (0, h - 3), (0, 0), (0, 0))
    pog = ((0, 0), (h - 3, 0), (0, 0), (0, 0))
    grad = (
        grad.reshape(n_img, h, across, C).astype(f32)
        + jnp.pad(from_above.reshape(n_img, 3, across, C), gap).astype(f32)
        + jnp.pad(from_below.reshape(n_img, 3, across, C), pog).astype(f32)
    ).astype(bf16)
    vectors = small[:, C:].reshape(-1)

    def vector(first, size):
        return vectors[first * 128 : first * 128 + size]

    gdg, gds, gpb, gng, gnb, gdwb = (vector(S_VEC + k * C // 128, C) for k in range(6))
    gdb, geb = vector(S_VEC + V_DB * C // 128, CO), vector(S_EB, HID)
    gls = (jnp.sum(project_weight.astype(f32) * gpw, axis=0) + project_bias * gpb) / layer_scale
    gdk = small[:56, :C].reshape(7, 8, C)[:, :7]
    return (
        out.reshape(n_img, h // 2, across // 2, CO), grad, gdk, gdwb, gng, gnb, gew, geb, gpw, gpb, gls, gdg, gds,
        gdw.reshape(down_weight.shape), gdb,
    )


def solution(mesh):
    maps = P("dp", "sp", None, None)
    return jax.shard_map(
        functools.partial(per_device, mesh.shape["sp"], mesh.shape["dp"]),
        mesh=mesh,
        in_specs=(maps, P("dp", None), P("dp"), maps) + (P(),) * 13,
        out_specs=(maps, maps) + (P(),) * 13,
        check_vma=False,
    )
```
